256 devices in a mesh: band: 32 (over z_hi, y, core), grid: 8 (over x, z_lo).
Axes of the slice: x: 4, y: 4, z: 8 (z_hi: 4, z_lo: 2; z = z_hi * 2 + z_lo), core: 2. Of those that a mesh axis runs over, the one named last changes fastest.
Arguments:
- orbitals: float32 [32, 96, 9216], P('band', 'grid'), may hold values from -30 to 30
- energies: float32 [32], P('band'), may hold values from -2 to -0.5
- local_pot: float32 [96, 9216], P('grid', 'band'), may hold values from 0.5 to 2
- trial_pot: float32 [4, 96, 9216], P(None, 'grid', 'band'), may hold values from 0.2 to 1.5
Outputs:
- response: float32 [32, 4, 96, 9216], P('band', None, 'grid')
- residual: float32 [32, 4, 96, 9216], P('band', None, 'grid')
- direction: float32 [32, 4, 96, 9216], P('band', None, 'grid')
- density: float32 [4, 96, 9216], P(None, 'grid', 'band')
The draws below stay inside these ranges and needn't reach their ends.
All inputs are finite; a program needn't handle non-finite values.
Results may differ from the reference program's by a relative error of at most 0.0003.
Values sent between devices are 32-bit elements; how exact they have to be, the bound alone decides.
No kernel may reach another device: no remote copies, remote signals or barrier semaphores. Data moves between devices by JAX's collectives and lax.ppermute only.
A program may use at most 192 MiB of HBM per device.

```python
import math
import jax
import jax.numpy as jnp
from jax import lax

SIDE = 96
TRIALS = 4
BANDS = 32


def draw_orbitals(key, part):
    key = jax.random.fold_in(key, 11)
    key_base, key_scale, key_block = jax.random.split(key, 3)
    dims_shape = (BANDS, SIDE, SIDE * SIDE)
    plane_pos = jnp.arange(SIDE, dtype=jnp.float32)[None, :, None] / (SIDE - 1)
    amplitude = jnp.exp(jax.random.uniform(key_scale, dims_shape, jnp.float32, 0.0, math.log(3.16)))
    block_level = jnp.exp(jax.random.uniform(key_block, (BANDS, 4), jnp.float32, math.log(0.55), math.log(1.8)))
    block_factor = jnp.repeat(block_level, SIDE // 4, axis=1)[:, :, None]
    base_draw = jax.random.truncated_normal(key_base, -3.0, 3.0, dims_shape, jnp.float32)
    envelope = jnp.exp(plane_pos * (0.5 * math.log(3.0)))
    return base_draw * amplitude * envelope * block_factor


def draw_trial_pot(key, part):
    key = jax.random.fold_in(key, 13)
    key_level, key_cell = jax.random.split(key)
    dims_shape = (TRIALS, SIDE, SIDE * SIDE)
    levels = jax.random.uniform(key_level, (TRIALS, 4), jnp.float32, 0.35, 1.1)
    cells = jax.random.uniform(key_cell, dims_shape, jnp.float32, 0.6, 1.35)
    block_levels = jnp.repeat(levels, SIDE // 4, axis=1)[:, :, None]
    return block_levels * cells


def shard_levels(key, shape, pieces, low, high):
    factor_of = 1.0
    for axis_at, shards_of in pieces:
        heights = jax.random.uniform(jax.random.fold_in(jax.random.fold_in(key, 6), axis_at), (shards_of,), jnp.float32, low / len(pieces), high / len(pieces))
        factor_of = factor_of * jnp.repeat(jnp.exp(heights), shape[axis_at] // shards_of).reshape((-1,) + (1,) * (len(shape) - 1 - axis_at))
    return factor_of


def setup_inputs(seed: int = 0) -> dict:
    seeds = jax.random.split(jax.random.key(seed), 5)
    orbitals = draw_orbitals(jax.random.fold_in(seeds[4], 71), 0)
    energies = jnp.clip(-2.0 + 1.5 * jax.random.uniform(seeds[1], (BANDS,), jnp.float32) ** shard_levels(seeds[1], (BANDS,), ((0, 32),), -0.2, 0.2), -2.0, -0.5)
    local_pot = jnp.clip(0.5 + 1.5 * jax.random.uniform(seeds[2], (SIDE, SIDE * SIDE), jnp.float32) ** shard_levels(seeds[2], (SIDE, SIDE * SIDE), ((0, 8), (1, 32)), -0.2, 0.2), 0.5, 2.0)
    trial_pot = draw_trial_pot(jax.random.fold_in(seeds[4], 71), 0)
    return dict(orbitals=orbitals, energies=energies, local_pot=local_pot, trial_pot=trial_pot)


def kinetic_grid(points):
    index = jnp.arange(points, dtype=jnp.int32)
    signed = jnp.where(index < points // 2, index, index - points)
    squares = signed[:, None, None] ** 2 + signed[None, :, None] ** 2 + signed[None, None, :] ** 2
    prefactor = 0.5 * (2.0 * math.pi / (points * 0.49)) ** 2
    return jnp.where(squares < (points // 4) ** 2, prefactor * squares.astype(jnp.float32), jnp.float32(0.0))


def reference(orbitals, energies, local_pot, trial_pot):
    weights = kinetic_grid(SIDE)
    weighted = trial_pot[None] * orbitals[:, None]
    correlation = jnp.sum(weighted * orbitals[:, None], axis=(2, 3))
    norms = jnp.sum(orbitals * orbitals, axis=(1, 2))
    source = -(weighted - orbitals[:, None] * (correlation / norms[:, None])[:, :, None, None])
    start_norm = jnp.sum(source * source, axis=(2, 3))

    def apply_one(pair):
        field, shift = pair
        volume = field.reshape(TRIALS, SIDE, SIDE, SIDE)
        spectrum = jnp.fft.fftn(volume, axes=(1, 2, 3)) * weights
        kinetic = jnp.real(jnp.fft.ifftn(spectrum, axes=(1, 2, 3))).reshape(field.shape)
        return kinetic + (local_pot - shift) * field

    image = lax.map(apply_one, (source, energies))
    curvature = jnp.sum(source * image, axis=(2, 3))
    step_size = (start_norm / curvature)[:, :, None, None]
    response = step_size * source
    residual = source - step_size * image
    new_norm = jnp.sum(residual * residual, axis=(2, 3))
    direction = residual + (new_norm / start_norm)[:, :, None, None] * source
    density = (4.0 / BANDS) * jnp.sum(orbitals[:, None] * response, axis=0)
    return response, residual, direction, density
```

```python
import math

import jax
import jax.numpy as jnp
import ml_dtypes
import numpy as np
from jax import lax
from jax.experimental import pallas as pl
from jax.experimental.pallas import tpu as pltpu
from jax.sharding import PartitionSpec as P

points = 96
planes = 12
trials = 4
bands = 32
half = 24
groups = 8
rows = points * planes
chunk = rows // groups
spacing = 0.49
prefactor = 0.5 * (2.0 * math.pi / (points * spacing)) ** 2
f32 = jnp.float32
bf16 = jnp.bfloat16


def split_np(table):
    table = np.asarray(table, np.float32)
    high = table.astype(ml_dtypes.bfloat16)
    low = (table - high.astype(np.float32)).astype(ml_dtypes.bfloat16)
    return high, low


def angle(a, b):
    return (np.outer(a, b) % points) * (2.0 * np.pi / points)


def build_tables():
    grid = np.arange(points)
    signed = np.arange(2 * half) - half
    kz = np.arange(half)
    w1 = np.zeros((5 * 128, 256))
    az = angle(grid, kz)
    for p in range(5):
        w1[p * 128 : p * 128 + points, p * half : (p + 1) * half] = np.cos(az)
        w1[p * 128 : p * 128 + points, 128 + p * half : 128 + (p + 1) * half] = -np.sin(az)
    order = np.zeros(points, np.int64)
    part = np.zeros(points, np.int64)
    for jj in range(6):
        for c in range(2):
            for g in range(groups):
                order[(2 * jj + c) * 8 + g] = signed[6 * g + jj]
                part[(2 * jj + c) * 8 + g] = c
    ay = angle(order, grid)
    real = part[:, None] == 0
    g1 = np.concatenate(
        [np.where(real, np.cos(ay), -np.sin(ay)), np.where(real, np.sin(ay), np.cos(ay))], 1
    )
    g4 = np.concatenate(
        [np.where(real, np.cos(ay), -np.sin(ay)), np.where(real, np.sin(ay), np.cos(ay))], 1
    ).T
    ax = angle(signed, grid)
    cx, sx = np.cos(ax), np.sin(ax)
    g2 = np.block([[cx, sx], [-sx, cx]])
    g3 = np.block([[cx.T, -sx.T], [sx.T, cx.T]])
    w2 = np.zeros((256, 4 * 128))
    for p in range(4):
        w2[p * half : (p + 1) * half, p * 128 : p * 128 + points] = np.cos(az).T
        w2[128 + p * half : 128 + (p + 1) * half, p * 128 : p * 128 + points] = -np.sin(az).T
    return {"w1": split_np(w1), "g1": split_np(g1), "g2": split_np(g2), "g3": split_np(g3),
            "g4": split_np(g4), "w2": split_np(w2)}


def dot(a, b):
    return lax.dot_general(a, b, (((1,), (0,)), ((), ())), preferred_element_type=f32)


def split(value):
    high = value.astype(bf16)
    return high, (value - high.astype(f32)).astype(bf16)


def left_table(high, low, value):
    vh, vl = split(value)
    return dot(high, vh) + dot(high, vl) + dot(low, vh)


def right_table(vh, vl, high, low):
    return dot(vh, high) + dot(vl, high) + dot(vh, low)


def lane_of(shape):
    return lax.broadcasted_iota(jnp.int32, shape, 1)


def row_of(shape):
    return lax.broadcasted_iota(jnp.int32, shape, 0)


def total(value):
    return jnp.sum(jnp.sum(value, axis=0, keepdims=True), axis=1, keepdims=True)


def fold(value):
    return jnp.sum(value.reshape(value.shape[0] // 8, 8, 128), axis=0)


def tile_of(shape, entries):
    row, lane = row_of(shape), lane_of(shape)
    out = jnp.zeros(shape, f32)
    for r, l, value in entries:
        out = jnp.where((row == r) & (lane == l), value, out)
    return out


def spread(t0, t1, t2):
    lane = lane_of(t0.shape)
    c1 = pltpu.roll(jnp.where(lane >= 96, t0, t1), 32, 1)
    c2 = pltpu.roll(jnp.where(lane >= 64, t1, t2), 64, 1)
    return t0, c1, c2


def pack_kernel(trial_ref, local_ref, out_ref):
    lane = lane_of((planes, 128))
    fill = jnp.zeros((planes, 96), f32)

    def pieces(ref, *at):
        t2 = jnp.concatenate([ref[(*at, slice(None), slice(256, 288))], fill], axis=1)
        return spread(ref[(*at, slice(None), slice(0, 128))], ref[(*at, slice(None), slice(128, 256))], t2)

    last = pieces(trial_ref, 3)
    for q in range(3):
        mine = pieces(trial_ref, q)
        for i in range(3):
            tail = pltpu.roll(last[i], 96 - 32 * q, 1)
            out_ref[q * 36 + i * 12 : q * 36 + i * 12 + 12, :] = jnp.where(lane < 96, mine[i], tail)
    mine = pieces(local_ref)
    for i in range(3):
        out_ref[108 + i * 12 : 120 + i * 12, :] = jnp.where(lane < 96, mine[i], 0.0)


def unpack_last(b0, b1, b2):
    lane = lane_of(b0.shape)
    r0, r1, r2 = pltpu.roll(b0, 32, 1), pltpu.roll(b1, 64, 1), pltpu.roll(b2, 96, 1)
    return jnp.where(lane < 32, r0, jnp.where(lane < 64, r1, r2))


def orbital_kernel(o_ref, out_ref):
    lane = lane_of((planes, 128))
    for q in range(points // 4):
        t = [o_ref[0, :, 384 * q + 128 * i : 384 * q + 128 * i + 128] for i in range(3)]
        c = [*spread(*t), pltpu.roll(t[2], 96, 1)]
        for i in range(4):
            at = (4 * q + i) * planes
            out_ref[at : at + planes, :] = jnp.where(lane < 96, c[i], 0.0)


def forward_kernel(me_ref, t_ref, o_ref, w1h, w1l, g1h, g1l, field_ref, out_ref, stat_ref,
                   high, low, real, imag):
    me = me_ref[0]
    norm = jnp.zeros((36, 128), f32)
    corr = [jnp.zeros((36, 128), f32) for _ in range(trials)]
    for u in range(bands):
        d = u ^ me
        slot = ((d & 1) << 4) | (((d >> 1) & 3) << 2) | (d >> 3)
        blocks = [t_ref[slot, q * 36 : q * 36 + 36, :] for q in range(4)]
        fields = [*blocks[:3], unpack_last(*blocks[:3]), blocks[3]]
        here = slice(u * 36, u * 36 + 36)
        for p in range(5):
            field_ref[p, here, :] = fields[p]
        o = o_ref[here, :]
        square = o * o
        norm = norm + square
        for p in range(trials):
            corr[p] = corr[p] + fields[p] * square
    norm = total(norm)
    mean = [total(c) / norm for c in corr]

    size = 96

    def weigh(i, sums):
        at = pl.ds(pl.multiple_of(i * size, size), size)
        o = o_ref[at, :]
        out = []
        for p in range(trials):
            w = (field_ref[p, at, :] - mean[p]) * o
            high[at, p * 128 : p * 128 + 128], low[at, p * 128 : p * 128 + 128] = split(w)
            out.append(sums[p] + fold(w * w))
        high[at, 512:640], low[at, 512:640] = split(o)
        return tuple(out)

    second = lax.fori_loop(0, rows // size, weigh, tuple(jnp.zeros((8, 128), f32) for _ in range(trials)))
    second = [total(s) for s in second]
    stat_ref[...] = tile_of((8, 128), [(0, 0, norm)] + [(0, 1 + p, mean[p]) for p in range(trials)])

    big = 384

    def along_z(i, _):
        at = pl.ds(pl.multiple_of(i * big, big), big)
        a = right_table(high[at, :], low[at, :], w1h[...], w1l[...])
        real[at, :] = a[:, :128]
        imag[at, :] = a[:, 128:]
        return 0

    lax.fori_loop(0, rows // big, along_z, 0)

    row, lane = row_of((points, 128)), lane_of((points, 128))
    ride = jnp.where((row < 8) & (lane == 120), norm, 0.0)
    for p in range(trials):
        ride = jnp.where((row < 8) & (lane == 121 + p), mean[p], ride)
        ride = jnp.where((row >= 8) & (row < 16) & (lane == 120 + p), second[p], ride)
    for x in range(0, planes, 2):
        parts = [
            jnp.concatenate([ref[pl.ds(x + i, points, stride=planes), :] for i in range(2)], axis=1)
            for ref in (real, imag)
        ]
        y = left_table(g1h[...], g1l[...], jnp.concatenate(parts, axis=0))
        for i in range(2):
            mine = y[:, i * 128 : i * 128 + 128] + ride
            for r in range(12):
                out_ref[pl.ds((x + i) * 12 + r, groups, stride=chunk), :] = mine[8 * r : 8 * r + 8]


def local_kernel(energy_ref, field_ref, o_ref, stat_ref, out_ref):
    energy = energy_ref[0]
    mean = [stat_ref[0:1, 1 + p : 2 + p] for p in range(trials)]
    size = 96

    def step(i, sums):
        at = pl.ds(pl.multiple_of(i * size, size), size)
        o = o_ref[at, :]
        shift = (field_ref[4, at, :] - energy) * o
        out = [sums[0] + fold(shift * o)]
        for p in range(trials):
            w = (field_ref[p, at, :] - mean[p]) * o
            both = shift * (field_ref[p, at, :] - mean[p])
            out.append(sums[1 + p] + fold(both * o))
            out.append(sums[5 + p] + fold(both * w))
        return (out[0], *out[1::2], *out[2::2])

    sums = lax.fori_loop(0, rows // size, step, tuple(jnp.zeros((8, 128), f32) for _ in range(9)))
    out_ref[...] = tile_of((8, 128), [(0, n, total(s)) for n, s in enumerate(sums)])


def wave_kernel(place_ref, in_ref, stat_ref, sums_ref, g2h, g2l, g3h, g3l, out_ref, scal_ref):
    owner = place_ref[0]
    s0 = in_ref[pl.ds(0, points, stride=planes), :]
    s1 = in_ref[pl.ds(1, points, stride=planes), :]
    weight = s0[:, 120:121]
    whole = jnp.sum(weight, axis=0, keepdims=True)
    lane = lane_of((points, 128))
    coef = jnp.zeros((points, 128), f32)
    alpha, start = [], []
    for p in range(trials):
        mean = s0[:, 121 + p : 122 + p]
        a = jnp.sum(weight * mean, axis=0, keepdims=True) / whole
        off = a - mean
        spread_sum = jnp.sum(s1[:, 120 + p : 121 + p] + weight * off * off, axis=0, keepdims=True)
        alpha.append(a)
        start.append(spread_sum / planes)
        coef = jnp.where((lane >= p * half) & (lane < (p + 1) * half), off, coef)

    def source_of(r):
        d = in_ref[pl.ds(r, points, stride=planes), :]
        o = jnp.where((lane >= 96) & (lane < 120), d, 0.0)
        o = pltpu.roll(o, 32, 1)
        o = o + pltpu.roll(o, 24, 1)
        o = o + pltpu.roll(o, 48, 1)
        return jnp.where(lane < 96, coef * o - d, 0.0)

    wide = (2 * half, 128)
    m = row_of(wide) - half
    k = lane_of(wide)
    k = k - jnp.where(k >= 72, 72, jnp.where(k >= 48, 48, jnp.where(k >= 24, 24, 0)))
    doubled = jnp.where(k == 0, 1.0, 2.0) * (prefactor / float(points**3))
    energy = jnp.zeros((1, 128), f32)
    own = [jnp.where(lane_of((1, 128)) == 0, 0.0, 0.0)]
    for pair in (2, 1, 0):
        parts = [
            jnp.concatenate([source_of(2 * (2 * pair + i) + c) for i in range(2)], axis=1)
            for c in range(2)
        ]
        u = left_table(g2h[...], g2l[...], jnp.concatenate(parts, axis=0))
        weights = []
        for i in range(2):
            j = owner * 6 + (2 * pair + i) - half
            square = m * m + k * k + j * j
            weights.append(jnp.where(square < half * half, doubled * square.astype(f32), 0.0))
        w = jnp.concatenate(weights, axis=1)
        t = u * jnp.concatenate([w, w], axis=0)
        product = jnp.sum(u * t, axis=0, keepdims=True)
        energy = energy + product[:, :128] + product[:, 128:]
        e = left_table(g3h[...], g3l[...], t)
        if pair == 0:
            l1 = lane_of((1, 128))
            ride = jnp.zeros((1, 128), f32)
            entries = []
            for p in range(trials):
                kinetic = jnp.sum(jnp.where((l1 >= p * half) & (l1 < (p + 1) * half), energy, 0.0), axis=1, keepdims=True)
                off = alpha[p] - stat_ref[0:1, 1 + p : 2 + p]
                at_p = sums_ref[0:1, 5 + p : 6 + p] - 2.0 * off * sums_ref[0:1, 1 + p : 2 + p] + off * off * sums_ref[0:1, 0:1]
                ride = jnp.where(l1 == 96 + p, kinetic + at_p, ride)
                entries += [(0, p, alpha[p]), (0, 4 + p, start[p])]
            scal_ref[...] = tile_of((8, 128), entries)
            e = e + jnp.concatenate([ride, jnp.zeros((1, 128), f32)], axis=1)
        for i in range(2):
            for c in range(2):
                out_ref[pl.ds(2 * (2 * pair + i) + c, points, stride=planes), :] = (
                    e[c * points : (c + 1) * points, i * 128 : i * 128 + 128]
                )


def image_kernel(energy_ref, in_ref, scal_ref, field_ref, o_ref, g4h, g4l, w2h, w2l,
                 source_ref, residual_ref, norm_ref, coef_ref, real, imag):
    energy = energy_ref[0]
    shares = in_ref[pl.ds(0, groups, stride=chunk), :]
    curvature = jnp.sum(shares, axis=0, keepdims=True)
    alpha = [scal_ref[0:1, p : p + 1] for p in range(trials)]
    step = [scal_ref[0:1, 4 + p : 5 + p] / curvature[:, 96 + p : 97 + p] for p in range(trials)]
    coef = tile_of((8, 128), [(0, p, step[p]) for p in range(trials)] + [(0, 4 + p, alpha[p]) for p in range(trials)])
    for v in range(bands):
        coef_ref[v, :, :] = coef
    for x in range(0, planes, 2):
        b = jnp.concatenate(
            [
                jnp.concatenate(
                    [in_ref[pl.ds((x + i) * 12 + r, groups, stride=chunk), :] for r in range(12)], axis=0
                )
                for i in range(2)
            ],
            axis=1,
        )
        v = left_table(g4h[...], g4l[...], b)
        for i in range(2):
            real[pl.ds(x + i, points, stride=planes), :] = v[:points, i * 128 : i * 128 + 128]
            imag[pl.ds(x + i, points, stride=planes), :] = v[points:, i * 128 : i * 128 + 128]
    size = 96

    def back(i, sums):
        at = pl.ds(pl.multiple_of(i * size, size), size)
        vh, vl = split(jnp.concatenate([real[at, :], imag[at, :]], axis=1))
        kinetic = right_table(vh, vl, w2h[...], w2l[...])
        o = o_ref[at, :]
        shift = field_ref[4, at, :] - energy
        out = []
        for p in range(trials):
            source = (alpha[p] - field_ref[p, at, :]) * o
            image = kinetic[:, p * 128 : p * 128 + 128] + shift * source
            residual = source - step[p] * image
            source_ref[p, at, :] = source
            residual_ref[p, at, :] = residual
            out.append(sums[p] + fold(residual * residual))
        return tuple(out)

    sums = lax.fori_loop(0, rows // size, back, tuple(jnp.zeros((8, 128), f32) for _ in range(trials)))
    norms = tile_of((8, 128), [(0, p, total(s)) for p, s in enumerate(sums)])
    for g in range(groups):
        norm_ref[g, :, :] = norms


def flat_of(ref, q):
    c = [ref[0, (4 * q + i) * planes : (4 * q + i + 1) * planes, :] for i in range(4)]
    lane = lane_of((planes, 128))
    r1, r2, r3 = pltpu.roll(c[1], 96, 1), pltpu.roll(c[2], 64, 1), pltpu.roll(c[3], 32, 1)
    return jnp.where(lane < 96, c[0], r1), jnp.where(lane < 64, r1, r2), jnp.where(lane < 32, r2, r3)


def lane_value(tile, at):
    lane = lane_of((1, 128))
    return jnp.sum(jnp.where(lane == at, tile, 0.0), axis=1, keepdims=True)


def flat_kernel(coef_ref, source_ref, residual_ref, response_out, residual_out):
    step = lane_value(coef_ref[0, 0:1, :], pl.program_id(0))
    for q in range(points // 4):
        for i, (s, r) in enumerate(zip(flat_of(source_ref, q), flat_of(residual_ref, q))):
            at = slice(384 * q + 128 * i, 384 * q + 128 * i + 128)
            response_out[0, 0, :, at] = step * s
            residual_out[0, 0, :, at] = r


def direction_kernel(coef_ref, scal_ref, norm_ref, response_ref, residual_ref, out_ref):
    p = pl.program_id(0)
    step = lane_value(coef_ref[0, 0:1, :], p)
    start = lane_value(scal_ref[0:1, :], 4 + p)
    new = lane_value(jnp.sum(norm_ref[:, 0, :], axis=0, keepdims=True), p)
    ratio = new / start / step
    out_ref[...] = residual_ref[...] + ratio * response_ref[...]


def density_kernel(coef_ref, packed_ref, o_ref, out_ref):
    blocks = [packed_ref[q * 36 : q * 36 + 36, :] for q in range(3)]
    fields = [*blocks, unpack_last(*blocks)]
    sums = [jnp.zeros((36, 128), f32) for _ in range(trials)]
    for v in range(bands):
        square = o_ref[v, :, :]
        square = square * square
        for p in range(trials):
            step = coef_ref[v, 0:1, p : p + 1]
            alpha = coef_ref[v, 0:1, 4 + p : 5 + p]
            sums[p] = sums[p] + (step * (alpha - fields[p])) * square
    lane = lane_of((planes, 128))
    for p in range(trials):
        c = [sums[p][12 * i : 12 * i + 12] * (4.0 / bands) for i in range(3)]
        r1, r2 = pltpu.roll(c[1], 96, 1), pltpu.roll(c[2], 64, 1)
        out_ref[p, :, 0:128] = jnp.where(lane < 96, c[0], r1)
        out_ref[p, :, 128:256] = jnp.where(lane < 64, r1, r2)
        out_ref[p, :, 256:288] = r2[:, 0:32]


vmem = pl.BlockSpec(memory_space=pltpu.VMEM)
smem = pl.BlockSpec(memory_space=pltpu.SMEM)
params = pltpu.CompilerParams(vmem_limit_bytes=40 * 1024 * 1024)


def shape(*dims, dtype=f32):
    return jax.ShapeDtypeStruct(dims, dtype)


def call(kernel, ins, outs, scratch=(), name=None):
    return pl.pallas_call(
        kernel, out_shape=outs, in_specs=ins, out_specs=jax.tree.map(lambda _: vmem, outs),
        scratch_shapes=scratch, compiler_params=params, name=name,
    )


def pack(trial, local):
    return call(pack_kernel, [vmem] * 2, shape(144, 128), name="pack")(trial, local)


def orbital_rows(orbitals):
    return call(orbital_kernel, [vmem], shape(rows, 128), name="orbital_rows")(orbitals)


def forward(me, gathered, o, tables):
    return call(
        forward_kernel, [smem] + [vmem] * 6,
        (shape(5, rows, 128), shape(rows, 128), shape(8, 128)),
        [pltpu.VMEM((rows, 640), bf16), pltpu.VMEM((rows, 640), bf16),
         pltpu.VMEM((rows, 128), f32), pltpu.VMEM((rows, 128), f32)],
        name="forward",
    )(me, gathered, o, *tables["w1"], *tables["g1"])


def local_sums(energies, fields, o, stat):
    return call(local_kernel, [smem] + [vmem] * 3, shape(8, 128), name="local_sums")(energies, fields, o, stat)


def waves(place, arrived, stat, sums, tables):
    return call(
        wave_kernel, [smem] + [vmem] * 7, (shape(rows, 128), shape(8, 128)), name="waves"
    )(place, arrived, stat, sums, *tables["g2"], *tables["g3"])


def image(energies, arrived, scal, fields, o, tables):
    return call(
        image_kernel, [smem] + [vmem] * 8,
        (shape(trials, rows, 128), shape(trials, rows, 128), shape(groups, 8, 128), shape(bands, 8, 128)),
        [pltpu.VMEM((rows, 128), f32), pltpu.VMEM((rows, 128), f32)],
        name="image",
    )(energies, arrived, scal, fields, o, *tables["g4"], *tables["w2"])


def flat(coef, source, residual):
    small = pl.BlockSpec((bands, 8, 128), lambda p: (0, 0, 0))
    block = pl.BlockSpec((1, rows, 128), lambda p: (p, 0, 0))
    out = pl.BlockSpec((1, 1, planes, points * points), lambda p: (0, p, 0, 0))
    return pl.pallas_call(
        flat_kernel, grid=(trials,), in_specs=[small, block, block], out_specs=(out, out),
        out_shape=(shape(1, trials, planes, points * points),) * 2, compiler_params=params, name="flat",
    )(coef, source, residual)


def direct(coef, scal, norms, response, residual):
    out = pl.BlockSpec((1, 1, planes, points * points), lambda p: (0, p, 0, 0))
    return pl.pallas_call(
        direction_kernel, grid=(trials,),
        in_specs=[
            pl.BlockSpec((bands, 8, 128), lambda p: (0, 0, 0)),
            pl.BlockSpec((8, 128), lambda p: (0, 0)),
            pl.BlockSpec((groups, 8, 128), lambda p: (0, 0, 0)),
            out, out,
        ],
        out_specs=out, out_shape=shape(1, trials, planes, points * points),
        compiler_params=params, name="direction",
    )(coef, scal, norms, response, residual)


def density_of(coef, packed, o):
    return call(density_kernel, [vmem] * 3, shape(trials, planes, 288), name="density")(coef, packed, o)


def swapped(value, axis, size, mask):
    return lax.ppermute(value, axis, [(s, s ^ mask) for s in range(size)])


def gather_bands(packed):
    value = packed[None]
    for masks in ((8, 16, 24), (2, 4, 6), (1,)):
        value = jnp.concatenate([value] + [swapped(value, "band", bands, m) for m in masks], axis=0)
    return value


def on_device(orbitals, energies, local_pot, trial_pot):
    tables = {name: tuple(jnp.asarray(t) for t in pair) for name, pair in build_tables().items()}
    me = lax.axis_index("band").astype(jnp.int32).reshape(1)
    place = lax.axis_index("grid").astype(jnp.int32).reshape(1)
    packed = pack(trial_pot, local_pot)
    o = orbital_rows(orbitals)
    gathered = gather_bands(packed)
    o_bands = lax.all_to_all(o.reshape(bands, 36, 128), "band", 0, 0, tiled=True)
    fields, sent, stat = forward(me, gathered, o, tables)
    arrived = lax.all_to_all(sent.reshape(groups, chunk, 128), "grid", 0, 0, tiled=True).reshape(rows, 128)
    sums = local_sums(energies, fields, o, stat)
    back, scal = waves(place, arrived, stat, sums, tables)
    back = lax.all_to_all(back.reshape(groups, chunk, 128), "grid", 0, 0, tiled=True).reshape(rows, 128)
    source, residual, norms, coef = image(energies, back, scal, fields, o, tables)
    norms = lax.all_to_all(norms, "grid", 0, 0, tiled=True)
    coefs = lax.all_to_all(coef, "band", 0, 0, tiled=True)
    response, residual = flat(coef, source, residual)
    direction = direct(coef, scal, norms, response, residual)
    density = density_of(coefs, packed, o_bands)
    return response, residual, direction, density


def solution(mesh):
    return jax.shard_map(
        on_device,
        mesh=mesh,
        in_specs=(P("band", "grid", None), P("band"), P("grid", "band"), P(None, "grid", "band")),
        out_specs=(
            P("band", None, "grid", None),
            P("band", None, "grid", None),
            P("band", None, "grid", None),
            P(None, "grid", "band"),
        ),
        check_vma=False,
    )
```

```python
import math

import jax
import jax.numpy as jnp
import ml_dtypes
import numpy as np
from jax import lax
from jax.experimental import pallas as pl
from jax.experimental.pallas import tpu as pltpu
from jax.sharding import PartitionSpec as P

points = 96
planes = 12
trials = 4
bands = 32
half = 24
groups = 8
rows = points * planes
chunk = rows // groups
spacing = 0.49
prefactor = 0.5 * (2.0 * math.pi / (points * spacing)) ** 2
f32 = jnp.float32
bf16 = jnp.bfloat16


def split_np(table):
    table = np.asarray(table, np.float32)
    high = table.astype(ml_dtypes.bfloat16)
    low = (table - high.astype(np.float32)).astype(ml_dtypes.bfloat16)
    return high, low


def angle(a, b):
    return (np.outer(a, b) % points) * (2.0 * np.pi / points)


def build_tables():
    grid = np.arange(points)
    signed = np.arange(2 * half) - half
    kz = np.arange(half)
    w1 = np.zeros((5 * 128, 256))
    az = angle(grid, kz)
    for p in range(5):
        w1[p * 128 : p * 128 + points, p * half : (p + 1) * half] = np.cos(az)
        w1[p * 128 : p * 128 + points, 128 + p * half : 128 + (p + 1) * half] = -np.sin(az)
    order = np.zeros(points, np.int64)
    part = np.zeros(points, np.int64)
    for jj in range(6):
        for c in range(2):
            for g in range(groups):
                order[(2 * jj + c) * 8 + g] = signed[6 * g + jj]
                part[(2 * jj + c) * 8 + g] = c
    ay = angle(order, grid)
    real = part[:, None] == 0
    g1 = np.concatenate(
        [np.where(real, np.cos(ay), -np.sin(ay)), np.where(real, np.sin(ay), np.cos(ay))], 1
    )
    g4 = np.concatenate(
        [np.where(real, np.cos(ay), -np.sin(ay)), np.where(real, np.sin(ay), np.cos(ay))], 1
    ).T
    ax = angle(signed, grid)
    cx, sx = np.cos(ax), np.sin(ax)
    g2 = np.block([[cx, sx], [-sx, cx]])
    g3 = np.block([[cx.T, -sx.T], [sx.T, cx.T]])
    w2 = np.zeros((256, 4 * 128))
    for p in range(4):
        w2[p * half : (p + 1) * half, p * 128 : p * 128 + points] = np.cos(az).T
        w2[128 + p * half : 128 + (p + 1) * half, p * 128 : p * 128 + points] = -np.sin(az).T
    return {"w1": split_np(w1), "g1": split_np(g1), "g2": split_np(g2), "g3": split_np(g3),
            "g4": split_np(g4), "w2": split_np(w2)}


def dot(a, b):
    return lax.dot_general(a, b, (((1,), (0,)), ((), ())), preferred_element_type=f32)


def split(value):
    high = value.astype(bf16)
    return high, (value - high.astype(f32)).astype(bf16)


def left_table(high, low, value):
    vh, vl = split(value)
    return dot(high, vh) + dot(high, vl) + dot(low, vh)


def right_table(vh, vl, high, low):
    return dot(vh, high) + dot(vl, high) + dot(vh, low)


def lane_of(shape):
    return lax.broadcasted_iota(jnp.int32, shape, 1)


def row_of(shape):
    return lax.broadcasted_iota(jnp.int32, shape, 0)


def total(value):
    return jnp.sum(jnp.sum(value, axis=0, keepdims=True), axis=1, keepdims=True)


def fold(value):
    return jnp.sum(value.reshape(value.shape[0] // 8, 8, 128), axis=0)


def tile_of(shape, entries):
    row, lane = row_of(shape), lane_of(shape)
    out = jnp.zeros(shape, f32)
    for r, l, value in entries:
        out = jnp.where((row == r) & (lane == l), value, out)
    return out


def spread(t0, t1, t2):
    lane = lane_of(t0.shape)
    c1 = pltpu.roll(jnp.where(lane >= 96, t0, t1), 32, 1)
    c2 = pltpu.roll(jnp.where(lane >= 64, t1, t2), 64, 1)
    return t0, c1, c2


def pack_kernel(trial_ref, local_ref, out_ref):
    lane = lane_of((planes, 128))
    fill = jnp.zeros((planes, 96), f32)

    def pieces(ref, *at):
        t2 = jnp.concatenate([ref[(slice(None), *at, slice(256, 288))], fill], axis=1)
        return spread(ref[(slice(None), *at, slice(0, 128))], ref[(slice(None), *at, slice(128, 256))], t2)

    last = pieces(trial_ref, 3)
    for q in range(3):
        mine = pieces(trial_ref, q)
        for i in range(3):
            tail = pltpu.roll(last[i], 96 - 32 * q, 1)
            out_ref[q * 36 + i * 12 : q * 36 + i * 12 + 12, :] = jnp.where(lane < 96, mine[i], tail)
    mine = pieces(local_ref)
    for i in range(3):
        out_ref[108 + i * 12 : 120 + i * 12, :] = jnp.where(lane < 96, mine[i], 0.0)


def unpack_last(b0, b1, b2):
    lane = lane_of(b0.shape)
    r0, r1, r2 = pltpu.roll(b0, 32, 1), pltpu.roll(b1, 64, 1), pltpu.roll(b2, 96, 1)
    return jnp.where(lane < 32, r0, jnp.where(lane < 64, r1, r2))


def orbital_kernel(o_ref, out_ref):
    lane = lane_of((planes, 128))
    for q in range(points // 4):
        t = [o_ref[0, :, 384 * q + 128 * i : 384 * q + 128 * i + 128] for i in range(3)]
        c = [*spread(*t), pltpu.roll(t[2], 96, 1)]
        for i in range(4):
            at = (4 * q + i) * planes
            out_ref[at : at + planes, :] = jnp.where(lane < 96, c[i], 0.0)


def forward_kernel(me_ref, t_ref, o_ref, w1h, w1l, g1h, g1l, field_ref, out_ref, stat_ref,
                   high, low, real, imag):
    me = me_ref[0]
    norm = jnp.zeros((36, 128), f32)
    corr = [jnp.zeros((36, 128), f32) for _ in range(trials)]
    for u in range(bands):
        d = u ^ me
        slot = ((d & 1) << 4) | (((d >> 1) & 3) << 2) | (d >> 3)
        blocks = [t_ref[slot, q * 36 : q * 36 + 36, :] for q in range(4)]
        fields = [*blocks[:3], unpack_last(*blocks[:3]), blocks[3]]
        here = slice(u * 36, u * 36 + 36)
        for p in range(5):
            field_ref[p, here, :] = fields[p]
        o = o_ref[here, :]
        square = o * o
        norm = norm + square
        for p in range(trials):
            corr[p] = corr[p] + fields[p] * square
    norm = total(norm)
    mean = [total(c) / norm for c in corr]

    size = 96

    def weigh(i, sums):
        at = pl.ds(pl.multiple_of(i * size, size), size)
        o = o_ref[at, :]
        out = []
        for p in range(trials):
            w = (field_ref[p, at, :] - mean[p]) * o
            high[at, p * 128 : p * 128 + 128], low[at, p * 128 : p * 128 + 128] = split(w)
            out.append(sums[p] + fold(w * w))
        high[at, 512:640], low[at, 512:640] = split(o)
        return tuple(out)

    second = lax.fori_loop(0, rows // size, weigh, tuple(jnp.zeros((8, 128), f32) for _ in range(trials)))
    second = [total(s) for s in second]
    stat_ref[...] = tile_of((8, 128), [(0, 0, norm)] + [(0, 1 + p, mean[p]) for p in range(trials)])

    big = 384

    def along_z(i, _):
        at = pl.ds(pl.multiple_of(i * big, big), big)
        a = right_table(high[at, :], low[at, :], w1h[...], w1l[...])
        real[at, :] = a[:, :128]
        imag[at, :] = a[:, 128:]
        return 0

    lax.fori_loop(0, rows // big, along_z, 0)

    row, lane = row_of((points, 128)), lane_of((points, 128))
    ride = jnp.where((row < 8) & (lane == 120), norm, 0.0)
    for p in range(trials):
        ride = jnp.where((row < 8) & (lane == 121 + p), mean[p], ride)
        ride = jnp.where((row >= 8) & (row < 16) & (lane == 120 + p), second[p], ride)
    for x in range(0, planes, 2):
        parts = [
            jnp.concatenate([ref[pl.ds(x + i, points, stride=planes), :] for i in range(2)], axis=1)
            for ref in (real, imag)
        ]
        y = left_table(g1h[...], g1l[...], jnp.concatenate(parts, axis=0))
        for i in range(2):
            mine = y[:, i * 128 : i * 128 + 128] + ride
            for r in range(12):
                out_ref[pl.ds((x + i) * 12 + r, groups, stride=chunk), :] = mine[8 * r : 8 * r + 8]


def local_kernel(energy_ref, field_ref, o_ref, stat_ref, out_ref):
    energy = energy_ref[0]
    mean = [stat_ref[0:1, 1 + p : 2 + p] for p in range(trials)]
    size = 96

    def step(i, sums):
        at = pl.ds(pl.multiple_of(i * size, size), size)
        o = o_ref[at, :]
        shift = (field_ref[4, at, :] - energy) * o
        out = [sums[0] + fold(shift * o)]
        for p in range(trials):
            w = (field_ref[p, at, :] - mean[p]) * o
            both = shift * (field_ref[p, at, :] - mean[p])
            out.append(sums[1 + p] + fold(both * o))
            out.append(sums[5 + p] + fold(both * w))
        return (out[0], *out[1::2], *out[2::2])

    sums = lax.fori_loop(0, rows // size, step, tuple(jnp.zeros((8, 128), f32) for _ in range(9)))
    out_ref[...] = tile_of((8, 128), [(0, n, total(s)) for n, s in enumerate(sums)])


def wave_kernel(place_ref, in_ref, stat_ref, sums_ref, g2h, g2l, g3h, g3l, out_ref, scal_ref, coef_ref):
    owner = place_ref[0]
    s0 = in_ref[pl.ds(0, points, stride=planes), :]
    s1 = in_ref[pl.ds(1, points, stride=planes), :]
    weight = s0[:, 120:121]
    whole = jnp.sum(weight, axis=0, keepdims=True)
    lane = lane_of((points, 128))
    coef = jnp.zeros((points, 128), f32)
    alpha, start = [], []
    for p in range(trials):
        mean = s0[:, 121 + p : 122 + p]
        a = jnp.sum(weight * mean, axis=0, keepdims=True) / whole
        off = a - mean
        spread_sum = jnp.sum(s1[:, 120 + p : 121 + p] + weight * off * off, axis=0, keepdims=True)
        alpha.append(a)
        start.append(spread_sum / planes)
        coef = jnp.where((lane >= p * half) & (lane < (p + 1) * half), off, coef)

    def source_of(r):
        d = in_ref[pl.ds(r, points, stride=planes), :]
        o = jnp.where((lane >= 96) & (lane < 120), d, 0.0)
        o = pltpu.roll(o, 32, 1)
        o = o + pltpu.roll(o, 24, 1)
        o = o + pltpu.roll(o, 48, 1)
        return jnp.where(lane < 96, coef * o - d, 0.0)

    wide = (2 * half, 128)
    m = row_of(wide) - half
    k = lane_of(wide)
    k = k - jnp.where(k >= 72, 72, jnp.where(k >= 48, 48, jnp.where(k >= 24, 24, 0)))
    doubled = jnp.where(k == 0, 1.0, 2.0) * (prefactor / float(points**3))
    energy = jnp.zeros((1, 128), f32)
    own = [jnp.where(lane_of((1, 128)) == 0, 0.0, 0.0)]
    for pair in (2, 1, 0):
        parts = [
            jnp.concatenate([source_of(2 * (2 * pair + i) + c) for i in range(2)], axis=1)
            for c in range(2)
        ]
        u = left_table(g2h[...], g2l[...], jnp.concatenate(parts, axis=0))
        weights = []
        for i in range(2):
            j = owner * 6 + (2 * pair + i) - half
            square = m * m + k * k + j * j
            weights.append(jnp.where(square < half * half, doubled * square.astype(f32), 0.0))
        w = jnp.concatenate(weights, axis=1)
        t = u * jnp.concatenate([w, w], axis=0)
        product = jnp.sum(u * t, axis=0, keepdims=True)
        energy = energy + product[:, :128] + product[:, 128:]
        e = left_table(g3h[...], g3l[...], t)
        if pair == 0:
            l1 = lane_of((1, 128))
            ride = jnp.zeros((1, 128), f32)
            entries = []
            for p in range(trials):
                kinetic = jnp.sum(jnp.where((l1 >= p * half) & (l1 < (p + 1) * half), energy, 0.0), axis=1, keepdims=True)
                off = alpha[p] - stat_ref[0:1, 1 + p : 2 + p]
                at_p = sums_ref[0:1, 5 + p : 6 + p] - 2.0 * off * sums_ref[0:1, 1 + p : 2 + p] + off * off * sums_ref[0:1, 0:1]
                ride = jnp.where(l1 == 96 + p, kinetic + at_p, ride)
                entries += [(0, p, alpha[p]), (0, 4 + p, start[p])]
            scal_ref[...] = tile_of((8, 128), entries)
            mine = jnp.where(row_of((8, 128)) == 0, pltpu.roll(jnp.where(l1 < 100, ride, 0.0), 32, 1), 0.0)
            mine = mine + pltpu.roll(tile_of((8, 128), entries), 4, 1)
            for v in range(bands):
                coef_ref[v, :, :] = mine
            e = e + jnp.concatenate([ride, jnp.zeros((1, 128), f32)], axis=1)
        for i in range(2):
            for c in range(2):
                out_ref[pl.ds(2 * (2 * pair + i) + c, points, stride=planes), :] = (
                    e[c * points : (c + 1) * points, i * 128 : i * 128 + 128]
                )


def fold_bands(tile, at):
    lane = lane_of((8, 128))
    out = jnp.zeros((8, 128), f32)
    for b in range(4):
        part = jnp.where((lane >= at) & (lane < at + 4), tile[8 * b : 8 * b + 8], 0.0)
        out = out + pltpu.roll(part, (16 * b - at) % 128, 1)
    return out


def image_kernel(energy_ref, in_ref, scal_ref, field_ref, o_ref, g4h, g4l, w2h, w2l,
                 source_ref, residual_ref, norm_ref, step_ref, real, imag):
    energy = energy_ref[0]
    shares = in_ref[pl.ds(0, groups, stride=chunk), :]
    curvature = jnp.sum(shares, axis=0, keepdims=True)
    alpha = [scal_ref[0:1, p : p + 1] for p in range(trials)]
    step = [scal_ref[0:1, 4 + p : 5 + p] / curvature[:, 96 + p : 97 + p] for p in range(trials)]
    step_ref[...] = tile_of(
        (8, 128),
        [(0, p, step[p]) for p in range(trials)] + [(0, 4 + p, scal_ref[0:1, 4 + p : 5 + p]) for p in range(trials)],
    )
    for x in range(0, planes, 2):
        b = jnp.concatenate(
            [
                jnp.concatenate(
                    [in_ref[pl.ds((x + i) * 12 + r, groups, stride=chunk), :] for r in range(12)], axis=0
                )
                for i in range(2)
            ],
            axis=1,
        )
        v = left_table(g4h[...], g4l[...], b)
        for i in range(2):
            real[pl.ds(x + i, points, stride=planes), :] = v[:points, i * 128 : i * 128 + 128]
            imag[pl.ds(x + i, points, stride=planes), :] = v[points:, i * 128 : i * 128 + 128]
    size = 96

    def back(i, sums):
        at = pl.ds(pl.multiple_of(i * size, size), size)
        vh, vl = split(jnp.concatenate([real[at, :], imag[at, :]], axis=1))
        kinetic = right_table(vh, vl, w2h[...], w2l[...])
        o = o_ref[at, :]
        shift = field_ref[4, at, :] - energy
        out = []
        for p in range(trials):
            source = (alpha[p] - field_ref[p, at, :]) * o
            image = kinetic[:, p * 128 : p * 128 + 128] + shift * source
            residual = source - step[p] * image
            there = pl.ds(i * (size * trials) + p, size, stride=trials)
            source_ref[there, :] = source
            residual_ref[there, :] = residual
            out.append(sums[p] + fold(residual * residual))
        return tuple(out)

    sums = lax.fori_loop(0, rows // size, back, tuple(jnp.zeros((8, 128), f32) for _ in range(trials)))
    norm_ref[...] = tile_of((8, 128), [(0, 64 + p, total(s)) for p, s in enumerate(sums)])


def share_kernel(norm_ref, coef_ref, out_ref):
    tile = norm_ref[...] + fold_bands(coef_ref[:, 0, :], 0)
    for g in range(groups):
        out_ref[g, :, :] = tile


def lane_value(tile, at):
    lane = lane_of((1, 128))
    return jnp.sum(jnp.where(lane == at, tile, 0.0), axis=1, keepdims=True)


def per_trial(count, values):
    r = row_of((count, 128)) & 3
    out = jnp.zeros((count, 128), f32)
    for p in range(trials):
        out = jnp.where(r == p, values[p], out)
    return out


def flat_kernel(step_ref, source_ref, residual_ref, response_out, residual_out):
    size = planes * trials
    lane = lane_of((size, 128))
    step = per_trial(size, [step_ref[0:1, p : p + 1] for p in range(trials)])

    def tiles(ref, q):
        c = [ref[(4 * q + i) * size : (4 * q + i + 1) * size, :] for i in range(4)]
        r1, r2, r3 = pltpu.roll(c[1], 96, 1), pltpu.roll(c[2], 64, 1), pltpu.roll(c[3], 32, 1)
        return jnp.where(lane < 96, c[0], r1), jnp.where(lane < 64, r1, r2), jnp.where(lane < 32, r2, r3)

    for q in range(4):
        for i, (s, r) in enumerate(zip(tiles(source_ref, q), tiles(residual_ref, q))):
            at = slice(384 * q + 128 * i, 384 * q + 128 * i + 128)
            response_out[:, :, at] = (step * s).reshape(planes, trials, 128)
            residual_out[:, :, at] = r.reshape(planes, trials, 128)


def direction_kernel(step_ref, norm_ref, response_ref, residual_ref, out_ref):
    new = jnp.sum(norm_ref[:, 0, :], axis=0, keepdims=True)
    ratio = [
        new[:, 64 + p : 65 + p] / step_ref[0:1, 4 + p : 5 + p] / step_ref[0:1, p : p + 1] for p in range(trials)
    ]
    ratio = per_trial(trials, ratio)[:, 0:1]
    out_ref[...] = residual_ref[...] + ratio[None] * response_ref[...]


def density_kernel(norm_ref, coef_ref, packed_ref, o_ref, out_ref):
    curvature = norm_ref[0]
    for g in range(1, groups):
        curvature = curvature + norm_ref[g]
    alphas = fold_bands(coef_ref[:, 0, :], 4)
    steps = fold_bands(coef_ref[:, 0, :], 8) / jnp.where(curvature == 0.0, 1.0, curvature)
    blocks = [packed_ref[q * 36 : q * 36 + 36, :] for q in range(3)]
    fields = [*blocks, unpack_last(*blocks)]
    sums = [jnp.zeros((36, 128), f32) for _ in range(trials)]
    for v in range(bands):
        square = o_ref[v, :, :]
        square = square * square
        for p in range(trials):
            r, l = v % 8, 16 * (v // 8) + p
            step, alpha = steps[r : r + 1, l : l + 1], alphas[r : r + 1, l : l + 1]
            sums[p] = sums[p] + (step * (alpha - fields[p])) * square
    lane = lane_of((planes, 128))
    for p in range(trials):
        c = [sums[p][12 * i : 12 * i + 12] * (4.0 / bands) for i in range(3)]
        r1, r2 = pltpu.roll(c[1], 96, 1), pltpu.roll(c[2], 64, 1)
        out_ref[:, p, 0:128] = jnp.where(lane < 96, c[0], r1)
        out_ref[:, p, 128:256] = jnp.where(lane < 64, r1, r2)
        out_ref[:, p, 256:288] = r2[:, 0:32]


vmem = pl.BlockSpec(memory_space=pltpu.VMEM)
smem = pl.BlockSpec(memory_space=pltpu.SMEM)


def params(mebibytes):
    return pltpu.CompilerParams(vmem_limit_bytes=mebibytes * 1024 * 1024)


def shape(*dims, dtype=f32):
    return jax.ShapeDtypeStruct(dims, dtype)


def call(kernel, ins, outs, scratch=(), name=None, room=4):
    return pl.pallas_call(
        kernel, out_shape=outs, in_specs=ins, out_specs=jax.tree.map(lambda _: vmem, outs),
        scratch_shapes=scratch, compiler_params=params(room), name=name,
    )


def pack(trial, local):
    return call(pack_kernel, [vmem] * 2, shape(144, 128), name="pack")(jnp.transpose(trial, (1, 0, 2)), local)


def orbital_rows(orbitals):
    return call(orbital_kernel, [vmem], shape(rows, 128), name="orbital_rows")(orbitals)


def forward(me, gathered, o, tables):
    return call(
        forward_kernel, [smem] + [vmem] * 6,
        (shape(5, rows, 128), shape(rows, 128), shape(8, 128)),
        [pltpu.VMEM((rows, 640), bf16), pltpu.VMEM((rows, 640), bf16),
         pltpu.VMEM((rows, 128), f32), pltpu.VMEM((rows, 128), f32)],
        name="forward", room=8,
    )(me, gathered, o, *tables["w1"], *tables["g1"])


def local_sums(energies, fields, o, stat):
    return call(local_kernel, [smem] + [vmem] * 3, shape(8, 128), name="local_sums")(energies, fields, o, stat)


def waves(place, arrived, stat, sums, tables):
    return call(
        wave_kernel, [smem] + [vmem] * 7, (shape(rows, 128), shape(8, 128), shape(bands, 8, 128)), name="waves"
    )(place, arrived, stat, sums, *tables["g2"], *tables["g3"])


def image(energies, arrived, scal, fields, o, tables):
    return call(
        image_kernel, [smem] + [vmem] * 8,
        (shape(trials * rows, 128), shape(trials * rows, 128), shape(8, 128), shape(8, 128)),
        [pltpu.VMEM((rows, 128), f32), pltpu.VMEM((rows, 128), f32)],
        name="image", room=8,
    )(energies, arrived, scal, fields, o, *tables["g4"], *tables["w2"])


def share(norm, coefs):
    return call(share_kernel, [vmem] * 2, shape(groups, 8, 128), name="share")(norm, coefs)


steps_flat = 6
cell_block = pl.BlockSpec((planes, trials, points * points // steps_flat), lambda i: (0, 0, i))
cell_shape = shape(planes, trials, points * points)
small_block = pl.BlockSpec((8, 128), lambda i: (0, 0))


def flat(step, source, residual):
    block = pl.BlockSpec((trials * rows // steps_flat, 128), lambda i: (i, 0))
    return pl.pallas_call(
        flat_kernel, grid=(steps_flat,), in_specs=[small_block, block, block],
        out_specs=(cell_block, cell_block), out_shape=(cell_shape, cell_shape),
        compiler_params=params(8), name="flat",
        cost_estimate=pl.CostEstimate(flops=10**7, bytes_accessed=10**7, transcendentals=0),
    )(step, source, residual)


def direct(step, norms, response, residual):
    return pl.pallas_call(
        direction_kernel, grid=(steps_flat,),
        in_specs=[small_block, pl.BlockSpec((groups, 8, 128), lambda i: (0, 0, 0)), cell_block, cell_block],
        out_specs=cell_block, out_shape=cell_shape, compiler_params=params(8), name="direction",
    )(step, norms, response, residual)


def density_of(norms, coefs, packed, o):
    return call(density_kernel, [vmem] * 4, shape(planes, trials, 288), name="density")(norms, coefs, packed, o)


def outward(value):
    return jnp.transpose(value, (1, 0, 2))


def swapped(value, axis, size, mask):
    return lax.ppermute(value, axis, [(s, s ^ mask) for s in range(size)])


def gather_bands(packed):
    value = packed[None]
    for masks in ((8, 16, 24), (2, 4, 6), (1,)):
        value = jnp.concatenate([value] + [swapped(value, "band", bands, m) for m in masks], axis=0)
    return value


def on_device(orbitals, energies, local_pot, trial_pot):
    tables = {name: tuple(jnp.asarray(t) for t in pair) for name, pair in build_tables().items()}
    me = lax.axis_index("band").astype(jnp.int32).reshape(1)
    place = lax.axis_index("grid").astype(jnp.int32).reshape(1)
    packed = pack(trial_pot, local_pot)
    o = orbital_rows(orbitals)
    gathered = gather_bands(packed)
    o_bands = lax.all_to_all(o.reshape(bands, 36, 128), "band", 0, 0, tiled=True)
    fields, sent, stat = forward(me, gathered, o, tables)
    arrived = lax.all_to_all(sent.reshape(groups, chunk, 128), "grid", 0, 0, tiled=True).reshape(rows, 128)
    sums = local_sums(energies, fields, o, stat)
    back, scal, coef = waves(place, arrived, stat, sums, tables)
    back = lax.all_to_all(back.reshape(groups, chunk, 128), "grid", 0, 0, tiled=True).reshape(rows, 128)
    coefs = lax.all_to_all(coef, "band", 0, 0, tiled=True)
    source, residual, norm, step = image(energies, back, scal, fields, o, tables)
    norms = lax.all_to_all(share(norm, coefs), "grid", 0, 0, tiled=True)
    response, residual = flat(step, source, residual)
    direction = direct(step, norms, response, residual)
    density = density_of(norms, coefs, packed, o_bands)
    return outward(response)[None], outward(residual)[None], outward(direction)[None], outward(density)


def solution(mesh):
    return jax.shard_map(
        on_device,
        mesh=mesh,
        in_specs=(P("band", "grid", None), P("band"), P("grid", "band"), P(None, "grid", "band")),
        out_specs=(
            P("band", None, "grid", None),
            P("band", None, "grid", None),
            P("band", None, "grid", None),
            P(None, "grid", "band"),
        ),
        check_vma=False,
    )
```

```python
import math

import jax
import jax.numpy as jnp
import ml_dtypes
import numpy as np
from jax import lax
from jax.experimental import pallas as pl
from jax.experimental.pallas import tpu as pltpu
from jax.sharding import PartitionSpec as P

points = 96
planes = 12
trials = 4
bands = 32
half = 24
groups = 8
rows = points * planes
chunk = rows // groups
spacing = 0.49
prefactor = 0.5 * (2.0 * math.pi / (points * spacing)) ** 2
f32 = jnp.float32
bf16 = jnp.bfloat16


def split_np(table):
    table = np.asarray(table, np.float32)
    high = table.astype(ml_dtypes.bfloat16)
    low = (table - high.astype(np.float32)).astype(ml_dtypes.bfloat16)
    return np.stack([high, low])


def angle(a, b):
    return (np.outer(a, b) % points) * (2.0 * np.pi / points)


def build_tables():
    grid = np.arange(points)
    signed = np.arange(2 * half) - half
    kz = np.arange(half)
    w1 = np.zeros((5 * 128, 256))
    az = angle(grid, kz)
    for p in range(5):
        w1[p * 128 : p * 128 + points, p * half : (p + 1) * half] = np.cos(az)
        w1[p * 128 : p * 128 + points, 128 + p * half : 128 + (p + 1) * half] = -np.sin(az)
    order = np.zeros(points, np.int64)
    part = np.zeros(points, np.int64)
    for jj in range(6):
        for c in range(2):
            for g in range(groups):
                order[(2 * jj + c) * 8 + g] = signed[6 * g + jj]
                part[(2 * jj + c) * 8 + g] = c
    ay = angle(order, grid)
    real = part[:, None] == 0
    g1 = np.concatenate(
        [np.where(real, np.cos(ay), -np.sin(ay)), np.where(real, np.sin(ay), np.cos(ay))], 1
    )
    g4 = np.concatenate(
        [np.where(real, np.cos(ay), -np.sin(ay)), np.where(real, np.sin(ay), np.cos(ay))], 1
    ).T
    ax = angle(signed, grid)
    cx, sx = np.cos(ax), np.sin(ax)
    g2 = np.block([[cx, sx], [-sx, cx]])
    g3 = np.block([[cx.T, -sx.T], [sx.T, cx.T]])
    w2 = np.zeros((256, 4 * 128))
    for p in range(4):
        w2[p * half : (p + 1) * half, p * 128 : p * 128 + points] = np.cos(az).T
        w2[128 + p * half : 128 + (p + 1) * half, p * 128 : p * 128 + points] = -np.sin(az).T
    return {"w1": split_np(w1), "g1": split_np(g1), "g2": split_np(g2), "g3": split_np(g3),
            "g4": split_np(g4), "w2": split_np(w2)}


def dot(a, b):
    return lax.dot_general(a, b, (((1,), (0,)), ((), ())), preferred_element_type=f32)


def split(value):
    high = value.astype(bf16)
    return high, (value - high.astype(f32)).astype(bf16)


def left_table(table, value):
    vh, vl = split(value)
    return dot(table[0], vh) + dot(table[0], vl) + dot(table[1], vh)


def right_table(vh, vl, table):
    return dot(vh, table[0]) + dot(vl, table[0]) + dot(vh, table[1])


def begin(source, target, sem):
    copy = pltpu.make_async_copy(source, target, sem)
    copy.start()
    return copy


def lane_of(shape):
    return lax.broadcasted_iota(jnp.int32, shape, 1)


def row_of(shape):
    return lax.broadcasted_iota(jnp.int32, shape, 0)


def total(value):
    return jnp.sum(jnp.sum(value, axis=0, keepdims=True), axis=1, keepdims=True)


def fold(value):
    return jnp.sum(value.reshape(value.shape[0] // 8, 8, 128), axis=0)


def tile_of(shape, entries):
    row, lane = row_of(shape), lane_of(shape)
    out = jnp.zeros(shape, f32)
    for r, l, value in entries:
        out = jnp.where((row == r) & (lane == l), value, out)
    return out


def spread(t0, t1, t2):
    lane = lane_of(t0.shape)
    c1 = pltpu.roll(jnp.where(lane >= 96, t0, t1), 32, 1)
    c2 = pltpu.roll(jnp.where(lane >= 64, t1, t2), 64, 1)
    return t0, c1, c2


def pack_kernel(trial_ref, local_ref, out_ref):
    lane = lane_of((planes, 128))
    fill = jnp.zeros((planes, 96), f32)

    def pieces(ref, *at):
        t2 = jnp.concatenate([ref[(slice(None), *at, slice(256, 288))], fill], axis=1)
        return spread(ref[(slice(None), *at, slice(0, 128))], ref[(slice(None), *at, slice(128, 256))], t2)

    last = pieces(trial_ref, 3)
    for q in range(3):
        mine = pieces(trial_ref, q)
        for i in range(3):
            tail = pltpu.roll(last[i], 96 - 32 * q, 1)
            out_ref[q * 36 + i * 12 : q * 36 + i * 12 + 12, :] = jnp.where(lane < 96, mine[i], tail)
    mine = pieces(local_ref)
    for i in range(3):
        out_ref[108 + i * 12 : 120 + i * 12, :] = jnp.where(lane < 96, mine[i], 0.0)


def unpack_last(b0, b1, b2):
    lane = lane_of(b0.shape)
    r0, r1, r2 = pltpu.roll(b0, 32, 1), pltpu.roll(b1, 64, 1), pltpu.roll(b2, 96, 1)
    return jnp.where(lane < 32, r0, jnp.where(lane < 64, r1, r2))


def orbital_kernel(o_ref, packed_ref, far_out, base_out, packed_out, out_ref, base_ref, sems):
    kept = begin(packed_ref, packed_out, sems.at[0])
    lane = lane_of((planes, 128))
    for q in range(points // 4):
        t = [o_ref[0, :, 384 * q + 128 * i : 384 * q + 128 * i + 128] for i in range(3)]
        c = [*spread(*t), pltpu.roll(t[2], 96, 1)]
        for i in range(4):
            at = (4 * q + i) * planes
            out_ref[at : at + planes, :] = jnp.where(lane < 96, c[i], 0.0)
    for u in range(bands):
        mine = out_ref[u * 36 : u * 36 + 36, :]
        base_ref[u, 0:36, :] = mine
        base_ref[u, 36:40, :] = jnp.zeros((4, 128), f32)
    copies = [begin(out_ref, far_out, sems.at[2]), begin(base_ref, base_out, sems.at[1]), kept]
    for copy in copies:
        copy.wait()


def forward_kernel(p0, p1, p2, p3, p4, p5, p6, p7, o_far, w1_ref, g1_ref,
                   field_out, result_ref, stat_ref,
                   o_ref, field_ref, t_ref, w1, g1, out_ref, high, low, real, imag, sems):
    me = lax.axis_index("band")
    arrivals = [
        begin(piece, t_ref.at[pl.ds(4 * n, 4)], sems.at[n]) for n, piece in enumerate((p0, p1, p2, p3, p4, p5, p6, p7))
    ]
    arrivals.append(begin(o_far, o_ref, sems.at[10]))
    tables = [begin(w1_ref, w1, sems.at[8]), begin(g1_ref, g1, sems.at[9])]
    for copy in arrivals:
        copy.wait()
    norm = jnp.zeros((36, 128), f32)
    corr = [jnp.zeros((36, 128), f32) for _ in range(trials)]
    for u in range(bands):
        d = u ^ me
        slot = ((d & 1) << 4) | (((d >> 1) & 3) << 2) | (d >> 3)
        blocks = [t_ref[slot, q * 36 : q * 36 + 36, :] for q in range(4)]
        fields = [*blocks[:3], unpack_last(*blocks[:3]), blocks[3]]
        here = slice(u * 36, u * 36 + 36)
        for p in range(5):
            field_ref[p, here, :] = fields[p]
        o = o_ref[here, :]
        square = o * o
        norm = norm + square
        for p in range(trials):
            corr[p] = corr[p] + fields[p] * square
    kept = begin(field_ref, field_out, sems.at[1])
    norm = total(norm)
    mean = [total(c) / norm for c in corr]

    size = 96

    def weigh(i, sums):
        at = pl.ds(pl.multiple_of(i * size, size), size)
        o = o_ref[at, :]
        out = []
        for p in range(trials):
            w = (field_ref[p, at, :] - mean[p]) * o
            high[at, p * 128 : p * 128 + 128], low[at, p * 128 : p * 128 + 128] = split(w)
            out.append(sums[p] + fold(w * w))
        high[at, 512:640], low[at, 512:640] = split(o)
        return tuple(out)

    second = lax.fori_loop(0, rows // size, weigh, tuple(jnp.zeros((8, 128), f32) for _ in range(trials)))
    second = [total(s) for s in second]
    stat_ref[...] = tile_of((8, 128), [(0, 0, norm)] + [(0, 1 + p, mean[p]) for p in range(trials)])

    for copy in tables:
        copy.wait()
    big = 384

    def along_z(i, _):
        at = pl.ds(pl.multiple_of(i * big, big), big)
        a = right_table(high[at, :], low[at, :], w1)
        real[at, :] = a[:, :128]
        imag[at, :] = a[:, 128:]
        return 0

    lax.fori_loop(0, rows // big, along_z, 0)

    row, lane = row_of((points, 128)), lane_of((points, 128))
    ride = jnp.where((row < 8) & (lane == 120), norm, 0.0)
    for p in range(trials):
        ride = jnp.where((row < 8) & (lane == 121 + p), mean[p], ride)
        ride = jnp.where((row >= 8) & (row < 16) & (lane == 120 + p), second[p], ride)
    for x in range(0, planes, 2):
        parts = [
            jnp.concatenate([ref[pl.ds(x + i, points, stride=planes), :] for i in range(2)], axis=1)
            for ref in (real, imag)
        ]
        y = left_table(g1, jnp.concatenate(parts, axis=0))
        for i in range(2):
            mine = y[:, i * 128 : i * 128 + 128] + ride
            for r in range(12):
                out_ref[pl.ds((x + i) * 12 + r, groups, stride=chunk), :] = mine[8 * r : 8 * r + 8]
    begin(out_ref, result_ref, sems.at[0]).wait()
    kept.wait()


def local_kernel(energy_ref, field_ref, o_ref, stat_ref, g2_ref, g3_ref, g4_ref, w2_ref,
                 out_ref, g2, g3, g4, w2, sums, sems):
    step = pl.program_id(0)
    pairs = ((g2_ref, g2), (g3_ref, g3), (g4_ref, g4), (w2_ref, w2))

    @pl.when(step == 0)
    def _():
        sums[...] = jnp.zeros(sums.shape, f32)
        for n, (source, target) in enumerate(pairs):
            pltpu.make_async_copy(source, target, sems.at[n]).start()

    o = o_ref[...]
    shift = (field_ref[4] - energy_ref[0]) * o
    sums[0] += fold(shift * o)
    for p in range(trials):
        off = field_ref[p] - stat_ref[0:1, 1 + p : 2 + p]
        both = shift * off
        sums[1 + p] += fold(both * o)
        sums[5 + p] += fold(both * (off * o))

    @pl.when(step == pl.num_programs(0) - 1)
    def _():
        out_ref[...] = tile_of((8, 128), [(0, n, total(sums[n])) for n in range(9)])
        for n, (source, target) in enumerate(pairs):
            pltpu.make_async_copy(source, target, sems.at[n]).wait()


def wave_kernel(in_ref, stat_ref, sums_ref, g2, g3, base_ref, out_ref, scal_ref, tail_ref, sems):
    owner = lax.axis_index("grid")
    fetch = begin(base_ref.at[:, pl.ds(32, 8), :], tail_ref, sems.at[0])
    s0 = in_ref[pl.ds(0, points, stride=planes), :]
    s1 = in_ref[pl.ds(1, points, stride=planes), :]
    weight = s0[:, 120:121]
    whole = jnp.sum(weight, axis=0, keepdims=True)
    lane = lane_of((points, 128))
    coef = jnp.zeros((points, 128), f32)
    alpha, start = [], []
    for p in range(trials):
        mean = s0[:, 121 + p : 122 + p]
        a = jnp.sum(weight * mean, axis=0, keepdims=True) / whole
        off = a - mean
        spread_sum = jnp.sum(s1[:, 120 + p : 121 + p] + weight * off * off, axis=0, keepdims=True)
        alpha.append(a)
        start.append(spread_sum / planes)
        coef = jnp.where((lane >= p * half) & (lane < (p + 1) * half), off, coef)

    def source_of(r):
        d = in_ref[pl.ds(r, points, stride=planes), :]
        o = jnp.where((lane >= 96) & (lane < 120), d, 0.0)
        o = pltpu.roll(o, 32, 1)
        o = o + pltpu.roll(o, 24, 1)
        o = o + pltpu.roll(o, 48, 1)
        return jnp.where(lane < 96, coef * o - d, 0.0)

    wide = (2 * half, 128)
    m = row_of(wide) - half
    k = lane_of(wide)
    k = k - jnp.where(k >= 72, 72, jnp.where(k >= 48, 48, jnp.where(k >= 24, 24, 0)))
    doubled = jnp.where(k == 0, 1.0, 2.0) * (prefactor / float(points**3))
    energy = jnp.zeros((1, 128), f32)
    own = [jnp.where(lane_of((1, 128)) == 0, 0.0, 0.0)]
    for pair in (2, 1, 0):
        parts = [
            jnp.concatenate([source_of(2 * (2 * pair + i) + c) for i in range(2)], axis=1)
            for c in range(2)
        ]
        u = left_table(g2, jnp.concatenate(parts, axis=0))
        weights = []
        for i in range(2):
            j = owner * 6 + (2 * pair + i) - half
            square = m * m + k * k + j * j
            weights.append(jnp.where(square < half * half, doubled * square.astype(f32), 0.0))
        w = jnp.concatenate(weights, axis=1)
        t = u * jnp.concatenate([w, w], axis=0)
        product = jnp.sum(u * t, axis=0, keepdims=True)
        energy = energy + product[:, :128] + product[:, 128:]
        e = left_table(g3, t)
        if pair == 0:
            l1 = lane_of((1, 128))
            ride = jnp.zeros((1, 128), f32)
            entries = []
            for p in range(trials):
                kinetic = jnp.sum(jnp.where((l1 >= p * half) & (l1 < (p + 1) * half), energy, 0.0), axis=1, keepdims=True)
                off = alpha[p] - stat_ref[0:1, 1 + p : 2 + p]
                at_p = sums_ref[0:1, 5 + p : 6 + p] - 2.0 * off * sums_ref[0:1, 1 + p : 2 + p] + off * off * sums_ref[0:1, 0:1]
                ride = jnp.where(l1 == 96 + p, kinetic + at_p, ride)
                entries += [(0, p, alpha[p]), (0, 4 + p, start[p])]
            scal_ref[...] = tile_of((8, 128), entries)
            e = e + jnp.concatenate([ride, jnp.zeros((1, 128), f32)], axis=1)
        for i in range(2):
            for c in range(2):
                out_ref[pl.ds(2 * (2 * pair + i) + c, points, stride=planes), :] = (
                    e[c * points : (c + 1) * points, i * 128 : i * 128 + 128]
                )
    fetch.wait()


def step_kernel(in_ref, scal_ref, tail_ref, base_ref, step_ref, out_ref, tail, sems):
    shares = jnp.sum(in_ref[pl.ds(0, groups, stride=chunk), :], axis=0, keepdims=True)
    lane = lane_of((1, 128))
    start = jnp.where((lane >= 4) & (lane < 8), scal_ref[0:1, :], 0.0)
    curvature = pltpu.roll(jnp.where((lane >= 96) & (lane < 100), shares, 0.0), 36, 1)
    step = start / jnp.where((lane >= 4) & (lane < 8), curvature, 1.0)
    row = jnp.where(lane < 8, scal_ref[0:1, :], 0.0) + pltpu.roll(step, 4, 1)
    step_ref[...] = jnp.broadcast_to(row, (8, 128))
    last = jnp.where(row_of((8, 128)) == 4, row, 0.0)
    for v in range(bands):
        tail[v, :, :] = tail_ref[v, :, :] + last
    begin(tail, out_ref.at[:, pl.ds(32, 8), :], sems.at[0]).wait()


def image_kernel(energy_ref, in_ref, step_ref, field_far, o_far, g4, w2,
                 response_ref, residual_ref, norm_ref,
                 field_ref, o_ref, real, imag, mixed_s, mixed_r, flat_s, flat_r, sems, out_sems):
    energy = energy_ref[0]
    copies = [begin(field_far, field_ref, sems.at[0]), begin(o_far, o_ref, sems.at[1])]
    alpha = [step_ref[0:1, p : p + 1] for p in range(trials)]
    step = [step_ref[0:1, 8 + p : 9 + p] for p in range(trials)]
    for x in range(0, planes, 2):
        b = jnp.concatenate(
            [
                jnp.concatenate(
                    [in_ref[pl.ds((x + i) * 12 + r, groups, stride=chunk), :] for r in range(12)], axis=0
                )
                for i in range(2)
            ],
            axis=1,
        )
        v = left_table(g4, b)
        for i in range(2):
            real[pl.ds(x + i, points, stride=planes), :] = v[:points, i * 128 : i * 128 + 128]
            imag[pl.ds(x + i, points, stride=planes), :] = v[points:, i * 128 : i * 128 + 128]
    for copy in copies:
        copy.wait()
    size = 96
    mixed = planes * trials
    lane = lane_of((mixed, 128))

    def tiles(ref, q):
        c = [ref[(4 * q + i) * mixed : (4 * q + i + 1) * mixed, :] for i in range(4)]
        r1, r2, r3 = pltpu.roll(c[1], 96, 1), pltpu.roll(c[2], 64, 1), pltpu.roll(c[3], 32, 1)
        return jnp.where(lane < 96, c[0], r1), jnp.where(lane < 64, r1, r2), jnp.where(lane < 32, r2, r3)

    def back(i, sums):
        at = pl.ds(pl.multiple_of(i * size, size), size)
        vh, vl = split(jnp.concatenate([real[at, :], imag[at, :]], axis=1))
        kinetic = right_table(vh, vl, w2)
        o = o_ref[at, :]
        shift = field_ref[4, at, :] - energy
        out = []
        for p in range(trials):
            source = (alpha[p] - field_ref[p, at, :]) * o
            image = kinetic[:, p * 128 : p * 128 + 128] + shift * source
            residual = source - step[p] * image
            there = pl.ds(p, size, stride=trials)
            mixed_s[there, :] = step[p] * source
            mixed_r[there, :] = residual
            out.append(sums[p] + fold(residual * residual))
        for flat, ref in ((flat_s, mixed_s), (flat_r, mixed_r)):
            for q in range(2):
                for n, tile in enumerate(tiles(ref, q)):
                    flat[i, :, :, 384 * q + 128 * n : 384 * q + 128 * n + 128] = tile.reshape(planes, trials, 128)
        cells = pl.ds(pl.multiple_of(i * 768, 768), 768)
        begin(flat_s.at[i], response_ref.at[:, :, cells], out_sems.at[0, i])
        begin(flat_r.at[i], residual_ref.at[:, :, cells], out_sems.at[1, i])
        return tuple(out)

    sums = lax.fori_loop(0, rows // size, back, tuple(jnp.zeros((8, 128), f32) for _ in range(trials)))
    norm_ref[...] = tile_of((8, 128), [(0, p, total(s)) for p, s in enumerate(sums)])
    for i in range(rows // size):
        cells = pl.ds(i * 768, 768)
        pltpu.make_async_copy(flat_s.at[i], response_ref.at[:, :, cells], out_sems.at[0, i]).wait()
        pltpu.make_async_copy(flat_r.at[i], residual_ref.at[:, :, cells], out_sems.at[1, i]).wait()


def last_kernel(step_ref, n0, n1, n2, n3, n4, n5, n6, n7, packed_far, band_ref, response_ref, residual_ref,
                direction_ref, density_ref, packed_ref, bands_in, first, second, result, sems, out_sems):
    parts = 6
    width = points * points // parts
    arrival = begin(band_ref, bands_in, sems.at[2, 0])
    kept = begin(packed_far, packed_ref, sems.at[2, 1])
    loads = []
    for i in range(parts):
        cells = pl.ds(i * width, width)
        loads.append((begin(response_ref.at[:, :, cells], first.at[i], sems.at[0, i]),
                      begin(residual_ref.at[:, :, cells], second.at[i], sems.at[1, i])))
    new = n0[0:1, :]
    for part in (n1, n2, n3, n4, n5, n6, n7):
        new = new + part[0:1, :]
    ratio = [new[:, p : p + 1] / step_ref[0:1, 4 + p : 5 + p] / step_ref[0:1, 8 + p : 9 + p] for p in range(trials)]
    r = row_of((trials, 128))
    ratios = jnp.zeros((trials, 128), f32)
    for p in range(trials):
        ratios = jnp.where(r == p, ratio[p], ratios)
    ratios = ratios[:, 0:1][None]
    stores = []
    for i in range(parts):
        for copy in loads[i]:
            copy.wait()
        result[i, :, :, :] = second[i] + ratios * first[i]
        stores.append(begin(result.at[i], direction_ref.at[:, :, pl.ds(i * width, width)], out_sems.at[i]))
    arrival.wait()
    kept.wait()
    blocks = [packed_ref[q * 36 : q * 36 + 36, :] for q in range(3)]
    fields = [*blocks, unpack_last(*blocks)]
    sums = [jnp.zeros((36, 128), f32) for _ in range(trials)]
    for v in range(bands):
        square = bands_in[v, 0:36, :]
        square = square * square
        for p in range(trials):
            alpha, step = bands_in[v, 36:37, p : p + 1], bands_in[v, 36:37, 8 + p : 9 + p]
            sums[p] = sums[p] + (step * (alpha - fields[p])) * square
    lane = lane_of((planes, 128))
    for p in range(trials):
        c = [sums[p][12 * i : 12 * i + 12] * (4.0 / bands) for i in range(3)]
        r1, r2 = pltpu.roll(c[1], 96, 1), pltpu.roll(c[2], 64, 1)
        density_ref[:, p, 0:128] = jnp.where(lane < 96, c[0], r1)
        density_ref[:, p, 128:256] = jnp.where(lane < 64, r1, r2)
        density_ref[:, p, 256:288] = r2[:, 0:32]
    for copy in stores:
        copy.wait()


vmem = pl.BlockSpec(memory_space=pltpu.VMEM)
smem = pl.BlockSpec(memory_space=pltpu.SMEM)
hbm = pl.BlockSpec(memory_space=pl.ANY)
far = pl.BlockSpec(memory_space=pltpu.HBM)


BIG = 56000000
HUGE = 60000000


def shape(*dims, dtype=f32):
    return jax.ShapeDtypeStruct(dims, dtype)


def call(kernel, ins, outs, scratch=(), name=None, room=4 * 2**20, places=None, aliases=None, flops=10**6):
    return pl.pallas_call(
        kernel, out_shape=outs, in_specs=ins,
        out_specs=places if places is not None else jax.tree.map(lambda _: vmem, outs),
        scratch_shapes=scratch, compiler_params=pltpu.CompilerParams(vmem_limit_bytes=room), name=name, input_output_aliases=aliases or {},
        cost_estimate=pl.CostEstimate(flops=flops, bytes_accessed=10**6, transcendentals=0),
    )


def pack(trial, local):
    return call(pack_kernel, [vmem] * 2, shape(144, 128), name="pack")(jnp.transpose(trial, (1, 0, 2)), local)


def orbital_rows(orbitals, packed):
    return call(
        orbital_kernel, [vmem, vmem],
        (shape(rows, 128), shape(bands, 40, 128), shape(144, 128)),
        [buffer(rows, 128), buffer(bands, 40, 128), pltpu.SemaphoreType.DMA((3,))],
        name="orbital_rows", places=(far, far, far), room=BIG,
    )(orbitals, packed)


def buffer(*dims, dtype=f32):
    return pltpu.VMEM(dims, dtype)


def forward(pieces, o, tables):
    return call(
        forward_kernel, [far] * 11,
        (shape(5, rows, 128), shape(rows, 128), shape(8, 128)),
        [buffer(rows, 128), buffer(5, rows, 128), buffer(bands, 144, 128), buffer(2, 640, 256, dtype=bf16), buffer(2, 96, 192, dtype=bf16), buffer(rows, 128),
         buffer(rows, 640, dtype=bf16), buffer(rows, 640, dtype=bf16), buffer(rows, 128), buffer(rows, 128),
         pltpu.SemaphoreType.DMA((11,))],
        name="forward", room=HUGE, places=(far, far, vmem),
    )(*pieces, o, tables["w1"], tables["g1"])


def local_sums(energies, fields, o, stat, tables):
    size, count = 192, rows // 192
    tile = pl.BlockSpec((8, 128), lambda i: (0, 0))
    kinds = [tables[name] for name in ("g2", "g3", "g4", "w2")]
    return pl.pallas_call(
        local_kernel, grid=(count,),
        in_specs=[smem, pl.BlockSpec((5, size, 128), lambda i: (0, i, 0)), pl.BlockSpec((size, 128), lambda i: (i, 0)),
                  tile] + [far] * 4,
        out_specs=(tile, *[vmem] * 4),
        out_shape=(shape(8, 128), *[shape(*t.shape, dtype=bf16) for t in kinds]),
        scratch_shapes=[buffer(9, 8, 128), pltpu.SemaphoreType.DMA((4,))],
        compiler_params=pltpu.CompilerParams(vmem_limit_bytes=BIG), name="local_sums",
        cost_estimate=pl.CostEstimate(flops=10**7, bytes_accessed=10**7, transcendentals=0),
    )(energies, fields, o, stat, *kinds)


def waves(arrived, stat, sums, g2, g3, base):
    return call(
        wave_kernel, [vmem] * 5 + [far], (shape(rows, 128), shape(8, 128), shape(bands, 8, 128)),
        [pltpu.SemaphoreType.DMA((1,))], name="waves", room=8 * 2**20,
    )(arrived, stat, sums, g2, g3, base)


def steps(arrived, scal, tail, base):
    return call(
        step_kernel, [vmem] * 3 + [far], (shape(8, 128), shape(bands, 40, 128)),
        [buffer(bands, 8, 128), pltpu.SemaphoreType.DMA((1,))],
        name="steps", places=(vmem, far), aliases={3: 1},
    )(arrived, scal, tail, base)


def image(energies, arrived, step, fields, o, g4, w2):
    cells = shape(planes, trials, points * points)
    return call(
        image_kernel, [smem, vmem, vmem, far, far, vmem, vmem], (cells, cells, shape(8, 128)),
        [buffer(5, rows, 128), buffer(rows, 128), buffer(rows, 128), buffer(rows, 128),
         buffer(384, 128), buffer(384, 128),
         buffer(12, planes, trials, 768), buffer(12, planes, trials, 768),
         pltpu.SemaphoreType.DMA((2,)), pltpu.SemaphoreType.DMA((2, 12))],
        name="image", room=BIG, places=(far, far, vmem), flops=2 * 10**10,
    )(energies, arrived, step, fields, o, g4, w2)


def last(step, norms, packed, band, response, residual):
    cells = shape(planes, trials, points * points)
    part = buffer(6, planes, trials, points * points // 6)
    return call(
        last_kernel, [vmem] * 9 + [far] * 4, (cells, shape(planes, trials, 288)),
        [buffer(144, 128), buffer(bands, 40, 128), part, part, part, pltpu.SemaphoreType.DMA((3, 6)), pltpu.SemaphoreType.DMA((6,))],
        name="last", room=BIG, places=(far, vmem),
    )(step, *norms, packed, band, response, residual)


def outward(value):
    return jnp.transpose(value, (1, 0, 2))


def swapped(value, axis, size, mask):
    return lax.ppermute(value, axis, [(s, s ^ mask) for s in range(size)])


def gather_rows(packed):
    value = packed[None]
    return jnp.concatenate([value] + [swapped(value, "band", bands, m) for m in (8, 16, 24)], axis=0)


def gather_planes(quad):
    quads = [quad] + [swapped(quad, "band", bands, m) for m in (2, 4, 6)]
    return quads + [swapped(q, "band", bands, 1) for q in quads]


def on_device(orbitals, energies, local_pot, trial_pot):
    tables = {name: jnp.asarray(table) for name, table in build_tables().items()}
    packed = pack(trial_pot, local_pot)
    quad = gather_rows(packed)
    o_far, base, packed_far = orbital_rows(orbitals, packed)
    quad, o_far = lax.optimization_barrier((quad, o_far))
    pieces = gather_planes(quad)
    fields, sent, stat = forward(pieces, o_far, tables)
    arrived = lax.all_to_all(sent.reshape(groups, chunk, 128), "grid", 0, 0, tiled=True).reshape(rows, 128)
    sums, g2, g3, g4, w2 = local_sums(energies, fields, o_far, stat, tables)
    back, scal, tail = waves(arrived, stat, sums, g2, g3, base)
    back = lax.all_to_all(back.reshape(groups, chunk, 128), "grid", 0, 0, tiled=True).reshape(rows, 128)
    step, payload = steps(back, scal, tail, base)
    band = lax.all_to_all(payload, "band", 0, 0, tiled=True)
    response, residual, norm = image(energies, back, step, fields, o_far, g4, w2)
    norms = [norm] + [swapped(norm, "grid", groups, m) for m in range(1, groups)]
    direction, density = last(step, norms, packed_far, band, response, residual)
    return outward(response)[None], outward(residual)[None], outward(direction)[None], outward(density)


def solution(mesh):
    return jax.shard_map(
        on_device,
        mesh=mesh,
        in_specs=(P("band", "grid", None), P("band"), P("grid", "band"), P(None, "grid", "band")),
        out_specs=(
            P("band", None, "grid", None),
            P("band", None, "grid", None),
            P("band", None, "grid", None),
            P(None, "grid", "band"),
        ),
        check_vma=False,
    )
```

```python
import math

import jax
import jax.numpy as jnp
import ml_dtypes
import numpy as np
from jax import lax
from jax.experimental import pallas as pl
from jax.experimental.pallas import tpu as pltpu
from jax.sharding import PartitionSpec as P

points = 96
planes = 12
trials = 4
bands = 32
half = 24
groups = 8
rows = points * planes
chunk = rows // groups
spacing = 0.49
prefactor = 0.5 * (2.0 * math.pi / (points * spacing)) ** 2
f32 = jnp.float32
bf16 = jnp.bfloat16


def split_np(table):
    table = np.asarray(table, np.float32)
    high = table.astype(ml_dtypes.bfloat16)
    low = (table - high.astype(np.float32)).astype(ml_dtypes.bfloat16)
    return np.stack([high, low])


def angle(a, b):
    return (np.outer(a, b) % points) * (2.0 * np.pi / points)


def build_tables():
    grid = np.arange(points)
    signed = np.arange(2 * half) - half
    kz = np.arange(half)
    w1 = np.zeros((5 * 128, 256))
    az = angle(grid, kz)
    for p in range(5):
        w1[p * 128 : p * 128 + points, p * half : (p + 1) * half] = np.cos(az)
        w1[p * 128 : p * 128 + points, 128 + p * half : 128 + (p + 1) * half] = -np.sin(az)
    order = np.zeros(points, np.int64)
    part = np.zeros(points, np.int64)
    for jj in range(6):
        for c in range(2):
            for g in range(groups):
                order[(2 * jj + c) * 8 + g] = signed[6 * g + jj]
                part[(2 * jj + c) * 8 + g] = c
    ay = angle(order, grid)
    real = part[:, None] == 0
    g1 = np.concatenate(
        [np.where(real, np.cos(ay), -np.sin(ay)), np.where(real, np.sin(ay), np.cos(ay))], 1
    )
    g4 = np.concatenate(
        [np.where(real, np.cos(ay), -np.sin(ay)), np.where(real, np.sin(ay), np.cos(ay))], 1
    ).T
    ax = angle(signed, grid)
    cx, sx = np.cos(ax), np.sin(ax)
    g2 = np.block([[cx, sx], [-sx, cx]])
    g3 = np.block([[cx.T, -sx.T], [sx.T, cx.T]])
    w2 = np.zeros((256, 4 * 128))
    for p in range(4):
        w2[p * half : (p + 1) * half, p * 128 : p * 128 + points] = np.cos(az).T
        w2[128 + p * half : 128 + (p + 1) * half, p * 128 : p * 128 + points] = -np.sin(az).T
    return {"w1": split_np(w1), "g1": split_np(g1), "g2": split_np(g2), "g3": split_np(g3),
            "g4": split_np(g4), "w2": split_np(w2)}


def dot(a, b):
    return lax.dot_general(a, b, (((1,), (0,)), ((), ())), preferred_element_type=f32)


def split(value):
    high = value.astype(bf16)
    return high, (value - high.astype(f32)).astype(bf16)


def left_table(table, value):
    count = table.shape[1]
    vh, vl = split(value)
    both = dot(jnp.concatenate([table[0], table[1]], axis=0), vh)
    return both[:count] + both[count:] + dot(table[0], vl)


def right_table(vh, vl, table):
    count = vh.shape[0]
    both = dot(jnp.concatenate([vh, vl], axis=0), table[0])
    return both[:count] + both[count:] + dot(vh, table[1])


def begin(source, target, sem):
    copy = pltpu.make_async_copy(source, target, sem)
    copy.start()
    return copy


def lane_of(shape):
    return lax.broadcasted_iota(jnp.int32, shape, 1)


def row_of(shape):
    return lax.broadcasted_iota(jnp.int32, shape, 0)


def total(value):
    return jnp.sum(jnp.sum(value, axis=0, keepdims=True), axis=1, keepdims=True)


def fold(value):
    return jnp.sum(value.reshape(value.shape[0] // 8, 8, 128), axis=0)


def tile_of(shape, entries):
    row, lane = row_of(shape), lane_of(shape)
    out = jnp.zeros(shape, f32)
    for r, l, value in entries:
        out = jnp.where((row == r) & (lane == l), value, out)
    return out


def spread(t0, t1, t2):
    lane = lane_of(t0.shape)
    c1 = pltpu.roll(jnp.where(lane >= 96, t0, t1), 32, 1)
    c2 = pltpu.roll(jnp.where(lane >= 64, t1, t2), 64, 1)
    return t0, c1, c2


def pack_kernel(trial_far, local_far, out_ref, trial_ref, local_ref, sems):
    for copy in [begin(trial_far, trial_ref, sems.at[0]), begin(local_far, local_ref, sems.at[1])]:
        copy.wait()
    lane = lane_of((planes, 128))
    fill = jnp.zeros((planes, 96), f32)

    def pieces(ref, *at):
        t2 = jnp.concatenate([ref[(slice(None), *at, slice(256, 288))], fill], axis=1)
        return spread(ref[(slice(None), *at, slice(0, 128))], ref[(slice(None), *at, slice(128, 256))], t2)

    last = pieces(trial_ref, 3)
    for q in range(3):
        mine = pieces(trial_ref, q)
        for i in range(3):
            tail = pltpu.roll(last[i], 96 - 32 * q, 1)
            out_ref[q * 36 + i * 12 : q * 36 + i * 12 + 12, :] = jnp.where(lane < 96, mine[i], tail)
    mine = pieces(local_ref)
    for i in range(3):
        out_ref[108 + i * 12 : 120 + i * 12, :] = jnp.where(lane < 96, mine[i], 0.0)


def unpack_last(b0, b1, b2):
    lane = lane_of(b0.shape)
    r0, r1, r2 = pltpu.roll(b0, 32, 1), pltpu.roll(b1, 64, 1), pltpu.roll(b2, 96, 1)
    return jnp.where(lane < 32, r0, jnp.where(lane < 64, r1, r2))


def tighten(value):
    lane, tail = lane_of((9, 128)), value[27:36]
    return jnp.concatenate(
        [jnp.where(lane < 96, value[9 * t : 9 * t + 9], pltpu.roll(tail, 96 - 32 * t, 1)) for t in range(3)], axis=0
    )


def loosen(value):
    lane = lane_of((9, 128))
    r0, r1, r2 = (pltpu.roll(value[9 * t : 9 * t + 9], 32 + 32 * t, 1) for t in range(3))
    return jnp.concatenate([value, jnp.where(lane < 32, r0, jnp.where(lane < 64, r1, r2))], axis=0)


def orbital_kernel(o_ref, packed_ref, far_out, base_out, packed_out, out_ref, base_ref, sems):
    kept = begin(packed_ref, packed_out, sems.at[0])
    lane = lane_of((planes, 128))
    for q in range(points // 4):
        t = [o_ref[0, :, 384 * q + 128 * i : 384 * q + 128 * i + 128] for i in range(3)]
        c = [*spread(*t), pltpu.roll(t[2], 96, 1)]
        for i in range(4):
            at = (4 * q + i) * planes
            out_ref[at : at + planes, :] = jnp.where(lane < 96, c[i], 0.0)
    for u in range(bands):
        mine = out_ref[u * 36 : u * 36 + 36, :]
        base_ref[u, 0:27, :] = tighten(mine)
        base_ref[u, 27:32, :] = jnp.zeros((5, 128), f32)
    copies = [begin(out_ref, far_out, sems.at[2]), begin(base_ref, base_out, sems.at[1]), kept]
    for copy in copies:
        copy.wait()


def forward_kernel(p0, p1, p2, p3, p4, p5, p6, p7, o_far, w1_ref, g1_ref,
                   field_out, result_ref, stat_ref,
                   o_ref, field_ref, t_ref, w1, g1, out_ref, high, low, real, imag, sems):
    me = lax.axis_index("band")
    arrivals = [
        begin(piece, t_ref.at[pl.ds(4 * n, 4)], sems.at[n]) for n, piece in enumerate((p0, p1, p2, p3, p4, p5, p6, p7))
    ]
    arrivals.append(begin(o_far, o_ref, sems.at[10]))
    tables = [begin(w1_ref, w1, sems.at[8]), begin(g1_ref, g1, sems.at[9])]
    for copy in arrivals:
        copy.wait()
    norm = jnp.zeros((36, 128), f32)
    corr = [jnp.zeros((36, 128), f32) for _ in range(trials)]
    for u in range(bands):
        d = u ^ me
        along, across = (d >> 3, (d >> 1) & 3) if u & 1 else ((d >> 1) & 3, d >> 3)
        slot = ((d & 1) << 4) | (along << 2) | across
        blocks = [t_ref[slot, q * 36 : q * 36 + 36, :] for q in range(4)]
        fields = [*blocks[:3], unpack_last(*blocks[:3]), blocks[3]]
        here = slice(u * 36, u * 36 + 36)
        for p in range(5):
            field_ref[p, here, :] = fields[p]
        o = o_ref[here, :]
        square = o * o
        norm = norm + square
        for p in range(trials):
            corr[p] = corr[p] + fields[p] * square
    kept = begin(field_ref, field_out, sems.at[1])
    norm = total(norm)
    mean = [total(c) / norm for c in corr]

    size = 96

    def weigh(i, sums):
        at = pl.ds(pl.multiple_of(i * size, size), size)
        o = o_ref[at, :]
        out = []
        for p in range(trials):
            w = (field_ref[p, at, :] - mean[p]) * o
            high[at, p * 128 : p * 128 + 128], low[at, p * 128 : p * 128 + 128] = split(w)
            out.append(sums[p] + fold(w * w))
        high[at, 512:640], low[at, 512:640] = split(o)
        return tuple(out)

    second = lax.fori_loop(0, rows // size, weigh, tuple(jnp.zeros((8, 128), f32) for _ in range(trials)))
    second = [total(s) for s in second]
    stat_ref[...] = tile_of((8, 128), [(0, 0, norm)] + [(0, 1 + p, mean[p]) for p in range(trials)])

    for copy in tables:
        copy.wait()
    big = 384

    def along_z(i, _):
        at = pl.ds(pl.multiple_of(i * big, big), big)
        a = right_table(high[at, :], low[at, :], w1)
        real[at, :] = a[:, :128]
        imag[at, :] = a[:, 128:]
        return 0

    lax.fori_loop(0, rows // big, along_z, 0)

    row, lane = row_of((points, 128)), lane_of((points, 128))
    ride = jnp.where((row < 8) & (lane == 120), norm, 0.0)
    for p in range(trials):
        ride = jnp.where((row < 8) & (lane == 121 + p), mean[p], ride)
        ride = jnp.where((row >= 8) & (row < 16) & (lane == 120 + p), second[p], ride)
    for x in range(0, planes, 2):
        parts = [
            jnp.concatenate([ref[pl.ds(x + i, points, stride=planes), :] for i in range(2)], axis=1)
            for ref in (real, imag)
        ]
        y = left_table(g1, jnp.concatenate(parts, axis=0))
        for i in range(2):
            mine = y[:, i * 128 : i * 128 + 128] + ride
            for r in range(12):
                out_ref[pl.ds((x + i) * 12 + r, groups, stride=chunk), :] = mine[8 * r : 8 * r + 8]
    begin(out_ref, result_ref, sems.at[0]).wait()
    kept.wait()


def local_kernel(energy_ref, field_ref, o_ref, stat_ref, g2_ref, g3_ref, g4_ref, w2_ref,
                 out_ref, g2, g3, g4, w2, sums, sems):
    step = pl.program_id(0)
    pairs = ((g2_ref, g2), (g3_ref, g3), (g4_ref, g4), (w2_ref, w2))

    @pl.when(step == 0)
    def _():
        sums[...] = jnp.zeros(sums.shape, f32)
        for n, (source, target) in enumerate(pairs):
            pltpu.make_async_copy(source, target, sems.at[n]).start()

    o = o_ref[...]
    shift = (field_ref[4] - energy_ref[0]) * o
    sums[0] += fold(shift * o)
    for p in range(trials):
        off = field_ref[p] - stat_ref[0:1, 1 + p : 2 + p]
        both = shift * off
        sums[1 + p] += fold(both * o)
        sums[5 + p] += fold(both * (off * o))

    @pl.when(step == pl.num_programs(0) - 1)
    def _():
        out_ref[...] = tile_of((8, 128), [(0, n, total(sums[n])) for n in range(9)])
        for n, (source, target) in enumerate(pairs):
            pltpu.make_async_copy(source, target, sems.at[n]).wait()


def wave_kernel(in_ref, stat_ref, sums_ref, g2, g3, base_ref, out_ref, scal_ref, tail_ref, sems):
    owner = lax.axis_index("grid")
    fetch = begin(base_ref.at[:, pl.ds(24, 8), :], tail_ref, sems.at[0])
    s0 = in_ref[pl.ds(0, points, stride=planes), :]
    s1 = in_ref[pl.ds(1, points, stride=planes), :]
    weight = s0[:, 120:121]
    whole = jnp.sum(weight, axis=0, keepdims=True)
    lane = lane_of((points, 128))
    coef = jnp.zeros((points, 128), f32)
    alpha, start = [], []
    for p in range(trials):
        mean = s0[:, 121 + p : 122 + p]
        a = jnp.sum(weight * mean, axis=0, keepdims=True) / whole
        off = a - mean
        spread_sum = jnp.sum(s1[:, 120 + p : 121 + p] + weight * off * off, axis=0, keepdims=True)
        alpha.append(a)
        start.append(spread_sum / planes)
        coef = jnp.where((lane >= p * half) & (lane < (p + 1) * half), off, coef)

    def source_of(r):
        d = in_ref[pl.ds(r, points, stride=planes), :]
        o = jnp.where((lane >= 96) & (lane < 120), d, 0.0)
        o = pltpu.roll(o, 32, 1)
        o = o + pltpu.roll(o, 24, 1)
        o = o + pltpu.roll(o, 48, 1)
        return jnp.where(lane < 96, coef * o - d, 0.0)

    wide = (2 * half, 128)
    m = row_of(wide) - half
    k = lane_of(wide)
    k = k - jnp.where(k >= 72, 72, jnp.where(k >= 48, 48, jnp.where(k >= 24, 24, 0)))
    doubled = jnp.where(k == 0, 1.0, 2.0) * (prefactor / float(points**3))
    energy = jnp.zeros((1, 128), f32)
    own = [jnp.where(lane_of((1, 128)) == 0, 0.0, 0.0)]
    for pair in (2, 1, 0):
        parts = [
            jnp.concatenate([source_of(2 * (2 * pair + i) + c) for i in range(2)], axis=1)
            for c in range(2)
        ]
        u = left_table(g2, jnp.concatenate(parts, axis=0))
        weights = []
        for i in range(2):
            j = owner * 6 + (2 * pair + i) - half
            square = m * m + k * k + j * j
            weights.append(jnp.where(square < half * half, doubled * square.astype(f32), 0.0))
        w = jnp.concatenate(weights, axis=1)
        t = u * jnp.concatenate([w, w], axis=0)
        product = jnp.sum(u * t, axis=0, keepdims=True)
        energy = energy + product[:, :128] + product[:, 128:]
        e = left_table(g3, t)
        if pair == 0:
            l1 = lane_of((1, 128))
            ride = jnp.zeros((1, 128), f32)
            entries = []
            for p in range(trials):
                kinetic = jnp.sum(jnp.where((l1 >= p * half) & (l1 < (p + 1) * half), energy, 0.0), axis=1, keepdims=True)
                off = alpha[p] - stat_ref[0:1, 1 + p : 2 + p]
                at_p = sums_ref[0:1, 5 + p : 6 + p] - 2.0 * off * sums_ref[0:1, 1 + p : 2 + p] + off * off * sums_ref[0:1, 0:1]
                ride = jnp.where(l1 == 96 + p, kinetic + at_p, ride)
                entries += [(0, p, alpha[p]), (0, 4 + p, start[p])]
            scal_ref[...] = tile_of((8, 128), entries)
            e = e + jnp.concatenate([ride, jnp.zeros((1, 128), f32)], axis=1)
        for i in range(2):
            for c in range(2):
                out_ref[pl.ds(2 * (2 * pair + i) + c, points, stride=planes), :] = (
                    e[c * points : (c + 1) * points, i * 128 : i * 128 + 128]
                )
    fetch.wait()


def step_kernel(in_ref, scal_ref, tail_ref, base_ref, step_ref, out_ref, tail, sems):
    shares = jnp.sum(in_ref[pl.ds(0, groups, stride=chunk), :], axis=0, keepdims=True)
    lane = lane_of((1, 128))
    start = jnp.where((lane >= 4) & (lane < 8), scal_ref[0:1, :], 0.0)
    curvature = pltpu.roll(jnp.where((lane >= 96) & (lane < 100), shares, 0.0), 36, 1)
    step = start / jnp.where((lane >= 4) & (lane < 8), curvature, 1.0)
    row = jnp.where(lane < 8, scal_ref[0:1, :], 0.0) + pltpu.roll(step, 4, 1)
    step_ref[...] = jnp.broadcast_to(row, (8, 128))
    last = jnp.where(row_of((8, 128)) == 4, row, 0.0)
    for v in range(bands):
        tail[v, :, :] = tail_ref[v, :, :] + last
    begin(tail, out_ref.at[:, pl.ds(24, 8), :], sems.at[0]).wait()


def image_kernel(energy_ref, in_ref, step_ref, field_far, o_far, g4, w2,
                 response_ref, residual_ref, norm_ref,
                 field_ref, o_ref, real, imag, kinetic, mixed_s, mixed_r, flat_s, flat_r, sems, out_sems):
    energy = energy_ref[0]
    copies = [begin(field_far, field_ref, sems.at[0]), begin(o_far, o_ref, sems.at[1])]
    alpha = [step_ref[0:1, p : p + 1] for p in range(trials)]
    step = [step_ref[0:1, 8 + p : 9 + p] for p in range(trials)]
    for x in range(0, planes, 2):
        b = jnp.concatenate(
            [
                jnp.concatenate(
                    [in_ref[pl.ds((x + i) * 12 + r, groups, stride=chunk), :] for r in range(12)], axis=0
                )
                for i in range(2)
            ],
            axis=1,
        )
        v = left_table(g4, b)
        for i in range(2):
            real[pl.ds(x + i, points, stride=planes), :] = v[:points, i * 128 : i * 128 + 128]
            imag[pl.ds(x + i, points, stride=planes), :] = v[points:, i * 128 : i * 128 + 128]
    size = 96
    mixed = planes * trials
    lane = lane_of((mixed, 128))

    def tiles(ref, q):
        c = [ref[(4 * q + i) * mixed : (4 * q + i + 1) * mixed, :] for i in range(4)]
        r1, r2, r3 = pltpu.roll(c[1], 96, 1), pltpu.roll(c[2], 64, 1), pltpu.roll(c[3], 32, 1)
        return jnp.where(lane < 96, c[0], r1), jnp.where(lane < 64, r1, r2), jnp.where(lane < 32, r2, r3)

    big = 384

    def along_z(i, _):
        at = pl.ds(pl.multiple_of(i * big, big), big)
        vh, vl = split(jnp.concatenate([real[at, :], imag[at, :]], axis=1))
        kinetic[at, :] = right_table(vh, vl, w2)
        return 0

    lax.fori_loop(0, rows // big, along_z, 0)
    for copy in copies:
        copy.wait()

    def back(i, sums):
        at = pl.ds(pl.multiple_of(i * size, size), size)
        o = o_ref[at, :]
        shift = field_ref[4, at, :] - energy
        out = []
        for p in range(trials):
            source = (alpha[p] - field_ref[p, at, :]) * o
            image = kinetic[at, p * 128 : p * 128 + 128] + shift * source
            residual = source - step[p] * image
            there = pl.ds(p, size, stride=trials)
            mixed_s[there, :] = step[p] * source
            mixed_r[there, :] = residual
            out.append(sums[p] + fold(residual * residual))
        for flat, ref in ((flat_s, mixed_s), (flat_r, mixed_r)):
            for q in range(2):
                for n, tile in enumerate(tiles(ref, q)):
                    flat[i, :, :, 384 * q + 128 * n : 384 * q + 128 * n + 128] = tile.reshape(planes, trials, 128)
        cells = pl.ds(pl.multiple_of(i * 768, 768), 768)
        begin(flat_s.at[i], response_ref.at[:, :, cells], out_sems.at[0, i])
        begin(flat_r.at[i], residual_ref.at[:, :, cells], out_sems.at[1, i])
        return tuple(out)

    sums = lax.fori_loop(0, rows // size, back, tuple(jnp.zeros((8, 128), f32) for _ in range(trials)))
    norm_ref[...] = tile_of((8, 128), [(0, p, total(s)) for p, s in enumerate(sums)])
    for i in range(rows // size):
        cells = pl.ds(i * 768, 768)
        pltpu.make_async_copy(flat_s.at[i], response_ref.at[:, :, cells], out_sems.at[0, i]).wait()
        pltpu.make_async_copy(flat_r.at[i], residual_ref.at[:, :, cells], out_sems.at[1, i]).wait()


def last_kernel(step_ref, n0, n1, n2, n3, packed_far, band_ref, response_ref, residual_ref,
                direction_ref, density_ref, packed_ref, bands_in, first, second, result, sems, out_sems):
    parts = 6
    width = points * points // parts
    arrival = begin(band_ref, bands_in, sems.at[2, 0])
    kept = begin(packed_far, packed_ref, sems.at[2, 1])
    loads = []
    for i in range(parts):
        cells = pl.ds(i * width, width)
        loads.append((begin(response_ref.at[:, :, cells], first.at[i], sems.at[0, i]),
                      begin(residual_ref.at[:, :, cells], second.at[i], sems.at[1, i])))
    new = n0[0:1, :]
    for part in (n1, n2, n3):
        new = new + part[0:1, :]
    ratio = [new[:, p : p + 1] / step_ref[0:1, 4 + p : 5 + p] / step_ref[0:1, 8 + p : 9 + p] for p in range(trials)]
    r = row_of((trials, 128))
    ratios = jnp.zeros((trials, 128), f32)
    for p in range(trials):
        ratios = jnp.where(r == p, ratio[p], ratios)
    ratios = ratios[:, 0:1][None]
    stores = []
    for i in range(parts):
        for copy in loads[i]:
            copy.wait()
        result[i, :, :, :] = second[i] + ratios * first[i]
        stores.append(begin(result.at[i], direction_ref.at[:, :, pl.ds(i * width, width)], out_sems.at[i]))
    arrival.wait()
    kept.wait()
    blocks = [packed_ref[q * 36 : q * 36 + 36, :] for q in range(3)]
    fields = [tighten(field) for field in (*blocks, unpack_last(*blocks))]
    sums = [jnp.zeros((27, 128), f32) for _ in range(trials)]
    for v in range(bands):
        square = bands_in[v, 0:27, :]
        square = square * square
        for p in range(trials):
            alpha, step = bands_in[v, 28:29, p : p + 1], bands_in[v, 28:29, 8 + p : 9 + p]
            sums[p] = sums[p] + (step * (alpha - fields[p])) * square
    lane = lane_of((planes, 128))
    for p in range(trials):
        loose = loosen(sums[p]) * (4.0 / bands)
        c = [loose[12 * i : 12 * i + 12] for i in range(3)]
        r1, r2 = pltpu.roll(c[1], 96, 1), pltpu.roll(c[2], 64, 1)
        density_ref[:, p, 0:128] = jnp.where(lane < 96, c[0], r1)
        density_ref[:, p, 128:256] = jnp.where(lane < 64, r1, r2)
        density_ref[:, p, 256:288] = r2[:, 0:32]
    for copy in stores:
        copy.wait()


vmem = pl.BlockSpec(memory_space=pltpu.VMEM)
smem = pl.BlockSpec(memory_space=pltpu.SMEM)
hbm = pl.BlockSpec(memory_space=pl.ANY)
far = pl.BlockSpec(memory_space=pltpu.HBM)


BIG = 56000000
HUGE = 60000000


def shape(*dims, dtype=f32):
    return jax.ShapeDtypeStruct(dims, dtype)


def call(kernel, ins, outs, scratch=(), name=None, room=4 * 2**20, places=None, aliases=None, flops=10**6):
    return pl.pallas_call(
        kernel, out_shape=outs, in_specs=ins,
        out_specs=places if places is not None else jax.tree.map(lambda _: vmem, outs),
        scratch_shapes=scratch, compiler_params=pltpu.CompilerParams(vmem_limit_bytes=room), name=name, input_output_aliases=aliases or {},
        cost_estimate=pl.CostEstimate(flops=flops, bytes_accessed=10**6, transcendentals=0),
    )


def pack(trial, local):
    return call(
        pack_kernel, [far] * 2, shape(144, 128),
        [buffer(planes, trials, 288), buffer(planes, 288), pltpu.SemaphoreType.DMA((2,))], name="pack", room=66000000,
    )(jnp.transpose(trial, (1, 0, 2)), local)


def orbital_rows(orbitals, packed):
    return call(
        orbital_kernel, [vmem, vmem],
        (shape(rows, 128), shape(bands, 32, 128), shape(144, 128)),
        [buffer(rows, 128), buffer(bands, 32, 128), pltpu.SemaphoreType.DMA((3,))],
        name="orbital_rows", places=(far, far, far), room=BIG,
    )(orbitals, packed)


def buffer(*dims, dtype=f32):
    return pltpu.VMEM(dims, dtype)


def forward(pieces, o, tables):
    return call(
        forward_kernel, [far] * 11,
        (shape(5, rows, 128), shape(rows, 128), shape(8, 128)),
        [buffer(rows, 128), buffer(5, rows, 128), buffer(bands, 144, 128), buffer(2, 640, 256, dtype=bf16), buffer(2, 96, 192, dtype=bf16), buffer(rows, 128),
         buffer(rows, 640, dtype=bf16), buffer(rows, 640, dtype=bf16), buffer(rows, 128), buffer(rows, 128),
         pltpu.SemaphoreType.DMA((11,))],
        name="forward", room=HUGE, places=(far, far, vmem),
    )(*pieces, o, tables["w1"], tables["g1"])


def local_sums(energies, fields, o, stat, tables):
    size, count = 192, rows // 192
    tile = pl.BlockSpec((8, 128), lambda i: (0, 0))
    kinds = [tables[name] for name in ("g2", "g3", "g4", "w2")]
    return pl.pallas_call(
        local_kernel, grid=(count,),
        in_specs=[smem, pl.BlockSpec((5, size, 128), lambda i: (0, i, 0)), pl.BlockSpec((size, 128), lambda i: (i, 0)),
                  tile] + [far] * 4,
        out_specs=(tile, *[vmem] * 4),
        out_shape=(shape(8, 128), *[shape(*t.shape, dtype=bf16) for t in kinds]),
        scratch_shapes=[buffer(9, 8, 128), pltpu.SemaphoreType.DMA((4,))],
        compiler_params=pltpu.CompilerParams(vmem_limit_bytes=BIG), name="local_sums",
        cost_estimate=pl.CostEstimate(flops=10**7, bytes_accessed=10**7, transcendentals=0),
    )(energies, fields, o, stat, *kinds)


def waves(arrived, stat, sums, g2, g3, base):
    return call(
        wave_kernel, [vmem] * 5 + [far], (shape(rows, 128), shape(8, 128), shape(bands, 8, 128)),
        [pltpu.SemaphoreType.DMA((1,))], name="waves", room=8 * 2**20,
    )(arrived, stat, sums, g2, g3, base)


def steps(arrived, scal, tail, base):
    return call(
        step_kernel, [vmem] * 3 + [far], (shape(8, 128), shape(bands, 32, 128)),
        [buffer(bands, 8, 128), pltpu.SemaphoreType.DMA((1,))],
        name="steps", places=(vmem, far), aliases={3: 1},
    )(arrived, scal, tail, base)


def image(energies, arrived, step, fields, o, g4, w2):
    cells = shape(planes, trials, points * points)
    return call(
        image_kernel, [smem, vmem, vmem, far, far, vmem, vmem], (cells, cells, shape(8, 128)),
        [buffer(5, rows, 128), buffer(rows, 128), buffer(rows, 128), buffer(rows, 128), buffer(rows, 512),
         buffer(384, 128), buffer(384, 128),
         buffer(12, planes, trials, 768), buffer(12, planes, trials, 768),
         pltpu.SemaphoreType.DMA((2,)), pltpu.SemaphoreType.DMA((2, 12))],
        name="image", room=BIG, places=(far, far, vmem), flops=2 * 10**10,
    )(energies, arrived, step, fields, o, g4, w2)


def last(step, norms, packed, band, response, residual):
    cells = shape(planes, trials, points * points)
    part = buffer(6, planes, trials, points * points // 6)
    return call(
        last_kernel, [vmem] * 5 + [far, hbm, far, far], (cells, shape(planes, trials, 288)),
        [buffer(144, 128), buffer(bands, 32, 128), part, part, part, pltpu.SemaphoreType.DMA((3, 6)), pltpu.SemaphoreType.DMA((6,))],
        name="last", room=BIG, places=(far, vmem),
    )(step, *norms, packed, band, response, residual)


def outward(value):
    return jnp.transpose(value, (1, 0, 2))


def swapped(value, axis, size, mask):
    return lax.ppermute(value, axis, [(s, s ^ mask) for s in range(size)])


def crossed(value, even, odd):
    return lax.ppermute(value, "band", [(s, s ^ (odd if s & 1 else even)) for s in range(bands)])


along_z, along_y = (8, 16, 24), (2, 4, 6)


def gather_first(packed):
    value = packed[None]
    return jnp.concatenate([value] + [crossed(value, z, y) for z, y in zip(along_z, along_y)], axis=0)


def gather_second(quad):
    quads = [quad] + [crossed(quad, y, z) for z, y in zip(along_z, along_y)]
    return quads + [swapped(q, "band", bands, 1) for q in quads]


def on_device(orbitals, energies, local_pot, trial_pot):
    tables = {name: jnp.asarray(table) for name, table in build_tables().items()}
    packed = pack(trial_pot, local_pot)
    quad = gather_first(packed)
    o_far, base, packed_far = orbital_rows(orbitals, packed)
    quad, o_far = lax.optimization_barrier((quad, o_far))
    pieces = gather_second(quad)
    fields, sent, stat = forward(pieces, o_far, tables)
    arrived = lax.all_to_all(sent.reshape(groups, chunk, 128), "grid", 0, 0, tiled=True).reshape(rows, 128)
    sums, g2, g3, g4, w2 = local_sums(energies, fields, o_far, stat, tables)
    back, scal, tail = waves(arrived, stat, sums, g2, g3, base)
    back = lax.all_to_all(back.reshape(groups, chunk, 128), "grid", 0, 0, tiled=True).reshape(rows, 128)
    step, payload = steps(back, scal, tail, base)
    band = lax.all_to_all(payload, "band", 0, 0, tiled=True)
    response, residual, norm = image(energies, back, step, fields, o_far, g4, w2)
    norm = norm + swapped(norm, "grid", groups, 1)
    norms = [norm] + [swapped(norm, "grid", groups, m) for m in (2, 4, 6)]
    direction, density = last(step, norms, packed_far, band, response, residual)
    return outward(response)[None], outward(residual)[None], outward(direction)[None], outward(density)


def solution(mesh):
    return jax.shard_map(
        on_device,
        mesh=mesh,
        in_specs=(P("band", "grid", None), P("band"), P("grid", "band"), P(None, "grid", "band")),
        out_specs=(
            P("band", None, "grid", None),
            P("band", None, "grid", None),
            P("band", None, "grid", None),
            P(None, "grid", "band"),
        ),
        check_vma=False,
    )
```

```python
import math

import jax
import jax.numpy as jnp
import ml_dtypes
import numpy as np
from jax import lax
from jax.experimental import pallas as pl
from jax.experimental.pallas import tpu as pltpu
from jax.sharding import PartitionSpec as P

points = 96
planes = 12
trials = 4
bands = 32
half = 24
groups = 8
rows = points * planes
chunk = rows // groups
returned = 112
spacing = 0.49
prefactor = 0.5 * (2.0 * math.pi / (points * spacing)) ** 2
f32 = jnp.float32
bf16 = jnp.bfloat16


def split_np(table):
    table = np.asarray(table, np.float32)
    high = table.astype(ml_dtypes.bfloat16)
    low = (table - high.astype(np.float32)).astype(ml_dtypes.bfloat16)
    return np.stack([high, low])


def angle(a, b):
    return (np.outer(a, b) % points) * (2.0 * np.pi / points)


def build_tables():
    grid = np.arange(points)
    signed = np.arange(2 * half) - half
    kz = np.arange(half)
    w1 = np.zeros((5 * 128, 256))
    az = angle(grid, kz)
    for p in range(5):
        w1[p * 128 : p * 128 + points, p * half : (p + 1) * half] = np.cos(az)
        w1[p * 128 : p * 128 + points, 128 + p * half : 128 + (p + 1) * half] = -np.sin(az)
    order = np.zeros(points, np.int64)
    part = np.zeros(points, np.int64)
    for jj in range(6):
        for c in range(2):
            for g in range(groups):
                order[(2 * jj + c) * 8 + g] = signed[6 * g + jj]
                part[(2 * jj + c) * 8 + g] = c
    ay = angle(order, grid)
    real = part[:, None] == 0
    g1 = np.concatenate(
        [np.where(real, np.cos(ay), -np.sin(ay)), np.where(real, np.sin(ay), np.cos(ay))], 1
    )
    g4 = np.concatenate(
        [np.where(real, np.cos(ay), -np.sin(ay)), np.where(real, np.sin(ay), np.cos(ay))], 1
    ).T
    ax = angle(signed, grid)
    cx, sx = np.cos(ax), np.sin(ax)
    g2 = np.block([[cx, sx], [-sx, cx]])
    g3 = np.block([[cx.T, -sx.T], [sx.T, cx.T]])
    w2 = np.zeros((256, 4 * 128))
    for p in range(4):
        w2[p * half : (p + 1) * half, p * 128 : p * 128 + points] = np.cos(az).T
        w2[128 + p * half : 128 + (p + 1) * half, p * 128 : p * 128 + points] = -np.sin(az).T
    return {"w1": split_np(w1), "g1": split_np(g1), "g2": split_np(g2), "g3": split_np(g3),
            "g4": split_np(g4), "w2": split_np(w2)}


def dot(a, b):
    return lax.dot_general(a, b, (((1,), (0,)), ((), ())), preferred_element_type=f32)


def split(value):
    high = value.astype(bf16)
    return high, (value - high.astype(f32)).astype(bf16)


def left_table(table, value):
    count = table.shape[1]
    vh, vl = split(value)
    both = dot(jnp.concatenate([table[0], table[1]], axis=0), vh)
    return both[:count] + both[count:] + dot(table[0], vl)


def right_table(vh, vl, table):
    count = vh.shape[0]
    both = dot(jnp.concatenate([vh, vl], axis=0), table[0])
    return both[:count] + both[count:] + dot(vh, table[1])


def begin(source, target, sem):
    copy = pltpu.make_async_copy(source, target, sem)
    copy.start()
    return copy


def lane_of(shape):
    return lax.broadcasted_iota(jnp.int32, shape, 1)


def row_of(shape):
    return lax.broadcasted_iota(jnp.int32, shape, 0)


def total(value):
    return jnp.sum(jnp.sum(value, axis=0, keepdims=True), axis=1, keepdims=True)


def fold(value):
    return jnp.sum(value.reshape(value.shape[0] // 8, 8, 128), axis=0)


def tile_of(shape, entries):
    row, lane = row_of(shape), lane_of(shape)
    out = jnp.zeros(shape, f32)
    for r, l, value in entries:
        out = jnp.where((row == r) & (lane == l), value, out)
    return out


def spread(t0, t1, t2):
    lane = lane_of(t0.shape)
    c1 = pltpu.roll(jnp.where(lane >= 96, t0, t1), 32, 1)
    c2 = pltpu.roll(jnp.where(lane >= 64, t1, t2), 64, 1)
    return t0, c1, c2


def pack_kernel(trial_far, local_far, out_ref, trial_ref, local_ref, sems):
    for copy in [begin(trial_far, trial_ref, sems.at[0]), begin(local_far, local_ref, sems.at[1])]:
        copy.wait()
    lane = lane_of((planes, 128))
    fill = jnp.zeros((planes, 96), f32)

    def pieces(ref, *at):
        t2 = jnp.concatenate([ref[(slice(None), *at, slice(256, 288))], fill], axis=1)
        return spread(ref[(slice(None), *at, slice(0, 128))], ref[(slice(None), *at, slice(128, 256))], t2)

    last = pieces(trial_ref, 3)
    for q in range(3):
        mine = pieces(trial_ref, q)
        for i in range(3):
            tail = pltpu.roll(last[i], 96 - 32 * q, 1)
            out_ref[q * 36 + i * 12 : q * 36 + i * 12 + 12, :] = jnp.where(lane < 96, mine[i], tail)
    mine = pieces(local_ref)
    for i in range(3):
        out_ref[108 + i * 12 : 120 + i * 12, :] = jnp.where(lane < 96, mine[i], 0.0)


def unpack_last(b0, b1, b2):
    lane = lane_of(b0.shape)
    r0, r1, r2 = pltpu.roll(b0, 32, 1), pltpu.roll(b1, 64, 1), pltpu.roll(b2, 96, 1)
    return jnp.where(lane < 32, r0, jnp.where(lane < 64, r1, r2))


def tighten(value):
    lane, tail = lane_of((9, 128)), value[27:36]
    return jnp.concatenate(
        [jnp.where(lane < 96, value[9 * t : 9 * t + 9], pltpu.roll(tail, 96 - 32 * t, 1)) for t in range(3)], axis=0
    )


def loosen(value):
    lane = lane_of((9, 128))
    r0, r1, r2 = (pltpu.roll(value[9 * t : 9 * t + 9], 32 + 32 * t, 1) for t in range(3))
    return jnp.concatenate([value, jnp.where(lane < 32, r0, jnp.where(lane < 64, r1, r2))], axis=0)


def orbital_kernel(o_ref, packed_ref, far_out, base_out, packed_out, out_ref, base_ref, sems):
    kept = begin(packed_ref, packed_out, sems.at[0])
    lane = lane_of((planes, 128))
    for q in range(points // 4):
        t = [o_ref[0, :, 384 * q + 128 * i : 384 * q + 128 * i + 128] for i in range(3)]
        c = [*spread(*t), pltpu.roll(t[2], 96, 1)]
        for i in range(4):
            at = (4 * q + i) * planes
            out_ref[at : at + planes, :] = jnp.where(lane < 96, c[i], 0.0)
    for u in range(bands):
        mine = out_ref[u * 36 : u * 36 + 36, :]
        base_ref[u, 0:27, :] = tighten(mine)
        base_ref[u, 27:32, :] = jnp.zeros((5, 128), f32)
    copies = [begin(out_ref, far_out, sems.at[2]), begin(base_ref, base_out, sems.at[1]), kept]
    for copy in copies:
        copy.wait()


def forward_kernel(p0, p1, p2, p3, p4, p5, p6, p7, o_far, w1_ref, g1_ref,
                   field_out, result_ref, stat_ref,
                   o_ref, field_ref, t_ref, w1, g1, out_ref, high, low, real, imag, sems):
    me = lax.axis_index("band")
    arrivals = [
        begin(piece, t_ref.at[pl.ds(4 * n, 4)], sems.at[n]) for n, piece in enumerate((p0, p1, p2, p3, p4, p5, p6, p7))
    ]
    arrivals.append(begin(o_far, o_ref, sems.at[10]))
    tables = [begin(w1_ref, w1, sems.at[8]), begin(g1_ref, g1, sems.at[9])]
    for copy in arrivals:
        copy.wait()
    norm = jnp.zeros((36, 128), f32)
    corr = [jnp.zeros((36, 128), f32) for _ in range(trials)]
    for u in range(bands):
        d = u ^ me
        z, y = d >> 3, (d >> 1) & 3
        if u & 1:
            z, y = (z >> 1) | ((y >> 1) << 1), ((z ^ (z >> 1)) & 1) | (((y ^ (y >> 1)) & 1) << 1)
            along, across = z, y
        else:
            along, across = y, z
        slot = ((d & 1) << 4) | (along << 2) | across
        blocks = [t_ref[slot, q * 36 : q * 36 + 36, :] for q in range(4)]
        fields = [*blocks[:3], unpack_last(*blocks[:3]), blocks[3]]
        here = slice(u * 36, u * 36 + 36)
        for p in range(5):
            field_ref[p, here, :] = fields[p]
        o = o_ref[here, :]
        square = o * o
        norm = norm + square
        for p in range(trials):
            corr[p] = corr[p] + fields[p] * square
    kept = begin(field_ref, field_out, sems.at[1])
    norm = total(norm)
    mean = [total(c) / norm for c in corr]

    size = 96

    def weigh(i, sums):
        at = pl.ds(pl.multiple_of(i * size, size), size)
        o = o_ref[at, :]
        out = []
        for p in range(trials):
            w = (field_ref[p, at, :] - mean[p]) * o
            high[at, p * 128 : p * 128 + 128], low[at, p * 128 : p * 128 + 128] = split(w)
            out.append(sums[p] + fold(w * w))
        high[at, 512:640], low[at, 512:640] = split(o)
        return tuple(out)

    second = lax.fori_loop(0, rows // size, weigh, tuple(jnp.zeros((8, 128), f32) for _ in range(trials)))
    second = [total(s) for s in second]
    stat_ref[...] = tile_of((8, 128), [(0, 0, norm)] + [(0, 1 + p, mean[p]) for p in range(trials)])

    for copy in tables:
        copy.wait()
    big = 384

    def along_z(i, _):
        at = pl.ds(pl.multiple_of(i * big, big), big)
        a = right_table(high[at, :], low[at, :], w1)
        real[at, :] = a[:, :128]
        imag[at, :] = a[:, 128:]
        return 0

    lax.fori_loop(0, rows // big, along_z, 0)

    row, lane = row_of((points, 128)), lane_of((points, 128))
    ride = jnp.where((row < 8) & (lane == 120), norm, 0.0)
    for p in range(trials):
        ride = jnp.where((row < 8) & (lane == 121 + p), mean[p], ride)
        ride = jnp.where((row >= 8) & (row < 16) & (lane == 120 + p), second[p], ride)
    for x in range(0, planes, 2):
        parts = [
            jnp.concatenate([ref[pl.ds(x + i, points, stride=planes), :] for i in range(2)], axis=1)
            for ref in (real, imag)
        ]
        y = left_table(g1, jnp.concatenate(parts, axis=0))
        for i in range(2):
            mine = y[:, i * 128 : i * 128 + 128] + ride
            for r in range(12):
                out_ref[pl.ds((x + i) * 12 + r, groups, stride=chunk), :] = mine[8 * r : 8 * r + 8]
    begin(out_ref, result_ref, sems.at[0]).wait()
    kept.wait()


def local_kernel(energy_ref, field_ref, o_ref, stat_ref, g2_ref, g3_ref, g4_ref, w2_ref,
                 out_ref, g2, g3, g4, w2, sums, sems):
    step = pl.program_id(0)
    pairs = ((g2_ref, g2), (g3_ref, g3), (g4_ref, g4), (w2_ref, w2))

    @pl.when(step == 0)
    def _():
        sums[...] = jnp.zeros(sums.shape, f32)
        for n, (source, target) in enumerate(pairs):
            pltpu.make_async_copy(source, target, sems.at[n]).start()

    o = o_ref[...]
    shift = (field_ref[4] - energy_ref[0]) * o
    sums[0] += fold(shift * o)
    for p in range(trials):
        off = field_ref[p] - stat_ref[0:1, 1 + p : 2 + p]
        both = shift * off
        sums[1 + p] += fold(both * o)
        sums[5 + p] += fold(both * (off * o))

    @pl.when(step == pl.num_programs(0) - 1)
    def _():
        out_ref[...] = tile_of((8, 128), [(0, n, total(sums[n])) for n in range(9)])
        for n, (source, target) in enumerate(pairs):
            pltpu.make_async_copy(source, target, sems.at[n]).wait()


def wave_kernel(in_ref, stat_ref, sums_ref, g2, g3, base_ref, out_ref, scal_ref, tail_ref, sems):
    owner = lax.axis_index("grid")
    fetch = begin(base_ref.at[:, pl.ds(24, 8), :], tail_ref, sems.at[0])
    s0 = in_ref[pl.ds(0, points, stride=planes), :]
    s1 = in_ref[pl.ds(1, points, stride=planes), :]
    weight = s0[:, 120:121]
    whole = jnp.sum(weight, axis=0, keepdims=True)
    lane = lane_of((points, 128))
    coef = jnp.zeros((points, 128), f32)
    alpha, start = [], []
    for p in range(trials):
        mean = s0[:, 121 + p : 122 + p]
        a = jnp.sum(weight * mean, axis=0, keepdims=True) / whole
        off = a - mean
        spread_sum = jnp.sum(s1[:, 120 + p : 121 + p] + weight * off * off, axis=0, keepdims=True)
        alpha.append(a)
        start.append(spread_sum / planes)
        coef = jnp.where((lane >= p * half) & (lane < (p + 1) * half), off, coef)

    def source_of(r):
        d = in_ref[pl.ds(r, points, stride=planes), :]
        o = jnp.where((lane >= 96) & (lane < 120), d, 0.0)
        o = pltpu.roll(o, 32, 1)
        o = o + pltpu.roll(o, 24, 1)
        o = o + pltpu.roll(o, 48, 1)
        return jnp.where(lane < 96, coef * o - d, 0.0)

    wide = (2 * half, 128)
    m = row_of(wide) - half
    k = lane_of(wide)
    k = k - jnp.where(k >= 72, 72, jnp.where(k >= 48, 48, jnp.where(k >= 24, 24, 0)))
    doubled = jnp.where(k == 0, 1.0, 2.0) * (prefactor / float(points**3))
    energy = jnp.zeros((1, 128), f32)
    own = [jnp.where(lane_of((1, 128)) == 0, 0.0, 0.0)]
    tails, directs = [], []
    for pair in (2, 1, 0):
        parts = [
            jnp.concatenate([source_of(2 * (2 * pair + i) + c) for i in range(2)], axis=1)
            for c in range(2)
        ]
        u = left_table(g2, jnp.concatenate(parts, axis=0))
        weights = []
        for i in range(2):
            j = owner * 6 + (2 * pair + i) - half
            square = m * m + k * k + j * j
            weights.append(jnp.where(square < half * half, doubled * square.astype(f32), 0.0))
        w = jnp.concatenate(weights, axis=1)
        t = u * jnp.concatenate([w, w], axis=0)
        product = jnp.sum(u * t, axis=0, keepdims=True)
        energy = energy + product[:, :128] + product[:, 128:]
        e = left_table(g3, t)
        for i in range(2):
            for c in range(2):
                r = 2 * (2 * pair + i) + c
                value = e[c * points : (c + 1) * points, i * 128 : i * 128 + 128]
                if r >= 9:
                    tails.append((r - 9, value))
                else:
                    directs.append((r, value))
        if pair == 2:
            tails = [value for _, value in sorted(tails, key=lambda entry: entry[0])]
        for r, value in directs:
            spare = pltpu.roll(tails[r // 3], 96 - 32 * (r % 3), 1)
            value = jnp.where(lane < 96, value, spare)
            for g in range(groups):
                out_ref[pl.ds(g * returned + r, planes, stride=9), :] = value[planes * g : planes * g + planes]
        directs = []
    l1 = lane_of((1, 128))
    ride = jnp.zeros((1, 128), f32)
    entries = []
    for p in range(trials):
        kinetic = jnp.sum(jnp.where((l1 >= p * half) & (l1 < (p + 1) * half), energy, 0.0), axis=1, keepdims=True)
        off = alpha[p] - stat_ref[0:1, 1 + p : 2 + p]
        at_p = sums_ref[0:1, 5 + p : 6 + p] - 2.0 * off * sums_ref[0:1, 1 + p : 2 + p] + off * off * sums_ref[0:1, 0:1]
        ride = jnp.where(l1 == 96 + p, kinetic + at_p, ride)
        entries += [(0, p, alpha[p]), (0, 4 + p, start[p])]
    scal_ref[...] = tile_of((8, 128), entries)
    for g in range(groups):
        out_ref[g * returned + 108 : g * returned + 112, :] = jnp.broadcast_to(ride, (4, 128))
    fetch.wait()


def step_kernel(in_ref, scal_ref, tail_ref, base_ref, step_ref, out_ref, tail, sems):
    shares = jnp.sum(in_ref[pl.ds(108, groups, stride=returned), :], axis=0, keepdims=True)
    lane = lane_of((1, 128))
    start = jnp.where((lane >= 4) & (lane < 8), scal_ref[0:1, :], 0.0)
    curvature = pltpu.roll(jnp.where((lane >= 96) & (lane < 100), shares, 0.0), 36, 1)
    step = start / jnp.where((lane >= 4) & (lane < 8), curvature, 1.0)
    row = jnp.where(lane < 8, scal_ref[0:1, :], 0.0) + pltpu.roll(step, 4, 1)
    step_ref[...] = jnp.broadcast_to(row, (8, 128))
    last = jnp.where(row_of((8, 128)) == 4, row, 0.0)
    for v in range(bands):
        tail[v, :, :] = tail_ref[v, :, :] + last
    begin(tail, out_ref.at[:, pl.ds(24, 8), :], sems.at[0]).wait()


def image_kernel(energy_ref, in_ref, step_ref, field_far, o_far, g4, w2,
                 response_ref, residual_ref, norm_ref,
                 field_ref, o_ref, real, imag, kinetic, mixed_s, mixed_r, flat_s, flat_r, sems, out_sems):
    energy = energy_ref[0]
    copies = [begin(field_far, field_ref, sems.at[0]), begin(o_far, o_ref, sems.at[1])]
    alpha = [step_ref[0:1, p : p + 1] for p in range(trials)]
    step = [step_ref[0:1, 8 + p : 9 + p] for p in range(trials)]
    narrow = lane_of((groups, 128))

    def waves_of(x):
        r = [in_ref[pl.ds(x * 9 + n, groups, stride=returned), :] for n in range(9)]
        for n in range(3):
            r0, r1, r2 = (pltpu.roll(r[3 * n + t], 32 + 32 * t, 1) for t in range(3))
            r.append(jnp.where(narrow < 32, r0, jnp.where(narrow < 64, r1, r2)))
        return jnp.concatenate(r, axis=0)

    for x in range(0, planes, 2):
        b = jnp.concatenate([waves_of(x), waves_of(x + 1)], axis=1)
        v = left_table(g4, b)
        for i in range(2):
            real[pl.ds(x + i, points, stride=planes), :] = v[:points, i * 128 : i * 128 + 128]
            imag[pl.ds(x + i, points, stride=planes), :] = v[points:, i * 128 : i * 128 + 128]
    size = 96
    mixed = planes * trials
    lane = lane_of((mixed, 128))

    def tiles(ref, q):
        c = [ref[(4 * q + i) * mixed : (4 * q + i + 1) * mixed, :] for i in range(4)]
        r1, r2, r3 = pltpu.roll(c[1], 96, 1), pltpu.roll(c[2], 64, 1), pltpu.roll(c[3], 32, 1)
        return jnp.where(lane < 96, c[0], r1), jnp.where(lane < 64, r1, r2), jnp.where(lane < 32, r2, r3)

    big = 384

    def along_z(i, _):
        at = pl.ds(pl.multiple_of(i * big, big), big)
        vh, vl = split(jnp.concatenate([real[at, :], imag[at, :]], axis=1))
        kinetic[at, :] = right_table(vh, vl, w2)
        return 0

    lax.fori_loop(0, rows // big, along_z, 0)
    for copy in copies:
        copy.wait()

    def back(i, sums):
        at = pl.ds(pl.multiple_of(i * size, size), size)
        o = o_ref[at, :]
        shift = field_ref[4, at, :] - energy
        out = []
        for p in range(trials):
            source = (alpha[p] - field_ref[p, at, :]) * o
            image = kinetic[at, p * 128 : p * 128 + 128] + shift * source
            residual = source - step[p] * image
            there = pl.ds(p, size, stride=trials)
            mixed_s[there, :] = step[p] * source
            mixed_r[there, :] = residual
            out.append(sums[p] + fold(residual * residual))
        for flat, ref in ((flat_s, mixed_s), (flat_r, mixed_r)):
            for q in range(2):
                for n, tile in enumerate(tiles(ref, q)):
                    flat[i, :, :, 384 * q + 128 * n : 384 * q + 128 * n + 128] = tile.reshape(planes, trials, 128)
        cells = pl.ds(pl.multiple_of(i * 768, 768), 768)
        begin(flat_s.at[i], response_ref.at[:, :, cells], out_sems.at[0, i])
        begin(flat_r.at[i], residual_ref.at[:, :, cells], out_sems.at[1, i])
        return tuple(out)

    sums = lax.fori_loop(0, rows // size, back, tuple(jnp.zeros((8, 128), f32) for _ in range(trials)))
    norm_ref[...] = tile_of((8, 128), [(0, p, total(s)) for p, s in enumerate(sums)])
    for i in range(rows // size):
        cells = pl.ds(i * 768, 768)
        pltpu.make_async_copy(flat_s.at[i], response_ref.at[:, :, cells], out_sems.at[0, i]).wait()
        pltpu.make_async_copy(flat_r.at[i], residual_ref.at[:, :, cells], out_sems.at[1, i]).wait()


def last_kernel(step_ref, n0, n1, n2, n3, packed_far, band_ref, response_ref, residual_ref,
                direction_ref, density_ref, packed_ref, bands_in, first, second, result, sems, out_sems):
    parts = 6
    width = points * points // parts
    arrival = begin(band_ref, bands_in, sems.at[2, 0])
    kept = begin(packed_far, packed_ref, sems.at[2, 1])
    loads = []
    for i in range(parts):
        cells = pl.ds(i * width, width)
        loads.append((begin(response_ref.at[:, :, cells], first.at[i], sems.at[0, i]),
                      begin(residual_ref.at[:, :, cells], second.at[i], sems.at[1, i])))
    new = n0[0:1, :]
    for part in (n1, n2, n3):
        new = new + part[0:1, :]
    ratio = [new[:, p : p + 1] / step_ref[0:1, 4 + p : 5 + p] / step_ref[0:1, 8 + p : 9 + p] for p in range(trials)]
    r = row_of((trials, 128))
    ratios = jnp.zeros((trials, 128), f32)
    for p in range(trials):
        ratios = jnp.where(r == p, ratio[p], ratios)
    ratios = ratios[:, 0:1][None]
    stores = []
    for i in range(parts):
        for copy in loads[i]:
            copy.wait()
        result[i, :, :, :] = second[i] + ratios * first[i]
        stores.append(begin(result.at[i], direction_ref.at[:, :, pl.ds(i * width, width)], out_sems.at[i]))
    arrival.wait()
    kept.wait()
    blocks = [packed_ref[q * 36 : q * 36 + 36, :] for q in range(3)]
    fields = [tighten(field) for field in (*blocks, unpack_last(*blocks))]
    sums = [jnp.zeros((27, 128), f32) for _ in range(trials)]
    for v in range(bands):
        square = bands_in[v, 0:27, :]
        square = square * square
        for p in range(trials):
            alpha, step = bands_in[v, 28:29, p : p + 1], bands_in[v, 28:29, 8 + p : 9 + p]
            sums[p] = sums[p] + (step * (alpha - fields[p])) * square
    lane = lane_of((planes, 128))
    for p in range(trials):
        loose = loosen(sums[p]) * (4.0 / bands)
        c = [loose[12 * i : 12 * i + 12] for i in range(3)]
        r1, r2 = pltpu.roll(c[1], 96, 1), pltpu.roll(c[2], 64, 1)
        density_ref[:, p, 0:128] = jnp.where(lane < 96, c[0], r1)
        density_ref[:, p, 128:256] = jnp.where(lane < 64, r1, r2)
        density_ref[:, p, 256:288] = r2[:, 0:32]
    for copy in stores:
        copy.wait()


vmem = pl.BlockSpec(memory_space=pltpu.VMEM)
smem = pl.BlockSpec(memory_space=pltpu.SMEM)
hbm = pl.BlockSpec(memory_space=pl.ANY)
far = pl.BlockSpec(memory_space=pltpu.HBM)


BIG = 56000000
SOME = 54500000


def shape(*dims, dtype=f32):
    return jax.ShapeDtypeStruct(dims, dtype)


def call(kernel, ins, outs, scratch=(), name=None, room=4 * 2**20, places=None, aliases=None, flops=10**6):
    return pl.pallas_call(
        kernel, out_shape=outs, in_specs=ins,
        out_specs=places if places is not None else jax.tree.map(lambda _: vmem, outs),
        scratch_shapes=scratch, compiler_params=pltpu.CompilerParams(vmem_limit_bytes=room), name=name, input_output_aliases=aliases or {},
        cost_estimate=pl.CostEstimate(flops=flops, bytes_accessed=10**6, transcendentals=0),
    )


def pack(trial, local):
    return call(
        pack_kernel, [far] * 2, shape(144, 128),
        [buffer(planes, trials, 288), buffer(planes, 288), pltpu.SemaphoreType.DMA((2,))], name="pack", room=66000000,
    )(jnp.transpose(trial, (1, 0, 2)), local)


def orbital_rows(orbitals, packed):
    return call(
        orbital_kernel, [vmem, vmem],
        (shape(rows, 128), shape(bands, 32, 128), shape(144, 128)),
        [buffer(rows, 128), buffer(bands, 32, 128), pltpu.SemaphoreType.DMA((3,))],
        name="orbital_rows", places=(far, far, far), room=BIG,
    )(orbitals, packed)


def buffer(*dims, dtype=f32):
    return pltpu.VMEM(dims, dtype)


def forward(pieces, o, tables):
    return call(
        forward_kernel, [hbm] * 8 + [far] * 3,
        (shape(5, rows, 128), shape(rows, 128), shape(8, 128)),
        [buffer(rows, 128), buffer(5, rows, 128), buffer(bands, 144, 128), buffer(2, 640, 256, dtype=bf16), buffer(2, 96, 192, dtype=bf16), buffer(rows, 128),
         buffer(rows, 640, dtype=bf16), buffer(rows, 640, dtype=bf16), buffer(rows, 128), buffer(rows, 128),
         pltpu.SemaphoreType.DMA((11,))],
        name="forward", room=SOME, places=(far, far, vmem),
    )(*pieces, o, tables["w1"], tables["g1"])


def local_sums(energies, fields, o, stat, tables):
    size, count = 192, rows // 192
    tile = pl.BlockSpec((8, 128), lambda i: (0, 0))
    kinds = [tables[name] for name in ("g2", "g3", "g4", "w2")]
    return pl.pallas_call(
        local_kernel, grid=(count,),
        in_specs=[smem, pl.BlockSpec((5, size, 128), lambda i: (0, i, 0)), pl.BlockSpec((size, 128), lambda i: (i, 0)),
                  tile] + [far] * 4,
        out_specs=(tile, *[vmem] * 4),
        out_shape=(shape(8, 128), *[shape(*t.shape, dtype=bf16) for t in kinds]),
        scratch_shapes=[buffer(9, 8, 128), pltpu.SemaphoreType.DMA((4,))],
        compiler_params=pltpu.CompilerParams(vmem_limit_bytes=BIG), name="local_sums",
        cost_estimate=pl.CostEstimate(flops=10**7, bytes_accessed=10**7, transcendentals=0),
    )(energies, fields, o, stat, *kinds)


def waves(arrived, stat, sums, g2, g3, base):
    return call(
        wave_kernel, [vmem] * 5 + [far], (shape(groups * returned, 128), shape(8, 128), shape(bands, 8, 128)),
        [pltpu.SemaphoreType.DMA((1,))], name="waves", room=8 * 2**20,
    )(arrived, stat, sums, g2, g3, base)


def steps(arrived, scal, tail, base):
    return call(
        step_kernel, [vmem] * 3 + [far], (shape(8, 128), shape(bands, 32, 128)),
        [buffer(bands, 8, 128), pltpu.SemaphoreType.DMA((1,))],
        name="steps", places=(vmem, far), aliases={3: 1},
    )(arrived, scal, tail, base)


def image(energies, arrived, step, fields, o, g4, w2):
    cells = shape(planes, trials, points * points)
    return call(
        image_kernel, [smem, vmem, vmem, far, far, vmem, vmem], (cells, cells, shape(8, 128)),
        [buffer(5, rows, 128), buffer(rows, 128), buffer(rows, 128), buffer(rows, 128), buffer(rows, 512),
         buffer(384, 128), buffer(384, 128),
         buffer(12, planes, trials, 768), buffer(12, planes, trials, 768),
         pltpu.SemaphoreType.DMA((2,)), pltpu.SemaphoreType.DMA((2, 12))],
        name="image", room=BIG, places=(far, far, vmem), flops=2 * 10**10,
    )(energies, arrived, step, fields, o, g4, w2)


def last(step, norms, packed, band, response, residual):
    cells = shape(planes, trials, points * points)
    part = buffer(6, planes, trials, points * points // 6)
    return call(
        last_kernel, [vmem] * 5 + [far, hbm, far, far], (cells, shape(planes, trials, 288)),
        [buffer(144, 128), buffer(bands, 32, 128), part, part, part, pltpu.SemaphoreType.DMA((3, 6)), pltpu.SemaphoreType.DMA((6,))],
        name="last", room=SOME, places=(far, vmem),
    )(step, *norms, packed, band, response, residual)


def outward(value):
    return jnp.transpose(value, (1, 0, 2))


def swapped(value, axis, size, mask):
    return lax.ppermute(value, axis, [(s, s ^ mask) for s in range(size)])


def crossed(value, even, odd):
    return lax.ppermute(value, "band", [(s, s ^ (odd if s & 1 else even)) for s in range(bands)])


first_masks = ((8, 8), (16, 2), (24, 10))
second_masks = ((2, 24), (4, 6), (6, 30))


def gather_first(packed):
    value = packed[None]
    return jnp.concatenate([value] + [crossed(value, *masks) for masks in first_masks], axis=0)


def gather_second(quad):
    quads = [quad] + [crossed(quad, *masks) for masks in second_masks]
    return quads + [swapped(q, "band", bands, 1) for q in quads]


def on_device(orbitals, energies, local_pot, trial_pot):
    tables = {name: jnp.asarray(table) for name, table in build_tables().items()}
    packed = pack(trial_pot, local_pot)
    quad = gather_first(packed)
    o_far, base, packed_far = orbital_rows(orbitals, packed)
    quad, o_far = lax.optimization_barrier((quad, o_far))
    pieces = gather_second(quad)
    fields, sent, stat = forward(pieces, o_far, tables)
    arrived = lax.all_to_all(sent.reshape(groups, chunk, 128), "grid", 0, 0, tiled=True).reshape(rows, 128)
    sums, g2, g3, g4, w2 = local_sums(energies, fields, o_far, stat, tables)
    back, scal, tail = waves(arrived, stat, sums, g2, g3, base)
    back = lax.all_to_all(back.reshape(groups, returned, 128), "grid", 0, 0, tiled=True).reshape(groups * returned, 128)
    step, payload = steps(back, scal, tail, base)
    band = lax.all_to_all(payload, "band", 0, 0, tiled=True)
    response, residual, norm = image(energies, back, step, fields, o_far, g4, w2)
    norm = norm + swapped(norm, "grid", groups, 1)
    norms = [norm] + [swapped(norm, "grid", groups, m) for m in (2, 4, 6)]
    direction, density = last(step, norms, packed_far, band, response, residual)
    return outward(response)[None], outward(residual)[None], outward(direction)[None], outward(density)


def solution(mesh):
    return jax.shard_map(
        on_device,
        mesh=mesh,
        in_specs=(P("band", "grid", None), P("band"), P("grid", "band"), P(None, "grid", "band")),
        out_specs=(
            P("band", None, "grid", None),
            P("band", None, "grid", None),
            P("band", None, "grid", None),
            P(None, "grid", "band"),
        ),
        check_vma=False,
    )
```

```python
import math

import jax
import jax.numpy as jnp
import ml_dtypes
import numpy as np
from jax import lax
from jax.experimental import pallas as pl
from jax.experimental.pallas import tpu as pltpu
from jax.sharding import PartitionSpec as P

points = 96
planes = 12
trials = 4
bands = 32
half = 24
groups = 8
rows = points * planes
chunk = rows // groups
returned = 112
spacing = 0.49
prefactor = 0.5 * (2.0 * math.pi / (points * spacing)) ** 2
f32 = jnp.float32
bf16 = jnp.bfloat16


def split_np(table):
    table = np.asarray(table, np.float32)
    high = table.astype(ml_dtypes.bfloat16)
    low = (table - high.astype(np.float32)).astype(ml_dtypes.bfloat16)
    return np.stack([high, low])


def angle(a, b):
    return (np.outer(a, b) % points) * (2.0 * np.pi / points)


def build_tables():
    grid = np.arange(points)
    signed = np.arange(2 * half) - half
    kz = np.arange(half)
    w1 = np.zeros((5 * 128, 256))
    az = angle(grid, kz)
    for p in range(5):
        w1[p * 128 : p * 128 + points, p * half : (p + 1) * half] = np.cos(az)
        w1[p * 128 : p * 128 + points, 128 + p * half : 128 + (p + 1) * half] = -np.sin(az)
    order = np.zeros(points, np.int64)
    part = np.zeros(points, np.int64)
    for jj in range(6):
        for c in range(2):
            for g in range(groups):
                order[(2 * jj + c) * 8 + g] = signed[6 * g + jj]
                part[(2 * jj + c) * 8 + g] = c
    ay = angle(order, grid)
    real = part[:, None] == 0
    g1 = np.concatenate(
        [np.where(real, np.cos(ay), -np.sin(ay)), np.where(real, np.sin(ay), np.cos(ay))], 1
    )
    g4 = np.concatenate(
        [np.where(real, np.cos(ay), -np.sin(ay)), np.where(real, np.sin(ay), np.cos(ay))], 1
    ).T
    ax = angle(signed, grid)
    cx, sx = np.cos(ax), np.sin(ax)
    g2 = np.block([[cx, sx], [-sx, cx]])
    g3 = np.block([[cx.T, -sx.T], [sx.T, cx.T]])
    w2 = np.zeros((256, 4 * 128))
    for p in range(4):
        w2[p * half : (p + 1) * half, p * 128 : p * 128 + points] = np.cos(az).T
        w2[128 + p * half : 128 + (p + 1) * half, p * 128 : p * 128 + points] = -np.sin(az).T
    return {"w1": split_np(w1), "g1": split_np(g1), "g2": split_np(g2), "g3": split_np(g3),
            "g4": split_np(g4), "w2": split_np(w2)}


def dot(a, b):
    return lax.dot_general(a, b, (((1,), (0,)), ((), ())), preferred_element_type=f32)


def split(value):
    high = value.astype(bf16)
    return high, (value - high.astype(f32)).astype(bf16)


def left_table(table, value):
    count = table.shape[1]
    vh, vl = split(value)
    both = dot(jnp.concatenate([table[0], table[1]], axis=0), vh)
    return both[:count] + both[count:] + dot(table[0], vl)


def right_table(vh, vl, table):
    count = vh.shape[0]
    both = dot(jnp.concatenate([vh, vl], axis=0), table[0])
    return both[:count] + both[count:] + dot(vh, table[1])


def begin(source, target, sem):
    copy = pltpu.make_async_copy(source, target, sem)
    copy.start()
    return copy


def lane_of(shape):
    return lax.broadcasted_iota(jnp.int32, shape, 1)


def row_of(shape):
    return lax.broadcasted_iota(jnp.int32, shape, 0)


def total(value):
    return jnp.sum(jnp.sum(value, axis=0, keepdims=True), axis=1, keepdims=True)


def fold(value):
    return jnp.sum(value.reshape(value.shape[0] // 8, 8, 128), axis=0)


def tile_of(shape, entries):
    row, lane = row_of(shape), lane_of(shape)
    out = jnp.zeros(shape, f32)
    for r, l, value in entries:
        out = jnp.where((row == r) & (lane == l), value, out)
    return out


def spread(t0, t1, t2):
    lane = lane_of(t0.shape)
    c1 = pltpu.roll(jnp.where(lane >= 96, t0, t1), 32, 1)
    c2 = pltpu.roll(jnp.where(lane >= 64, t1, t2), 64, 1)
    return t0, c1, c2


def pack_kernel(trial_far, local_far, out_ref, trial_ref, local_ref, sems):
    for copy in [begin(trial_far, trial_ref, sems.at[0]), begin(local_far, local_ref, sems.at[1])]:
        copy.wait()
    lane = lane_of((planes, 128))
    fill = jnp.zeros((planes, 96), f32)

    def pieces(ref, *at):
        t2 = jnp.concatenate([ref[(slice(None), *at, slice(256, 288))], fill], axis=1)
        return spread(ref[(slice(None), *at, slice(0, 128))], ref[(slice(None), *at, slice(128, 256))], t2)

    last = pieces(trial_ref, 3)
    for q in range(3):
        mine = pieces(trial_ref, q)
        for i in range(3):
            tail = pltpu.roll(last[i], 96 - 32 * q, 1)
            out_ref[q * 36 + i * 12 : q * 36 + i * 12 + 12, :] = jnp.where(lane < 96, mine[i], tail)
    mine = pieces(local_ref)
    for i in range(3):
        out_ref[108 + i * 12 : 120 + i * 12, :] = jnp.where(lane < 96, mine[i], 0.0)


def unpack_last(b0, b1, b2):
    lane = lane_of(b0.shape)
    r0, r1, r2 = pltpu.roll(b0, 32, 1), pltpu.roll(b1, 64, 1), pltpu.roll(b2, 96, 1)
    return jnp.where(lane < 32, r0, jnp.where(lane < 64, r1, r2))


def tighten(value):
    lane, tail = lane_of((9, 128)), value[27:36]
    return jnp.concatenate(
        [jnp.where(lane < 96, value[9 * t : 9 * t + 9], pltpu.roll(tail, 96 - 32 * t, 1)) for t in range(3)], axis=0
    )


def loosen(value):
    lane = lane_of((9, 128))
    r0, r1, r2 = (pltpu.roll(value[9 * t : 9 * t + 9], 32 + 32 * t, 1) for t in range(3))
    return jnp.concatenate([value, jnp.where(lane < 32, r0, jnp.where(lane < 64, r1, r2))], axis=0)


def orbital_kernel(o_ref, packed_ref, far_out, base_out, packed_out, out_ref, base_ref, sems):
    kept = begin(packed_ref, packed_out, sems.at[0])
    lane = lane_of((planes, 128))
    for q in range(points // 4):
        t = [o_ref[0, :, 384 * q + 128 * i : 384 * q + 128 * i + 128] for i in range(3)]
        c = [*spread(*t), pltpu.roll(t[2], 96, 1)]
        for i in range(4):
            at = (4 * q + i) * planes
            out_ref[at : at + planes, :] = jnp.where(lane < 96, c[i], 0.0)
    for u in range(bands):
        mine = out_ref[u * 36 : u * 36 + 36, :]
        base_ref[u, 0:27, :] = tighten(mine)
        base_ref[u, 27:32, :] = jnp.zeros((5, 128), f32)
    copies = [begin(out_ref, far_out, sems.at[2]), begin(base_ref, base_out, sems.at[1]), kept]
    for copy in copies:
        copy.wait()


def forward_kernel(p0, p1, p2, p3, p4, p5, p6, p7, o_far, w1_ref, g1_ref,
                   field_out, result_ref, stat_ref,
                   o_ref, field_ref, t_ref, w1, g1, out_ref, high, low, real, imag, sems):
    me = lax.axis_index("band")
    arrivals = [
        begin(piece, t_ref.at[pl.ds(4 * n, 4)], sems.at[n]) for n, piece in enumerate((p0, p1, p2, p3, p4, p5, p6, p7))
    ]
    arrivals.append(begin(o_far, o_ref, sems.at[10]))
    tables = [begin(w1_ref, w1, sems.at[8]), begin(g1_ref, g1, sems.at[9])]
    for copy in arrivals:
        copy.wait()
    norm = jnp.zeros((36, 128), f32)
    corr = [jnp.zeros((36, 128), f32) for _ in range(trials)]
    for u in range(bands):
        d = u ^ me
        z, y = d >> 3, (d >> 1) & 3
        if u & 1:
            z, y = (z >> 1) | ((y >> 1) << 1), ((z ^ (z >> 1)) & 1) | (((y ^ (y >> 1)) & 1) << 1)
            along, across = z, y
        else:
            along, across = y, z
        slot = ((d & 1) << 4) | (along << 2) | across
        blocks = [t_ref[slot, q * 36 : q * 36 + 36, :] for q in range(4)]
        fields = [*blocks[:3], unpack_last(*blocks[:3]), blocks[3]]
        here = slice(u * 36, u * 36 + 36)
        for p in range(5):
            field_ref[p, here, :] = fields[p]
        o = o_ref[here, :]
        square = o * o
        norm = norm + square
        for p in range(trials):
            corr[p] = corr[p] + fields[p] * square
    kept = begin(field_ref, field_out, sems.at[1])
    norm = total(norm)
    mean = [total(c) / norm for c in corr]

    size = 96

    def weigh(i, sums):
        at = pl.ds(pl.multiple_of(i * size, size), size)
        o = o_ref[at, :]
        out = []
        for p in range(trials):
            w = (field_ref[p, at, :] - mean[p]) * o
            high[at, p * 128 : p * 128 + 128], low[at, p * 128 : p * 128 + 128] = split(w)
            out.append(sums[p] + fold(w * w))
        high[at, 512:640], low[at, 512:640] = split(o)
        return tuple(out)

    second = lax.fori_loop(0, rows // size, weigh, tuple(jnp.zeros((8, 128), f32) for _ in range(trials)))
    second = [total(s) for s in second]
    stat_ref[...] = tile_of((8, 128), [(0, 0, norm)] + [(0, 1 + p, mean[p]) for p in range(trials)])

    for copy in tables:
        copy.wait()
    big = 384

    def along_z(i, _):
        at = pl.ds(pl.multiple_of(i * big, big), big)
        a = right_table(high[at, :], low[at, :], w1)
        real[at, :] = a[:, :128]
        imag[at, :] = a[:, 128:]
        return 0

    lax.fori_loop(0, rows // big, along_z, 0)

    row, lane = row_of((points, 128)), lane_of((points, 128))
    ride = jnp.where((row < 8) & (lane == 120), norm, 0.0)
    for p in range(trials):
        ride = jnp.where((row < 8) & (lane == 121 + p), mean[p], ride)
        ride = jnp.where((row >= 8) & (row < 16) & (lane == 120 + p), second[p], ride)
    for x in range(0, planes, 2):
        parts = [
            jnp.concatenate([ref[pl.ds(x + i, points, stride=planes), :] for i in range(2)], axis=1)
            for ref in (real, imag)
        ]
        y = left_table(g1, jnp.concatenate(parts, axis=0))
        for i in range(2):
            mine = y[:, i * 128 : i * 128 + 128] + ride
            for r in range(12):
                out_ref[pl.ds((x + i) * 12 + r, groups, stride=chunk), :] = mine[8 * r : 8 * r + 8]
    begin(out_ref, result_ref, sems.at[0]).wait()
    kept.wait()


def local_kernel(energy_ref, field_ref, o_ref, stat_ref, g2_ref, g3_ref, g4_ref, w2_ref, base_ref,
                 out_ref, g2, g3, g4, w2, tail_ref, sums, sems):
    step = pl.program_id(0)
    pairs = ((g2_ref, g2), (g3_ref, g3), (g4_ref, g4), (w2_ref, w2), (base_ref.at[:, pl.ds(24, 8), :], tail_ref))

    @pl.when(step == 0)
    def _():
        sums[...] = jnp.zeros(sums.shape, f32)
        for n, (source, target) in enumerate(pairs):
            pltpu.make_async_copy(source, target, sems.at[n]).start()

    o = o_ref[...]
    shift = (field_ref[4] - energy_ref[0]) * o
    sums[0] += fold(shift * o)
    for p in range(trials):
        off = field_ref[p] - stat_ref[0:1, 1 + p : 2 + p]
        both = shift * off
        sums[1 + p] += fold(both * o)
        sums[5 + p] += fold(both * (off * o))

    @pl.when(step == pl.num_programs(0) - 1)
    def _():
        out_ref[...] = tile_of((8, 128), [(0, n, total(sums[n])) for n in range(9)])
        for n, (source, target) in enumerate(pairs):
            pltpu.make_async_copy(source, target, sems.at[n]).wait()


def wave_kernel(in_ref, stat_ref, sums_ref, g2, g3, out_ref, scal_ref):
    owner = lax.axis_index("grid")
    s0 = in_ref[pl.ds(0, points, stride=planes), :]
    s1 = in_ref[pl.ds(1, points, stride=planes), :]
    weight = s0[:, 120:121]
    whole = jnp.sum(weight, axis=0, keepdims=True)
    lane = lane_of((points, 128))
    coef = jnp.zeros((points, 128), f32)
    alpha, start = [], []
    for p in range(trials):
        mean = s0[:, 121 + p : 122 + p]
        a = jnp.sum(weight * mean, axis=0, keepdims=True) / whole
        off = a - mean
        spread_sum = jnp.sum(s1[:, 120 + p : 121 + p] + weight * off * off, axis=0, keepdims=True)
        alpha.append(a)
        start.append(spread_sum / planes)
        coef = jnp.where((lane >= p * half) & (lane < (p + 1) * half), off, coef)

    def source_of(r):
        d = in_ref[pl.ds(r, points, stride=planes), :]
        o = jnp.where((lane >= 96) & (lane < 120), d, 0.0)
        o = pltpu.roll(o, 32, 1)
        o = o + pltpu.roll(o, 24, 1)
        o = o + pltpu.roll(o, 48, 1)
        return jnp.where(lane < 96, coef * o - d, 0.0)

    wide = (2 * half, 128)
    m = row_of(wide) - half
    k = lane_of(wide)
    k = k - jnp.where(k >= 72, 72, jnp.where(k >= 48, 48, jnp.where(k >= 24, 24, 0)))
    doubled = jnp.where(k == 0, 1.0, 2.0) * (prefactor / float(points**3))
    energy = jnp.zeros((1, 128), f32)
    own = [jnp.where(lane_of((1, 128)) == 0, 0.0, 0.0)]
    tails, directs = [], []
    for pair in (2, 1, 0):
        parts = [
            jnp.concatenate([source_of(2 * (2 * pair + i) + c) for i in range(2)], axis=1)
            for c in range(2)
        ]
        u = left_table(g2, jnp.concatenate(parts, axis=0))
        weights = []
        for i in range(2):
            j = owner * 6 + (2 * pair + i) - half
            square = m * m + k * k + j * j
            weights.append(jnp.where(square < half * half, doubled * square.astype(f32), 0.0))
        w = jnp.concatenate(weights, axis=1)
        t = u * jnp.concatenate([w, w], axis=0)
        product = jnp.sum(u * t, axis=0, keepdims=True)
        energy = energy + product[:, :128] + product[:, 128:]
        e = left_table(g3, t)
        for i in range(2):
            for c in range(2):
                r = 2 * (2 * pair + i) + c
                value = e[c * points : (c + 1) * points, i * 128 : i * 128 + 128]
                if r >= 9:
                    tails.append((r - 9, value))
                else:
                    directs.append((r, value))
        if pair == 2:
            tails = [value for _, value in sorted(tails, key=lambda entry: entry[0])]
        for r, value in directs:
            spare = pltpu.roll(tails[r // 3], 96 - 32 * (r % 3), 1)
            value = jnp.where(lane < 96, value, spare)
            for g in range(groups):
                out_ref[pl.ds(g * returned + r, planes, stride=9), :] = value[planes * g : planes * g + planes]
        directs = []
    l1 = lane_of((1, 128))
    ride = jnp.zeros((1, 128), f32)
    entries = []
    for p in range(trials):
        kinetic = jnp.sum(jnp.where((l1 >= p * half) & (l1 < (p + 1) * half), energy, 0.0), axis=1, keepdims=True)
        off = alpha[p] - stat_ref[0:1, 1 + p : 2 + p]
        at_p = sums_ref[0:1, 5 + p : 6 + p] - 2.0 * off * sums_ref[0:1, 1 + p : 2 + p] + off * off * sums_ref[0:1, 0:1]
        ride = jnp.where(l1 == 96 + p, kinetic + at_p, ride)
        entries += [(0, p, alpha[p]), (0, 4 + p, start[p])]
    scal_ref[...] = tile_of((8, 128), entries)
    for g in range(groups):
        out_ref[g * returned + 108 : g * returned + 112, :] = jnp.broadcast_to(ride, (4, 128))


def step_kernel(in_ref, scal_ref, tail_ref, base_ref, step_ref, out_ref, tail, sems):
    shares = jnp.sum(in_ref[pl.ds(108, groups, stride=returned), :], axis=0, keepdims=True)
    lane = lane_of((1, 128))
    start = jnp.where((lane >= 4) & (lane < 8), scal_ref[0:1, :], 0.0)
    curvature = pltpu.roll(jnp.where((lane >= 96) & (lane < 100), shares, 0.0), 36, 1)
    step = start / jnp.where((lane >= 4) & (lane < 8), curvature, 1.0)
    row = jnp.where(lane < 8, scal_ref[0:1, :], 0.0) + pltpu.roll(step, 4, 1)
    step_ref[...] = jnp.broadcast_to(row, (8, 128))
    last = jnp.where(row_of((8, 128)) == 4, row, 0.0)
    for v in range(bands):
        tail[v, :, :] = tail_ref[v, :, :] + last
    begin(tail, out_ref.at[:, pl.ds(24, 8), :], sems.at[0]).wait()


def image_kernel(energy_ref, in_ref, step_ref, field_far, o_far, g4, w2,
                 response_ref, residual_ref, norm_ref,
                 field_ref, o_ref, real, imag, kinetic, mixed_s, mixed_r, flat_s, flat_r, sems, out_sems):
    energy = energy_ref[0]
    third = rows // 3
    copies = []
    for n in range(3):
        at = pl.ds(n * third, third)
        copies.append((begin(field_far.at[:, at, :], field_ref.at[:, at, :], sems.at[n]),
                       begin(o_far.at[at], o_ref.at[at], sems.at[3 + n])))
    alpha = [step_ref[0:1, p : p + 1] for p in range(trials)]
    step = [step_ref[0:1, 8 + p : 9 + p] for p in range(trials)]
    narrow = lane_of((groups, 128))

    def waves_of(x):
        r = [in_ref[pl.ds(x * 9 + n, groups, stride=returned), :] for n in range(9)]
        for n in range(3):
            r0, r1, r2 = (pltpu.roll(r[3 * n + t], 32 + 32 * t, 1) for t in range(3))
            r.append(jnp.where(narrow < 32, r0, jnp.where(narrow < 64, r1, r2)))
        return jnp.concatenate(r, axis=0)

    for x in range(0, planes, 2):
        b = jnp.concatenate([waves_of(x), waves_of(x + 1)], axis=1)
        v = left_table(g4, b)
        for i in range(2):
            real[pl.ds(x + i, points, stride=planes), :] = v[:points, i * 128 : i * 128 + 128]
            imag[pl.ds(x + i, points, stride=planes), :] = v[points:, i * 128 : i * 128 + 128]
    size = 96
    mixed = planes * trials
    lane = lane_of((mixed, 128))

    def tiles(ref, q):
        c = [ref[(4 * q + i) * mixed : (4 * q + i + 1) * mixed, :] for i in range(4)]
        r1, r2, r3 = pltpu.roll(c[1], 96, 1), pltpu.roll(c[2], 64, 1), pltpu.roll(c[3], 32, 1)
        return jnp.where(lane < 96, c[0], r1), jnp.where(lane < 64, r1, r2), jnp.where(lane < 32, r2, r3)

    big = 384

    def along_z(i, _):
        at = pl.ds(pl.multiple_of(i * big, big), big)
        vh, vl = split(jnp.concatenate([real[at, :], imag[at, :]], axis=1))
        kinetic[at, :] = right_table(vh, vl, w2)
        return 0

    lax.fori_loop(0, rows // big, along_z, 0)

    def back(i, sums):
        at = pl.ds(pl.multiple_of(i * size, size), size)
        o = o_ref[at, :]
        shift = field_ref[4, at, :] - energy
        out = []
        for p in range(trials):
            source = (alpha[p] - field_ref[p, at, :]) * o
            image = kinetic[at, p * 128 : p * 128 + 128] + shift * source
            residual = source - step[p] * image
            there = pl.ds(p, size, stride=trials)
            mixed_s[there, :] = step[p] * source
            mixed_r[there, :] = residual
            out.append(sums[p] + fold(residual * residual))
        for flat, ref in ((flat_s, mixed_s), (flat_r, mixed_r)):
            for q in range(2):
                for n, tile in enumerate(tiles(ref, q)):
                    flat[i, :, :, 384 * q + 128 * n : 384 * q + 128 * n + 128] = tile.reshape(planes, trials, 128)
        cells = pl.ds(pl.multiple_of(i * 768, 768), 768)
        begin(flat_s.at[i], response_ref.at[:, :, cells], out_sems.at[0, i])
        begin(flat_r.at[i], residual_ref.at[:, :, cells], out_sems.at[1, i])
        return tuple(out)

    sums = tuple(jnp.zeros((8, 128), f32) for _ in range(trials))
    for n in range(3):
        for copy in copies[n]:
            copy.wait()
        sums = lax.fori_loop(n * (third // size), (n + 1) * (third // size), back, sums)
    norm_ref[...] = tile_of((8, 128), [(0, p, total(s)) for p, s in enumerate(sums)])
    for i in range(rows // size):
        cells = pl.ds(i * 768, 768)
        pltpu.make_async_copy(flat_s.at[i], response_ref.at[:, :, cells], out_sems.at[0, i]).wait()
        pltpu.make_async_copy(flat_r.at[i], residual_ref.at[:, :, cells], out_sems.at[1, i]).wait()


def last_kernel(step_ref, n0, n1, n2, n3, packed_far, band_ref, response_ref, residual_ref,
                direction_ref, density_ref, packed_ref, bands_in, first, second, result, sems, out_sems):
    parts = 6
    width = points * points // parts
    arrival = begin(band_ref, bands_in, sems.at[2, 0])
    kept = begin(packed_far, packed_ref, sems.at[2, 1])
    loads = []
    for i in range(parts):
        cells = pl.ds(i * width, width)
        loads.append((begin(response_ref.at[:, :, cells], first.at[i], sems.at[0, i]),
                      begin(residual_ref.at[:, :, cells], second.at[i], sems.at[1, i])))
    new = n0[0:1, :]
    for part in (n1, n2, n3):
        new = new + part[0:1, :]
    ratio = [new[:, p : p + 1] / step_ref[0:1, 4 + p : 5 + p] / step_ref[0:1, 8 + p : 9 + p] for p in range(trials)]
    r = row_of((trials, 128))
    ratios = jnp.zeros((trials, 128), f32)
    for p in range(trials):
        ratios = jnp.where(r == p, ratio[p], ratios)
    ratios = ratios[:, 0:1][None]
    stores = []
    for i in range(parts):
        for copy in loads[i]:
            copy.wait()
        result[i, :, :, :] = second[i] + ratios * first[i]
        stores.append(begin(result.at[i], direction_ref.at[:, :, pl.ds(i * width, width)], out_sems.at[i]))
    arrival.wait()
    kept.wait()
    blocks = [packed_ref[q * 36 : q * 36 + 36, :] for q in range(3)]
    fields = [tighten(field) for field in (*blocks, unpack_last(*blocks))]
    sums = [jnp.zeros((27, 128), f32) for _ in range(trials)]
    for v in range(bands):
        square = bands_in[v, 0:27, :]
        square = square * square
        for p in range(trials):
            alpha, step = bands_in[v, 28:29, p : p + 1], bands_in[v, 28:29, 8 + p : 9 + p]
            sums[p] = sums[p] + (step * (alpha - fields[p])) * square
    lane = lane_of((planes, 128))
    for p in range(trials):
        loose = loosen(sums[p]) * (4.0 / bands)
        c = [loose[12 * i : 12 * i + 12] for i in range(3)]
        r1, r2 = pltpu.roll(c[1], 96, 1), pltpu.roll(c[2], 64, 1)
        density_ref[:, p, 0:128] = jnp.where(lane < 96, c[0], r1)
        density_ref[:, p, 128:256] = jnp.where(lane < 64, r1, r2)
        density_ref[:, p, 256:288] = r2[:, 0:32]
    for copy in stores:
        copy.wait()


vmem = pl.BlockSpec(memory_space=pltpu.VMEM)
smem = pl.BlockSpec(memory_space=pltpu.SMEM)
hbm = pl.BlockSpec(memory_space=pl.ANY)
far = pl.BlockSpec(memory_space=pltpu.HBM)


BIG = 56000000
SOME = 54500000


def shape(*dims, dtype=f32):
    return jax.ShapeDtypeStruct(dims, dtype)


def call(kernel, ins, outs, scratch=(), name=None, room=4 * 2**20, places=None, aliases=None, flops=10**6):
    return pl.pallas_call(
        kernel, out_shape=outs, in_specs=ins,
        out_specs=places if places is not None else jax.tree.map(lambda _: vmem, outs),
        scratch_shapes=scratch, compiler_params=pltpu.CompilerParams(vmem_limit_bytes=room), name=name, input_output_aliases=aliases or {},
        cost_estimate=pl.CostEstimate(flops=flops, bytes_accessed=10**6, transcendentals=0),
    )


def pack(trial, local):
    return call(
        pack_kernel, [far] * 2, shape(144, 128),
        [buffer(planes, trials, 288), buffer(planes, 288), pltpu.SemaphoreType.DMA((2,))], name="pack", room=66000000,
    )(jnp.transpose(trial, (1, 0, 2)), local)


def orbital_rows(orbitals, packed):
    return call(
        orbital_kernel, [vmem, vmem],
        (shape(rows, 128), shape(bands, 32, 128), shape(144, 128)),
        [buffer(rows, 128), buffer(bands, 32, 128), pltpu.SemaphoreType.DMA((3,))],
        name="orbital_rows", places=(far, far, far), room=BIG,
    )(orbitals, packed)


def buffer(*dims, dtype=f32):
    return pltpu.VMEM(dims, dtype)


def forward(pieces, o, tables):
    return call(
        forward_kernel, [hbm] * 8 + [far] * 3,
        (shape(5, rows, 128), shape(rows, 128), shape(8, 128)),
        [buffer(rows, 128), buffer(5, rows, 128), buffer(bands, 144, 128), buffer(2, 640, 256, dtype=bf16), buffer(2, 96, 192, dtype=bf16), buffer(rows, 128),
         buffer(rows, 640, dtype=bf16), buffer(rows, 640, dtype=bf16), buffer(rows, 128), buffer(rows, 128),
         pltpu.SemaphoreType.DMA((11,))],
        name="forward", room=SOME, places=(far, far, vmem),
    )(*pieces, o, tables["w1"], tables["g1"])


def local_sums(energies, fields, o, stat, tables, base):
    size, count = 192, rows // 192
    tile = pl.BlockSpec((8, 128), lambda i: (0, 0))
    kinds = [tables[name] for name in ("g2", "g3", "g4", "w2")]
    return pl.pallas_call(
        local_kernel, grid=(count,),
        in_specs=[smem, pl.BlockSpec((5, size, 128), lambda i: (0, i, 0)), pl.BlockSpec((size, 128), lambda i: (i, 0)),
                  tile] + [far] * 5,
        out_specs=(tile, *[vmem] * 5),
        out_shape=(shape(8, 128), *[shape(*t.shape, dtype=bf16) for t in kinds], shape(bands, 8, 128)),
        scratch_shapes=[buffer(9, 8, 128), pltpu.SemaphoreType.DMA((5,))],
        compiler_params=pltpu.CompilerParams(vmem_limit_bytes=BIG), name="local_sums",
        cost_estimate=pl.CostEstimate(flops=10**7, bytes_accessed=10**7, transcendentals=0),
    )(energies, fields, o, stat, *kinds, base)


def waves(arrived, stat, sums, g2, g3):
    return call(
        wave_kernel, [vmem] * 5, (shape(groups * returned, 128), shape(8, 128)), name="waves", room=8 * 2**20,
    )(arrived, stat, sums, g2, g3)


def steps(arrived, scal, tail, base):
    return call(
        step_kernel, [vmem] * 3 + [far], (shape(8, 128), shape(bands, 32, 128)),
        [buffer(bands, 8, 128), pltpu.SemaphoreType.DMA((1,))],
        name="steps", places=(vmem, far), aliases={3: 1},
    )(arrived, scal, tail, base)


def image(energies, arrived, step, fields, o, g4, w2):
    cells = shape(planes, trials, points * points)
    return call(
        image_kernel, [smem, vmem, vmem, far, far, vmem, vmem], (cells, cells, shape(8, 128)),
        [buffer(5, rows, 128), buffer(rows, 128), buffer(rows, 128), buffer(rows, 128), buffer(rows, 512),
         buffer(384, 128), buffer(384, 128),
         buffer(12, planes, trials, 768), buffer(12, planes, trials, 768),
         pltpu.SemaphoreType.DMA((6,)), pltpu.SemaphoreType.DMA((2, 12))],
        name="image", room=BIG, places=(far, far, vmem), flops=2 * 10**10,
    )(energies, arrived, step, fields, o, g4, w2)


def last(step, norms, packed, band, response, residual):
    cells = shape(planes, trials, points * points)
    part = buffer(6, planes, trials, points * points // 6)
    return call(
        last_kernel, [vmem] * 5 + [far, hbm, far, far], (cells, shape(planes, trials, 288)),
        [buffer(144, 128), buffer(bands, 32, 128), part, part, part, pltpu.SemaphoreType.DMA((3, 6)), pltpu.SemaphoreType.DMA((6,))],
        name="last", room=SOME, places=(far, vmem),
    )(step, *norms, packed, band, response, residual)


def outward(value):
    return jnp.transpose(value, (1, 0, 2))


def swapped(value, axis, size, mask):
    return lax.ppermute(value, axis, [(s, s ^ mask) for s in range(size)])


def crossed(value, even, odd):
    return lax.ppermute(value, "band", [(s, s ^ (odd if s & 1 else even)) for s in range(bands)])


first_masks = ((8, 8), (16, 2), (24, 10))
second_masks = ((2, 24), (4, 6), (6, 30))


def gather_first(packed):
    value = packed[None]
    return jnp.concatenate([value] + [crossed(value, *masks) for masks in first_masks], axis=0)


def gather_second(quad):
    quads = [quad] + [crossed(quad, *masks) for masks in second_masks]
    return quads + [swapped(q, "band", bands, 1) for q in quads]


def on_device(orbitals, energies, local_pot, trial_pot):
    tables = {name: jnp.asarray(table) for name, table in build_tables().items()}
    packed = pack(trial_pot, local_pot)
    quad = gather_first(packed)
    o_far, base, packed_far = orbital_rows(orbitals, packed)
    quad, o_far = lax.optimization_barrier((quad, o_far))
    pieces = gather_second(quad)
    fields, sent, stat = forward(pieces, o_far, tables)
    arrived = lax.all_to_all(sent.reshape(groups, chunk, 128), "grid", 0, 0, tiled=True).reshape(rows, 128)
    sums, g2, g3, g4, w2, tail = local_sums(energies, fields, o_far, stat, tables, base)
    back, scal = waves(arrived, stat, sums, g2, g3)
    back = lax.all_to_all(back.reshape(groups, returned, 128), "grid", 0, 0, tiled=True).reshape(groups * returned, 128)
    step, payload = steps(back, scal, tail, base)
    band = lax.all_to_all(payload, "band", 0, 0, tiled=True)
    response, residual, norm = image(energies, back, step, fields, o_far, g4, w2)
    norm = norm + swapped(norm, "grid", groups, 1)
    norms = [norm] + [swapped(norm, "grid", groups, m) for m in (2, 4, 6)]
    direction, density = last(step, norms, packed_far, band, response, residual)
    return outward(response)[None], outward(residual)[None], outward(direction)[None], outward(density)


def solution(mesh):
    return jax.shard_map(
        on_device,
        mesh=mesh,
        in_specs=(P("band", "grid", None), P("band"), P("grid", "band"), P(None, "grid", "band")),
        out_specs=(
            P("band", None, "grid", None),
            P("band", None, "grid", None),
            P("band", None, "grid", None),
            P(None, "grid", "band"),
        ),
        check_vma=False,
    )
```

```python
import math

import jax
import jax.numpy as jnp
import ml_dtypes
import numpy as np
from jax import lax
from jax.experimental import pallas as pl
from jax.experimental.pallas import tpu as pltpu
from jax.sharding import PartitionSpec as P

points = 96
planes = 12
trials = 4
bands = 32
half = 24
groups = 8
rows = points * planes
chunk = rows // groups
returned = 112
spacing = 0.49
prefactor = 0.5 * (2.0 * math.pi / (points * spacing)) ** 2
f32 = jnp.float32
bf16 = jnp.bfloat16


def split_np(table):
    table = np.asarray(table, np.float32)
    high = table.astype(ml_dtypes.bfloat16)
    low = (table - high.astype(np.float32)).astype(ml_dtypes.bfloat16)
    return np.stack([high, low])


def angle(a, b):
    return (np.outer(a, b) % points) * (2.0 * np.pi / points)


def build_tables():
    grid = np.arange(points)
    signed = np.arange(2 * half) - half
    kz = np.arange(half)
    w1 = np.zeros((5 * 128, 256))
    az = angle(grid, kz)
    for p in range(5):
        w1[p * 128 : p * 128 + points, p * half : (p + 1) * half] = np.cos(az)
        w1[p * 128 : p * 128 + points, 128 + p * half : 128 + (p + 1) * half] = -np.sin(az)
    order = np.zeros(points, np.int64)
    part = np.zeros(points, np.int64)
    for jj in range(6):
        for c in range(2):
            for g in range(groups):
                order[(2 * jj + c) * 8 + g] = signed[6 * g + jj]
                part[(2 * jj + c) * 8 + g] = c
    ay = angle(order, grid)
    real = part[:, None] == 0
    g1 = np.concatenate(
        [np.where(real, np.cos(ay), -np.sin(ay)), np.where(real, np.sin(ay), np.cos(ay))], 1
    )
    g4 = np.concatenate(
        [np.where(real, np.cos(ay), -np.sin(ay)), np.where(real, np.sin(ay), np.cos(ay))], 1
    ).T
    ax = angle(signed, grid)
    cx, sx = np.cos(ax), np.sin(ax)
    g2 = np.block([[cx, sx], [-sx, cx]])
    g3 = np.block([[cx.T, -sx.T], [sx.T, cx.T]])
    w2 = np.zeros((256, 4 * 128))
    for p in range(4):
        w2[p * half : (p + 1) * half, p * 128 : p * 128 + points] = np.cos(az).T
        w2[128 + p * half : 128 + (p + 1) * half, p * 128 : p * 128 + points] = -np.sin(az).T
    return {"w1": split_np(w1), "g1": split_np(g1), "g2": split_np(g2), "g3": split_np(g3),
            "g4": split_np(g4), "w2": split_np(w2)}


def dot(a, b):
    return lax.dot_general(a, b, (((1,), (0,)), ((), ())), preferred_element_type=f32)


def split(value):
    high = value.astype(bf16)
    return high, (value - high.astype(f32)).astype(bf16)


def left_table(table, value):
    count = table.shape[1]
    vh, vl = split(value)
    both = dot(jnp.concatenate([table[0], table[1]], axis=0), vh)
    return both[:count] + both[count:] + dot(table[0], vl)


def right_table(vh, vl, table):
    count = vh.shape[0]
    both = dot(jnp.concatenate([vh, vl], axis=0), table[0])
    return both[:count] + both[count:] + dot(vh, table[1])


def begin(source, target, sem):
    copy = pltpu.make_async_copy(source, target, sem)
    copy.start()
    return copy


def lane_of(shape):
    return lax.broadcasted_iota(jnp.int32, shape, 1)


def row_of(shape):
    return lax.broadcasted_iota(jnp.int32, shape, 0)


def total(value):
    return jnp.sum(jnp.sum(value, axis=0, keepdims=True), axis=1, keepdims=True)


def fold(value):
    return jnp.sum(value.reshape(value.shape[0] // 8, 8, 128), axis=0)


def tile_of(shape, entries):
    row, lane = row_of(shape), lane_of(shape)
    out = jnp.zeros(shape, f32)
    for r, l, value in entries:
        out = jnp.where((row == r) & (lane == l), value, out)
    return out


def spread(t0, t1, t2):
    lane = lane_of(t0.shape)
    c1 = pltpu.roll(jnp.where(lane >= 96, t0, t1), 32, 1)
    c2 = pltpu.roll(jnp.where(lane >= 64, t1, t2), 64, 1)
    return t0, c1, c2


def pack_kernel(trial_far, local_far, out_ref, trial_ref, local_ref, sems):
    for copy in [begin(trial_far, trial_ref, sems.at[0]), begin(local_far, local_ref, sems.at[1])]:
        copy.wait()
    lane = lane_of((planes, 128))
    fill = jnp.zeros((planes, 96), f32)

    def pieces(ref, *at):
        t2 = jnp.concatenate([ref[(slice(None), *at, slice(256, 288))], fill], axis=1)
        return spread(ref[(slice(None), *at, slice(0, 128))], ref[(slice(None), *at, slice(128, 256))], t2)

    last = pieces(trial_ref, 3)
    for q in range(3):
        mine = pieces(trial_ref, q)
        for i in range(3):
            tail = pltpu.roll(last[i], 96 - 32 * q, 1)
            out_ref[q * 36 + i * 12 : q * 36 + i * 12 + 12, :] = jnp.where(lane < 96, mine[i], tail)
    mine = pieces(local_ref)
    for i in range(3):
        out_ref[108 + i * 12 : 120 + i * 12, :] = jnp.where(lane < 96, mine[i], 0.0)


def unpack_last(b0, b1, b2):
    lane = lane_of(b0.shape)
    r0, r1, r2 = pltpu.roll(b0, 32, 1), pltpu.roll(b1, 64, 1), pltpu.roll(b2, 96, 1)
    return jnp.where(lane < 32, r0, jnp.where(lane < 64, r1, r2))


def tighten(value):
    lane, tail = lane_of((9, 128)), value[27:36]
    return jnp.concatenate(
        [jnp.where(lane < 96, value[9 * t : 9 * t + 9], pltpu.roll(tail, 96 - 32 * t, 1)) for t in range(3)], axis=0
    )


def loosen(value):
    lane = lane_of((9, 128))
    r0, r1, r2 = (pltpu.roll(value[9 * t : 9 * t + 9], 32 + 32 * t, 1) for t in range(3))
    return jnp.concatenate([value, jnp.where(lane < 32, r0, jnp.where(lane < 64, r1, r2))], axis=0)


def orbital_kernel(o_ref, packed_ref, far_out, base_out, packed_out, out_ref, base_ref, sems):
    kept = begin(packed_ref, packed_out, sems.at[0])
    lane = lane_of((planes, 128))
    for q in range(points // 4):
        t = [o_ref[0, :, 384 * q + 128 * i : 384 * q + 128 * i + 128] for i in range(3)]
        c = [*spread(*t), pltpu.roll(t[2], 96, 1)]
        for i in range(4):
            at = (4 * q + i) * planes
            out_ref[at : at + planes, :] = jnp.where(lane < 96, c[i], 0.0)
    for u in range(bands):
        mine = out_ref[u * 36 : u * 36 + 36, :]
        base_ref[u, 0:27, :] = tighten(mine)
        base_ref[u, 27:32, :] = jnp.zeros((5, 128), f32)
    copies = [begin(out_ref, far_out, sems.at[2]), begin(base_ref, base_out, sems.at[1]), kept]
    for copy in copies:
        copy.wait()


def forward_kernel(p0, p1, p2, p3, p4, p5, p6, p7, o_far, w1_ref, g1_ref,
                   field_out, result_ref, stat_ref,
                   o_ref, field_ref, t_ref, w1, g1, out_ref, high, low, real, imag, sems):
    me = lax.axis_index("band")
    arrivals = [
        begin(piece, t_ref.at[pl.ds(4 * n, 4)], sems.at[n]) for n, piece in enumerate((p0, p1, p2, p3, p4, p5, p6, p7))
    ]
    arrivals.append(begin(o_far, o_ref, sems.at[10]))
    tables = [begin(w1_ref, w1, sems.at[8]), begin(g1_ref, g1, sems.at[9])]
    for copy in arrivals:
        copy.wait()
    norm = jnp.zeros((36, 128), f32)
    corr = [jnp.zeros((36, 128), f32) for _ in range(trials)]
    for u in range(bands):
        d = u ^ me
        z, y = d >> 3, (d >> 1) & 3
        if u & 1:
            z, y = (z >> 1) | ((y >> 1) << 1), ((z ^ (z >> 1)) & 1) | (((y ^ (y >> 1)) & 1) << 1)
            along, across = z, y
        else:
            along, across = y, z
        slot = ((d & 1) << 4) | (along << 2) | across
        blocks = [t_ref[slot, q * 36 : q * 36 + 36, :] for q in range(4)]
        fields = [*blocks[:3], unpack_last(*blocks[:3]), blocks[3]]
        here = slice(u * 36, u * 36 + 36)
        for p in range(5):
            field_ref[p, here, :] = fields[p]
        o = o_ref[here, :]
        square = o * o
        norm = norm + square
        for p in range(trials):
            corr[p] = corr[p] + fields[p] * square
    kept = begin(field_ref, field_out, sems.at[1])
    norm = total(norm)
    mean = [total(c) / norm for c in corr]

    size = 96

    def weigh(i, sums):
        at = pl.ds(pl.multiple_of(i * size, size), size)
        o = o_ref[at, :]
        out = []
        for p in range(trials):
            w = (field_ref[p, at, :] - mean[p]) * o
            high[at, p * 128 : p * 128 + 128], low[at, p * 128 : p * 128 + 128] = split(w)
            out.append(sums[p] + fold(w * w))
        high[at, 512:640], low[at, 512:640] = split(o)
        return tuple(out)

    second = lax.fori_loop(0, rows // size, weigh, tuple(jnp.zeros((8, 128), f32) for _ in range(trials)))
    second = [total(s) for s in second]
    stat_ref[...] = tile_of((8, 128), [(0, 0, norm)] + [(0, 1 + p, mean[p]) for p in range(trials)])

    for copy in tables:
        copy.wait()
    big = 384

    def along_z(i, _):
        at = pl.ds(pl.multiple_of(i * big, big), big)
        a = right_table(high[at, :], low[at, :], w1)
        real[at, :] = a[:, :128]
        imag[at, :] = a[:, 128:]
        return 0

    lax.fori_loop(0, rows // big, along_z, 0)

    row, lane = row_of((points, 128)), lane_of((points, 128))
    ride = jnp.where((row < 8) & (lane == 120), norm, 0.0)
    for p in range(trials):
        ride = jnp.where((row < 8) & (lane == 121 + p), mean[p], ride)
        ride = jnp.where((row >= 8) & (row < 16) & (lane == 120 + p), second[p], ride)
    for x in range(0, planes, 2):
        parts = [
            jnp.concatenate([ref[pl.ds(x + i, points, stride=planes), :] for i in range(2)], axis=1)
            for ref in (real, imag)
        ]
        y = left_table(g1, jnp.concatenate(parts, axis=0))
        for i in range(2):
            mine = y[:, i * 128 : i * 128 + 128] + ride
            for r in range(12):
                out_ref[pl.ds((x + i) * 12 + r, groups, stride=chunk), :] = mine[8 * r : 8 * r + 8]
    begin(out_ref, result_ref, sems.at[0]).wait()
    kept.wait()


def local_kernel(energy_ref, field_ref, o_ref, stat_ref, g2_ref, g3_ref, g4_ref, w2_ref, base_ref,
                 out_ref, g2, g3, g4, w2, tail_ref, sums, sems):
    step = pl.program_id(0)
    pairs = ((g2_ref, g2), (g3_ref, g3), (g4_ref, g4), (w2_ref, w2), (base_ref.at[:, pl.ds(24, 8), :], tail_ref))

    @pl.when(step == 0)
    def _():
        sums[...] = jnp.zeros(sums.shape, f32)
        for n, (source, target) in enumerate(pairs):
            pltpu.make_async_copy(source, target, sems.at[n]).start()

    o = o_ref[...]
    shift = (field_ref[4] - energy_ref[0]) * o
    sums[0] += fold(shift * o)
    for p in range(trials):
        off = field_ref[p] - stat_ref[0:1, 1 + p : 2 + p]
        both = shift * off
        sums[1 + p] += fold(both * o)
        sums[5 + p] += fold(both * (off * o))

    @pl.when(step == pl.num_programs(0) - 1)
    def _():
        out_ref[...] = tile_of((8, 128), [(0, n, total(sums[n])) for n in range(9)])
        for n, (source, target) in enumerate(pairs):
            pltpu.make_async_copy(source, target, sems.at[n]).wait()


def wave_kernel(in_ref, stat_ref, sums_ref, g2, g3, out_ref, scal_ref):
    owner = lax.axis_index("grid")
    s0 = in_ref[pl.ds(0, points, stride=planes), :]
    s1 = in_ref[pl.ds(1, points, stride=planes), :]
    weight = s0[:, 120:121]
    whole = jnp.sum(weight, axis=0, keepdims=True)
    lane = lane_of((points, 128))
    coef = jnp.zeros((points, 128), f32)
    alpha, start = [], []
    for p in range(trials):
        mean = s0[:, 121 + p : 122 + p]
        a = jnp.sum(weight * mean, axis=0, keepdims=True) / whole
        off = a - mean
        spread_sum = jnp.sum(s1[:, 120 + p : 121 + p] + weight * off * off, axis=0, keepdims=True)
        alpha.append(a)
        start.append(spread_sum / planes)
        coef = jnp.where((lane >= p * half) & (lane < (p + 1) * half), off, coef)

    def source_of(r):
        d = in_ref[pl.ds(r, points, stride=planes), :]
        o = jnp.where((lane >= 96) & (lane < 120), d, 0.0)
        o = pltpu.roll(o, 32, 1)
        o = o + pltpu.roll(o, 24, 1)
        o = o + pltpu.roll(o, 48, 1)
        return jnp.where(lane < 96, coef * o - d, 0.0)

    wide = (2 * half, 128)
    m = row_of(wide) - half
    k = lane_of(wide)
    k = k - jnp.where(k >= 72, 72, jnp.where(k >= 48, 48, jnp.where(k >= 24, 24, 0)))
    doubled = jnp.where(k == 0, 1.0, 2.0) * (prefactor / float(points**3))
    energy = jnp.zeros((1, 128), f32)
    own = [jnp.where(lane_of((1, 128)) == 0, 0.0, 0.0)]
    tails, directs = [], []
    for pair in (2, 1, 0):
        parts = [
            jnp.concatenate([source_of(2 * (2 * pair + i) + c) for i in range(2)], axis=1)
            for c in range(2)
        ]
        u = left_table(g2, jnp.concatenate(parts, axis=0))
        weights = []
        for i in range(2):
            j = owner * 6 + (2 * pair + i) - half
            square = m * m + k * k + j * j
            weights.append(jnp.where(square < half * half, doubled * square.astype(f32), 0.0))
        w = jnp.concatenate(weights, axis=1)
        t = u * jnp.concatenate([w, w], axis=0)
        product = jnp.sum(u * t, axis=0, keepdims=True)
        energy = energy + product[:, :128] + product[:, 128:]
        e = left_table(g3, t)
        for i in range(2):
            for c in range(2):
                r = 2 * (2 * pair + i) + c
                value = e[c * points : (c + 1) * points, i * 128 : i * 128 + 128]
                if r >= 9:
                    tails.append((r - 9, value))
                else:
                    directs.append((r, value))
        if pair == 2:
            tails = [value for _, value in sorted(tails, key=lambda entry: entry[0])]
        for r, value in directs:
            spare = pltpu.roll(tails[r // 3], 96 - 32 * (r % 3), 1)
            value = jnp.where(lane < 96, value, spare)
            for g in range(groups):
                out_ref[pl.ds(g * returned + r, planes, stride=9), :] = value[planes * g : planes * g + planes]
        directs = []
    l1 = lane_of((1, 128))
    ride = jnp.zeros((1, 128), f32)
    entries = []
    for p in range(trials):
        kinetic = jnp.sum(jnp.where((l1 >= p * half) & (l1 < (p + 1) * half), energy, 0.0), axis=1, keepdims=True)
        off = alpha[p] - stat_ref[0:1, 1 + p : 2 + p]
        at_p = sums_ref[0:1, 5 + p : 6 + p] - 2.0 * off * sums_ref[0:1, 1 + p : 2 + p] + off * off * sums_ref[0:1, 0:1]
        ride = jnp.where(l1 == 96 + p, kinetic + at_p, ride)
        entries += [(0, p, alpha[p]), (0, 4 + p, start[p])]
    scal_ref[...] = tile_of((8, 128), entries)
    for g in range(groups):
        out_ref[g * returned + 108 : g * returned + 112, :] = jnp.broadcast_to(ride, (4, 128))


def step_kernel(in_ref, scal_ref, tail_ref, base_ref, step_ref, out_ref, tail, sems):
    shares = jnp.sum(in_ref[pl.ds(108, groups, stride=returned), :], axis=0, keepdims=True)
    lane = lane_of((1, 128))
    start = jnp.where((lane >= 4) & (lane < 8), scal_ref[0:1, :], 0.0)
    curvature = pltpu.roll(jnp.where((lane >= 96) & (lane < 100), shares, 0.0), 36, 1)
    step = start / jnp.where((lane >= 4) & (lane < 8), curvature, 1.0)
    row = jnp.where(lane < 8, scal_ref[0:1, :], 0.0) + pltpu.roll(step, 4, 1)
    step_ref[...] = jnp.broadcast_to(row, (8, 128))
    last = jnp.where(row_of((8, 128)) == 4, row, 0.0)
    for v in range(bands):
        tail[v, :, :] = tail_ref[v, :, :] + last
    begin(tail, out_ref.at[:, pl.ds(24, 8), :], sems.at[0]).wait()


def image_kernel(energy_ref, in_ref, step_ref, field_far, o_far, g4, w2,
                 response_ref, residual_ref, norm_ref,
                 field_ref, o_ref, real, imag, kinetic, mixed_s, mixed_r, flat_s, flat_r, sems, out_sems):
    energy = energy_ref[0]
    third = rows // 3
    copies = []
    for n in range(3):
        at = pl.ds(n * third, third)
        copies.append((begin(field_far.at[:, at, :], field_ref.at[:, at, :], sems.at[n]),
                       begin(o_far.at[at], o_ref.at[at], sems.at[3 + n])))
    alpha = [step_ref[0:1, p : p + 1] for p in range(trials)]
    step = [step_ref[0:1, 8 + p : 9 + p] for p in range(trials)]
    narrow = lane_of((groups, 128))

    def waves_of(x):
        r = [in_ref[pl.ds(x * 9 + n, groups, stride=returned), :] for n in range(9)]
        for n in range(3):
            r0, r1, r2 = (pltpu.roll(r[3 * n + t], 32 + 32 * t, 1) for t in range(3))
            r.append(jnp.where(narrow < 32, r0, jnp.where(narrow < 64, r1, r2)))
        return jnp.concatenate(r, axis=0)

    for x in range(0, planes, 2):
        b = jnp.concatenate([waves_of(x), waves_of(x + 1)], axis=1)
        v = left_table(g4, b)
        for i in range(2):
            real[pl.ds(x + i, points, stride=planes), :] = v[:points, i * 128 : i * 128 + 128]
            imag[pl.ds(x + i, points, stride=planes), :] = v[points:, i * 128 : i * 128 + 128]
    size = 96
    mixed = planes * trials
    lane = lane_of((mixed, 128))

    def tiles(ref, q):
        c = [ref[(4 * q + i) * mixed : (4 * q + i + 1) * mixed, :] for i in range(4)]
        r1, r2, r3 = pltpu.roll(c[1], 96, 1), pltpu.roll(c[2], 64, 1), pltpu.roll(c[3], 32, 1)
        return jnp.where(lane < 96, c[0], r1), jnp.where(lane < 64, r1, r2), jnp.where(lane < 32, r2, r3)

    big = 384

    def along_z(i, _):
        at = pl.ds(pl.multiple_of(i * big, big), big)
        vh, vl = split(jnp.concatenate([real[at, :], imag[at, :]], axis=1))
        kinetic[at, :] = right_table(vh, vl, w2)
        return 0

    lax.fori_loop(0, rows // big, along_z, 0)

    def back(i, sums):
        at = pl.ds(pl.multiple_of(i * size, size), size)
        o = o_ref[at, :]
        shift = field_ref[4, at, :] - energy
        out = []
        for p in range(trials):
            source = (alpha[p] - field_ref[p, at, :]) * o
            image = kinetic[at, p * 128 : p * 128 + 128] + shift * source
            residual = source - step[p] * image
            there = pl.ds(p, size, stride=trials)
            mixed_s[there, :] = step[p] * source
            mixed_r[there, :] = residual
            out.append(sums[p] + fold(residual * residual))
        for flat, ref in ((flat_s, mixed_s), (flat_r, mixed_r)):
            for q in range(2):
                for n, tile in enumerate(tiles(ref, q)):
                    flat[i, :, :, 384 * q + 128 * n : 384 * q + 128 * n + 128] = tile.reshape(planes, trials, 128)
        cells = pl.ds(pl.multiple_of(i * 768, 768), 768)
        begin(flat_s.at[i], response_ref.at[:, :, cells], out_sems.at[0, i])
        begin(flat_r.at[i], residual_ref.at[:, :, cells], out_sems.at[1, i])
        return tuple(out)

    sums = tuple(jnp.zeros((8, 128), f32) for _ in range(trials))
    for n in range(3):
        for copy in copies[n]:
            copy.wait()
        sums = lax.fori_loop(n * (third // size), (n + 1) * (third // size), back, sums)
    norm_ref[...] = tile_of((8, 128), [(0, p, total(s)) for p, s in enumerate(sums)])
    for i in range(rows // size):
        cells = pl.ds(i * 768, 768)
        pltpu.make_async_copy(flat_s.at[i], response_ref.at[:, :, cells], out_sems.at[0, i]).wait()
        pltpu.make_async_copy(flat_r.at[i], residual_ref.at[:, :, cells], out_sems.at[1, i]).wait()


def direction_kernel(step_ref, n0, n1, response_ref, residual_ref, direction_ref, first, second, result, sems, out_sems):
    parts = 6
    width = points * points // parts
    loads = []
    for i in range(parts):
        cells = pl.ds(i * width, width)
        loads.append((begin(response_ref.at[:, :, cells], first.at[i], sems.at[0, i]),
                      begin(residual_ref.at[:, :, cells], second.at[i], sems.at[1, i])))
    new = n0[0:1, :] + n1[0:1, :]
    ratio = [new[:, p : p + 1] / step_ref[0:1, 4 + p : 5 + p] / step_ref[0:1, 8 + p : 9 + p] for p in range(trials)]
    r = row_of((trials, 128))
    ratios = jnp.zeros((trials, 128), f32)
    for p in range(trials):
        ratios = jnp.where(r == p, ratio[p], ratios)
    ratios = ratios[:, 0:1][None]
    stores = []
    for i in range(parts):
        for copy in loads[i]:
            copy.wait()
        result[i, :, :, :] = second[i] + ratios * first[i]
        stores.append(begin(result.at[i], direction_ref.at[:, :, pl.ds(i * width, width)], out_sems.at[i]))
    for copy in stores:
        copy.wait()


def density_kernel(packed_far, band_ref, density_ref, packed_ref, bands_in, sems):
    arrival = begin(band_ref, bands_in, sems.at[0])
    kept = begin(packed_far, packed_ref, sems.at[1])
    kept.wait()
    blocks = [packed_ref[q * 36 : q * 36 + 36, :] for q in range(3)]
    fields = [tighten(field) for field in (*blocks, unpack_last(*blocks))]
    sums = [jnp.zeros((27, 128), f32) for _ in range(trials)]
    arrival.wait()
    for v in range(bands):
        square = bands_in[v, 0:27, :]
        square = square * square
        for p in range(trials):
            alpha, step = bands_in[v, 28:29, p : p + 1], bands_in[v, 28:29, 8 + p : 9 + p]
            sums[p] = sums[p] + (step * (alpha - fields[p])) * square
    lane = lane_of((planes, 128))
    for p in range(trials):
        loose = loosen(sums[p]) * (4.0 / bands)
        c = [loose[12 * i : 12 * i + 12] for i in range(3)]
        r1, r2 = pltpu.roll(c[1], 96, 1), pltpu.roll(c[2], 64, 1)
        density_ref[:, p, 0:128] = jnp.where(lane < 96, c[0], r1)
        density_ref[:, p, 128:256] = jnp.where(lane < 64, r1, r2)
        density_ref[:, p, 256:288] = r2[:, 0:32]


vmem = pl.BlockSpec(memory_space=pltpu.VMEM)
smem = pl.BlockSpec(memory_space=pltpu.SMEM)
hbm = pl.BlockSpec(memory_space=pl.ANY)
far = pl.BlockSpec(memory_space=pltpu.HBM)


BIG = 56000000
SOME = 54500000


def shape(*dims, dtype=f32):
    return jax.ShapeDtypeStruct(dims, dtype)


def call(kernel, ins, outs, scratch=(), name=None, room=4 * 2**20, places=None, aliases=None, flops=10**6):
    return pl.pallas_call(
        kernel, out_shape=outs, in_specs=ins,
        out_specs=places if places is not None else jax.tree.map(lambda _: vmem, outs),
        scratch_shapes=scratch, compiler_params=pltpu.CompilerParams(vmem_limit_bytes=room), name=name, input_output_aliases=aliases or {},
        cost_estimate=pl.CostEstimate(flops=flops, bytes_accessed=10**6, transcendentals=0),
    )


def pack(trial, local):
    return call(
        pack_kernel, [far] * 2, shape(144, 128),
        [buffer(planes, trials, 288), buffer(planes, 288), pltpu.SemaphoreType.DMA((2,))], name="pack", room=66000000,
    )(jnp.transpose(trial, (1, 0, 2)), local)


def orbital_rows(orbitals, packed):
    return call(
        orbital_kernel, [vmem, vmem],
        (shape(rows, 128), shape(bands, 32, 128), shape(144, 128)),
        [buffer(rows, 128), buffer(bands, 32, 128), pltpu.SemaphoreType.DMA((3,))],
        name="orbital_rows", places=(far, far, far), room=BIG,
    )(orbitals, packed)


def buffer(*dims, dtype=f32):
    return pltpu.VMEM(dims, dtype)


def forward(pieces, o, tables):
    return call(
        forward_kernel, [hbm] * 8 + [far] * 3,
        (shape(5, rows, 128), shape(rows, 128), shape(8, 128)),
        [buffer(rows, 128), buffer(5, rows, 128), buffer(bands, 144, 128), buffer(2, 640, 256, dtype=bf16), buffer(2, 96, 192, dtype=bf16), buffer(rows, 128),
         buffer(rows, 640, dtype=bf16), buffer(rows, 640, dtype=bf16), buffer(rows, 128), buffer(rows, 128),
         pltpu.SemaphoreType.DMA((11,))],
        name="forward", room=SOME, places=(far, far, vmem),
    )(*pieces, o, tables["w1"], tables["g1"])


def local_sums(energies, fields, o, stat, tables, base):
    size, count = 192, rows // 192
    tile = pl.BlockSpec((8, 128), lambda i: (0, 0))
    kinds = [tables[name] for name in ("g2", "g3", "g4", "w2")]
    return pl.pallas_call(
        local_kernel, grid=(count,),
        in_specs=[smem, pl.BlockSpec((5, size, 128), lambda i: (0, i, 0)), pl.BlockSpec((size, 128), lambda i: (i, 0)),
                  tile] + [far] * 5,
        out_specs=(tile, *[vmem] * 5),
        out_shape=(shape(8, 128), *[shape(*t.shape, dtype=bf16) for t in kinds], shape(bands, 8, 128)),
        scratch_shapes=[buffer(9, 8, 128), pltpu.SemaphoreType.DMA((5,))],
        compiler_params=pltpu.CompilerParams(vmem_limit_bytes=BIG), name="local_sums",
        cost_estimate=pl.CostEstimate(flops=10**7, bytes_accessed=10**7, transcendentals=0),
    )(energies, fields, o, stat, *kinds, base)


def waves(arrived, stat, sums, g2, g3):
    return call(
        wave_kernel, [vmem] * 5, (shape(groups * returned, 128), shape(8, 128)), name="waves", room=8 * 2**20,
    )(arrived, stat, sums, g2, g3)


def steps(arrived, scal, tail, base):
    return call(
        step_kernel, [vmem] * 3 + [far], (shape(8, 128), shape(bands, 32, 128)),
        [buffer(bands, 8, 128), pltpu.SemaphoreType.DMA((1,))],
        name="steps", places=(vmem, far), aliases={3: 1},
    )(arrived, scal, tail, base)


def image(energies, arrived, step, fields, o, g4, w2):
    cells = shape(planes, trials, points * points)
    return call(
        image_kernel, [smem, vmem, vmem, far, far, vmem, vmem], (cells, cells, shape(8, 128)),
        [buffer(5, rows, 128), buffer(rows, 128), buffer(rows, 128), buffer(rows, 128), buffer(rows, 512),
         buffer(384, 128), buffer(384, 128),
         buffer(12, planes, trials, 768), buffer(12, planes, trials, 768),
         pltpu.SemaphoreType.DMA((6,)), pltpu.SemaphoreType.DMA((2, 12))],
        name="image", room=BIG, places=(far, far, vmem), flops=2 * 10**10,
    )(energies, arrived, step, fields, o, g4, w2)


def direct(step, norms, response, residual):
    part = buffer(6, planes, trials, points * points // 6)
    return call(
        direction_kernel, [vmem] * 3 + [far] * 2, shape(planes, trials, points * points),
        [part, part, part, pltpu.SemaphoreType.DMA((2, 6)), pltpu.SemaphoreType.DMA((6,))],
        name="direction", room=BIG, places=far, flops=10**7,
    )(step, *norms, response, residual)


def density_of(packed, band):
    return call(
        density_kernel, [far, hbm], shape(planes, trials, 288),
        [buffer(144, 128), buffer(bands, 32, 128), pltpu.SemaphoreType.DMA((2,))], name="density",
    )(packed, band)


def outward(value):
    return jnp.transpose(value, (1, 0, 2))


def swapped(value, axis, size, mask):
    return lax.ppermute(value, axis, [(s, s ^ mask) for s in range(size)])


def crossed(value, even, odd):
    return lax.ppermute(value, "band", [(s, s ^ (odd if s & 1 else even)) for s in range(bands)])


first_masks = ((8, 8), (16, 2), (24, 10))
second_masks = ((2, 24), (4, 6), (6, 30))


def gather_first(packed):
    value = packed[None]
    return jnp.concatenate([value] + [crossed(value, *masks) for masks in first_masks], axis=0)


def gather_second(quad):
    quads = [quad] + [crossed(quad, *masks) for masks in second_masks]
    return quads + [swapped(q, "band", bands, 1) for q in quads]


def on_device(orbitals, energies, local_pot, trial_pot):
    tables = {name: jnp.asarray(table) for name, table in build_tables().items()}
    packed = pack(trial_pot, local_pot)
    quad = gather_first(packed)
    o_far, base, packed_far = orbital_rows(orbitals, packed)
    quad, o_far = lax.optimization_barrier((quad, o_far))
    pieces = gather_second(quad)
    fields, sent, stat = forward(pieces, o_far, tables)
    arrived = lax.all_to_all(sent.reshape(groups, chunk, 128), "grid", 0, 0, tiled=True).reshape(rows, 128)
    sums, g2, g3, g4, w2, tail = local_sums(energies, fields, o_far, stat, tables, base)
    back, scal = waves(arrived, stat, sums, g2, g3)
    back = lax.all_to_all(back.reshape(groups, returned, 128), "grid", 0, 0, tiled=True).reshape(groups * returned, 128)
    step, payload = steps(back, scal, tail, base)
    band = lax.all_to_all(payload, "band", 0, 0, tiled=True)
    response, residual, norm = image(energies, back, step, fields, o_far, g4, w2)
    norm = norm + swapped(norm, "grid", groups, 2) + swapped(norm, "grid", groups, 4) + swapped(norm, "grid", groups, 6)
    norms = [norm, swapped(norm, "grid", groups, 1)]
    direction = direct(step, norms, response, residual)
    density = density_of(packed_far, band)
    return outward(response)[None], outward(residual)[None], outward(direction)[None], outward(density)


def solution(mesh):
    return jax.shard_map(
        on_device,
        mesh=mesh,
        in_specs=(P("band", "grid", None), P("band"), P("grid", "band"), P(None, "grid", "band")),
        out_specs=(
            P("band", None, "grid", None),
            P("band", None, "grid", None),
            P("band", None, "grid", None),
            P(None, "grid", "band"),
        ),
        check_vma=False,
    )
```

```python
import math

import jax
import jax.numpy as jnp
import ml_dtypes
import numpy as np
from jax import lax
from jax.experimental import pallas as pl
from jax.experimental.pallas import tpu as pltpu
from jax.sharding import PartitionSpec as P

points = 96
planes = 12
trials = 4
bands = 32
half = 24
groups = 8
rows = points * planes
chunk = rows // groups
returned = 112
spacing = 0.49
prefactor = 0.5 * (2.0 * math.pi / (points * spacing)) ** 2
f32 = jnp.float32
bf16 = jnp.bfloat16


def split_np(table):
    table = np.asarray(table, np.float32)
    high = table.astype(ml_dtypes.bfloat16)
    low = (table - high.astype(np.float32)).astype(ml_dtypes.bfloat16)
    return np.stack([high, low])


def angle(a, b):
    return (np.outer(a, b) % points) * (2.0 * np.pi / points)


def build_tables():
    grid = np.arange(points)
    signed = np.arange(2 * half) - half
    kz = np.arange(half)
    w1 = np.zeros((5 * 128, 256))
    az = angle(grid, kz)
    for p in range(5):
        w1[p * 128 : p * 128 + points, p * half : (p + 1) * half] = np.cos(az)
        w1[p * 128 : p * 128 + points, 128 + p * half : 128 + (p + 1) * half] = -np.sin(az)
    order = np.zeros(points, np.int64)
    part = np.zeros(points, np.int64)
    for jj in range(6):
        for c in range(2):
            for g in range(groups):
                order[(2 * jj + c) * 8 + g] = signed[6 * g + jj]
                part[(2 * jj + c) * 8 + g] = c
    ay = angle(order, grid)
    real = part[:, None] == 0
    g1 = np.concatenate(
        [np.where(real, np.cos(ay), -np.sin(ay)), np.where(real, np.sin(ay), np.cos(ay))], 1
    )
    g4 = np.concatenate(
        [np.where(real, np.cos(ay), -np.sin(ay)), np.where(real, np.sin(ay), np.cos(ay))], 1
    ).T
    ax = angle(signed, grid)
    cx, sx = np.cos(ax), np.sin(ax)
    g2 = np.block([[cx, sx], [-sx, cx]])
    g3 = np.block([[cx.T, -sx.T], [sx.T, cx.T]])
    w2 = np.zeros((256, 4 * 128))
    for p in range(4):
        w2[p * half : (p + 1) * half, p * 128 : p * 128 + points] = np.cos(az).T
        w2[128 + p * half : 128 + (p + 1) * half, p * 128 : p * 128 + points] = -np.sin(az).T
    return {"w1": split_np(w1), "g1": split_np(g1), "g2": split_np(g2), "g3": split_np(g3),
            "g4": split_np(g4), "w2": split_np(w2)}


def dot(a, b):
    return lax.dot_general(a, b, (((1,), (0,)), ((), ())), preferred_element_type=f32)


def split(value):
    high = value.astype(bf16)
    return high, (value - high.astype(f32)).astype(bf16)


def left_table(table, value):
    count = table.shape[1]
    vh, vl = split(value)
    both = dot(jnp.concatenate([table[0], table[1]], axis=0), vh)
    return both[:count] + both[count:] + dot(table[0], vl)


def right_table(vh, vl, table):
    count = vh.shape[0]
    both = dot(jnp.concatenate([vh, vl], axis=0), table[0])
    return both[:count] + both[count:] + dot(vh, table[1])


def begin(source, target, sem):
    copy = pltpu.make_async_copy(source, target, sem)
    copy.start()
    return copy


def lane_of(shape):
    return lax.broadcasted_iota(jnp.int32, shape, 1)


def row_of(shape):
    return lax.broadcasted_iota(jnp.int32, shape, 0)


def total(value):
    return jnp.sum(jnp.sum(value, axis=0, keepdims=True), axis=1, keepdims=True)


def fold(value):
    return jnp.sum(value.reshape(value.shape[0] // 8, 8, 128), axis=0)


def tile_of(shape, entries):
    row, lane = row_of(shape), lane_of(shape)
    out = jnp.zeros(shape, f32)
    for r, l, value in entries:
        out = jnp.where((row == r) & (lane == l), value, out)
    return out


def spread(t0, t1, t2):
    lane = lane_of(t0.shape)
    c1 = pltpu.roll(jnp.where(lane >= 96, t0, t1), 32, 1)
    c2 = pltpu.roll(jnp.where(lane >= 64, t1, t2), 64, 1)
    return t0, c1, c2


def pack_kernel(trial_far, local_far, out_ref, trial_ref, local_ref, sems):
    for copy in [begin(trial_far, trial_ref, sems.at[0]), begin(local_far, local_ref, sems.at[1])]:
        copy.wait()
    lane = lane_of((planes, 128))
    fill = jnp.zeros((planes, 96), f32)

    def pieces(ref, *at):
        t2 = jnp.concatenate([ref[(slice(None), *at, slice(256, 288))], fill], axis=1)
        return spread(ref[(slice(None), *at, slice(0, 128))], ref[(slice(None), *at, slice(128, 256))], t2)

    last = pieces(trial_ref, 3)
    for q in range(3):
        mine = pieces(trial_ref, q)
        for i in range(3):
            tail = pltpu.roll(last[i], 96 - 32 * q, 1)
            out_ref[q * 36 + i * 12 : q * 36 + i * 12 + 12, :] = jnp.where(lane < 96, mine[i], tail)
    mine = pieces(local_ref)
    for i in range(3):
        out_ref[108 + i * 12 : 120 + i * 12, :] = jnp.where(lane < 96, mine[i], 0.0)


def unpack_last(b0, b1, b2):
    lane = lane_of(b0.shape)
    r0, r1, r2 = pltpu.roll(b0, 32, 1), pltpu.roll(b1, 64, 1), pltpu.roll(b2, 96, 1)
    return jnp.where(lane < 32, r0, jnp.where(lane < 64, r1, r2))


def tighten(value):
    lane, tail = lane_of((9, 128)), value[27:36]
    return jnp.concatenate(
        [jnp.where(lane < 96, value[9 * t : 9 * t + 9], pltpu.roll(tail, 96 - 32 * t, 1)) for t in range(3)], axis=0
    )


def loosen(value):
    lane = lane_of((9, 128))
    r0, r1, r2 = (pltpu.roll(value[9 * t : 9 * t + 9], 32 + 32 * t, 1) for t in range(3))
    return jnp.concatenate([value, jnp.where(lane < 32, r0, jnp.where(lane < 64, r1, r2))], axis=0)


def orbital_kernel(o_ref, packed_ref, far_out, base_out, packed_out, out_ref, base_ref, sems):
    kept = begin(packed_ref, packed_out, sems.at[0])
    lane = lane_of((planes, 128))
    for q in range(points // 4):
        t = [o_ref[0, :, 384 * q + 128 * i : 384 * q + 128 * i + 128] for i in range(3)]
        c = [*spread(*t), pltpu.roll(t[2], 96, 1)]
        for i in range(4):
            at = (4 * q + i) * planes
            out_ref[at : at + planes, :] = jnp.where(lane < 96, c[i], 0.0)
    for u in range(bands):
        mine = out_ref[u * 36 : u * 36 + 36, :]
        base_ref[u, 0:27, :] = tighten(mine)
        base_ref[u, 27:32, :] = jnp.zeros((5, 128), f32)
    copies = [begin(out_ref, far_out, sems.at[2]), begin(base_ref, base_out, sems.at[1]), kept]
    for copy in copies:
        copy.wait()


def forward_kernel(p0, p1, p2, p3, p4, p5, p6, p7, o_far, w1_ref, g1_ref,
                   field_out, result_ref, stat_ref,
                   o_ref, field_ref, t_ref, w1, g1, out_ref, high, low, real, imag, sems):
    me = lax.axis_index("band")
    arrivals = [
        begin(piece, t_ref.at[pl.ds(4 * n, 4)], sems.at[n]) for n, piece in enumerate((p0, p1, p2, p3, p4, p5, p6, p7))
    ]
    arrivals.append(begin(o_far, o_ref, sems.at[10]))
    tables = [begin(w1_ref, w1, sems.at[8]), begin(g1_ref, g1, sems.at[9])]
    for copy in arrivals:
        copy.wait()
    norm = jnp.zeros((36, 128), f32)
    corr = [jnp.zeros((36, 128), f32) for _ in range(trials)]
    for u in range(bands):
        d = u ^ me
        z, y = d >> 3, (d >> 1) & 3
        if u & 1:
            z, y = (z >> 1) | ((y >> 1) << 1), ((z ^ (z >> 1)) & 1) | (((y ^ (y >> 1)) & 1) << 1)
            along, across = z, y
        else:
            along, across = y, z
        slot = ((d & 1) << 4) | (along << 2) | across
        blocks = [t_ref[slot, q * 36 : q * 36 + 36, :] for q in range(4)]
        fields = [*blocks[:3], unpack_last(*blocks[:3]), blocks[3]]
        here = slice(u * 36, u * 36 + 36)
        for p in range(5):
            field_ref[p, here, :] = fields[p]
        o = o_ref[here, :]
        square = o * o
        norm = norm + square
        for p in range(trials):
            corr[p] = corr[p] + fields[p] * square
    kept = begin(field_ref, field_out, sems.at[1])
    norm = total(norm)
    mean = [total(c) / norm for c in corr]

    size = 96

    def weigh(i, sums):
        at = pl.ds(pl.multiple_of(i * size, size), size)
        o = o_ref[at, :]
        out = []
        for p in range(trials):
            w = (field_ref[p, at, :] - mean[p]) * o
            high[at, p * 128 : p * 128 + 128], low[at, p * 128 : p * 128 + 128] = split(w)
            out.append(sums[p] + fold(w * w))
        high[at, 512:640], low[at, 512:640] = split(o)
        return tuple(out)

    second = lax.fori_loop(0, rows // size, weigh, tuple(jnp.zeros((8, 128), f32) for _ in range(trials)))
    second = [total(s) for s in second]
    stat_ref[...] = tile_of((8, 128), [(0, 0, norm)] + [(0, 1 + p, mean[p]) for p in range(trials)])

    for copy in tables:
        copy.wait()
    big = 576

    def along_z(i, _):
        at = pl.ds(pl.multiple_of(i * big, big), big)
        a = right_table(high[at, :], low[at, :], w1)
        real[at, :] = a[:, :128]
        imag[at, :] = a[:, 128:]
        return 0

    lax.fori_loop(0, rows // big, along_z, 0)

    row, lane = row_of((points, 128)), lane_of((points, 128))
    ride = jnp.where((row < 8) & (lane == 120), norm, 0.0)
    for p in range(trials):
        ride = jnp.where((row < 8) & (lane == 121 + p), mean[p], ride)
        ride = jnp.where((row >= 8) & (row < 16) & (lane == 120 + p), second[p], ride)
    for x in range(0, planes, 2):
        parts = [
            jnp.concatenate([ref[pl.ds(x + i, points, stride=planes), :] for i in range(2)], axis=1)
            for ref in (real, imag)
        ]
        y = left_table(g1, jnp.concatenate(parts, axis=0))
        for i in range(2):
            mine = y[:, i * 128 : i * 128 + 128] + ride
            for r in range(12):
                out_ref[pl.ds((x + i) * 12 + r, groups, stride=chunk), :] = mine[8 * r : 8 * r + 8]
    begin(out_ref, result_ref, sems.at[0]).wait()
    kept.wait()


def local_kernel(energy_ref, field_ref, o_ref, stat_ref, g2_ref, g3_ref, g4_ref, w2_ref, base_ref,
                 out_ref, g2, g3, g4, w2, tail_ref, sums, sems):
    step = pl.program_id(0)
    pairs = ((g2_ref, g2), (g3_ref, g3), (g4_ref, g4), (w2_ref, w2), (base_ref.at[:, pl.ds(24, 8), :], tail_ref))

    @pl.when(step == 0)
    def _():
        sums[...] = jnp.zeros(sums.shape, f32)
        for n, (source, target) in enumerate(pairs):
            pltpu.make_async_copy(source, target, sems.at[n]).start()

    o = o_ref[...]
    shift = (field_ref[4] - energy_ref[0]) * o
    sums[0] += fold(shift * o)
    for p in range(trials):
        off = field_ref[p] - stat_ref[0:1, 1 + p : 2 + p]
        both = shift * off
        sums[1 + p] += fold(both * o)
        sums[5 + p] += fold(both * (off * o))

    @pl.when(step == pl.num_programs(0) - 1)
    def _():
        out_ref[...] = tile_of((8, 128), [(0, n, total(sums[n])) for n in range(9)])
        for n, (source, target) in enumerate(pairs):
            pltpu.make_async_copy(source, target, sems.at[n]).wait()


def wave_kernel(in_ref, stat_ref, sums_ref, g2, g3, out_ref, scal_ref):
    owner = lax.axis_index("grid")
    s0 = in_ref[pl.ds(0, points, stride=planes), :]
    s1 = in_ref[pl.ds(1, points, stride=planes), :]
    weight = s0[:, 120:121]
    whole = jnp.sum(weight, axis=0, keepdims=True)
    lane = lane_of((points, 128))
    coef = jnp.zeros((points, 128), f32)
    alpha, start = [], []
    for p in range(trials):
        mean = s0[:, 121 + p : 122 + p]
        a = jnp.sum(weight * mean, axis=0, keepdims=True) / whole
        off = a - mean
        spread_sum = jnp.sum(s1[:, 120 + p : 121 + p] + weight * off * off, axis=0, keepdims=True)
        alpha.append(a)
        start.append(spread_sum / planes)
        coef = jnp.where((lane >= p * half) & (lane < (p + 1) * half), off, coef)

    def source_of(r):
        d = in_ref[pl.ds(r, points, stride=planes), :]
        o = jnp.where((lane >= 96) & (lane < 120), d, 0.0)
        o = pltpu.roll(o, 32, 1)
        o = o + pltpu.roll(o, 24, 1)
        o = o + pltpu.roll(o, 48, 1)
        return jnp.where(lane < 96, coef * o - d, 0.0)

    wide = (2 * half, 128)
    m = row_of(wide) - half
    k = lane_of(wide)
    k = k - jnp.where(k >= 72, 72, jnp.where(k >= 48, 48, jnp.where(k >= 24, 24, 0)))
    doubled = jnp.where(k == 0, 1.0, 2.0) * (prefactor / float(points**3))
    energy = jnp.zeros((1, 128), f32)
    own = [jnp.where(lane_of((1, 128)) == 0, 0.0, 0.0)]
    tails, directs = [], []
    for pair in (2, 1, 0):
        parts = [
            jnp.concatenate([source_of(2 * (2 * pair + i) + c) for i in range(2)], axis=1)
            for c in range(2)
        ]
        u = left_table(g2, jnp.concatenate(parts, axis=0))
        weights = []
        for i in range(2):
            j = owner * 6 + (2 * pair + i) - half
            square = m * m + k * k + j * j
            weights.append(jnp.where(square < half * half, doubled * square.astype(f32), 0.0))
        w = jnp.concatenate(weights, axis=1)
        t = u * jnp.concatenate([w, w], axis=0)
        product = jnp.sum(u * t, axis=0, keepdims=True)
        energy = energy + product[:, :128] + product[:, 128:]
        e = left_table(g3, t)
        for i in range(2):
            for c in range(2):
                r = 2 * (2 * pair + i) + c
                value = e[c * points : (c + 1) * points, i * 128 : i * 128 + 128]
                if r >= 9:
                    tails.append((r - 9, value))
                else:
                    directs.append((r, value))
        if pair == 2:
            tails = [value for _, value in sorted(tails, key=lambda entry: entry[0])]
        for r, value in directs:
            spare = pltpu.roll(tails[r // 3], 96 - 32 * (r % 3), 1)
            value = jnp.where(lane < 96, value, spare)
            for g in range(groups):
                out_ref[pl.ds(g * returned + r, planes, stride=9), :] = value[planes * g : planes * g + planes]
        directs = []
    l1 = lane_of((1, 128))
    ride = jnp.zeros((1, 128), f32)
    entries = []
    for p in range(trials):
        kinetic = jnp.sum(jnp.where((l1 >= p * half) & (l1 < (p + 1) * half), energy, 0.0), axis=1, keepdims=True)
        off = alpha[p] - stat_ref[0:1, 1 + p : 2 + p]
        at_p = sums_ref[0:1, 5 + p : 6 + p] - 2.0 * off * sums_ref[0:1, 1 + p : 2 + p] + off * off * sums_ref[0:1, 0:1]
        ride = jnp.where(l1 == 96 + p, kinetic + at_p, ride)
        entries += [(0, p, alpha[p]), (0, 4 + p, start[p])]
    scal_ref[...] = tile_of((8, 128), entries)
    for g in range(groups):
        out_ref[g * returned + 108 : g * returned + 112, :] = jnp.broadcast_to(ride, (4, 128))


def step_kernel(in_ref, scal_ref, tail_ref, base_ref, step_ref, out_ref, tail, sems):
    shares = jnp.sum(in_ref[pl.ds(108, groups, stride=returned), :], axis=0, keepdims=True)
    lane = lane_of((1, 128))
    start = jnp.where((lane >= 4) & (lane < 8), scal_ref[0:1, :], 0.0)
    curvature = pltpu.roll(jnp.where((lane >= 96) & (lane < 100), shares, 0.0), 36, 1)
    step = start / jnp.where((lane >= 4) & (lane < 8), curvature, 1.0)
    row = jnp.where(lane < 8, scal_ref[0:1, :], 0.0) + pltpu.roll(step, 4, 1)
    step_ref[...] = jnp.broadcast_to(row, (8, 128))
    last = jnp.where(row_of((8, 128)) == 4, row, 0.0)
    for v in range(bands):
        tail[v, :, :] = tail_ref[v, :, :] + last
    begin(tail, out_ref.at[:, pl.ds(24, 8), :], sems.at[0]).wait()


def image_kernel(energy_ref, in_ref, step_ref, field_far, o_far, g4, w2,
                 response_ref, residual_ref, norm_ref,
                 field_ref, o_ref, real, imag, kinetic, mixed_s, mixed_r, flat_s, flat_r, sems, out_sems):
    energy = energy_ref[0]
    third = rows // 3
    copies = []
    for n in range(3):
        at = pl.ds(n * third, third)
        copies.append((begin(field_far.at[:, at, :], field_ref.at[:, at, :], sems.at[n]),
                       begin(o_far.at[at], o_ref.at[at], sems.at[3 + n])))
    alpha = [step_ref[0:1, p : p + 1] for p in range(trials)]
    step = [step_ref[0:1, 8 + p : 9 + p] for p in range(trials)]
    narrow = lane_of((groups, 128))

    def waves_of(x):
        r = [in_ref[pl.ds(x * 9 + n, groups, stride=returned), :] for n in range(9)]
        for n in range(3):
            r0, r1, r2 = (pltpu.roll(r[3 * n + t], 32 + 32 * t, 1) for t in range(3))
            r.append(jnp.where(narrow < 32, r0, jnp.where(narrow < 64, r1, r2)))
        return jnp.concatenate(r, axis=0)

    for x in range(0, planes, 2):
        b = jnp.concatenate([waves_of(x), waves_of(x + 1)], axis=1)
        v = left_table(g4, b)
        for i in range(2):
            real[pl.ds(x + i, points, stride=planes), :] = v[:points, i * 128 : i * 128 + 128]
            imag[pl.ds(x + i, points, stride=planes), :] = v[points:, i * 128 : i * 128 + 128]
    size = 384
    mixed = planes * trials
    lane = lane_of((mixed, 128))

    def tiles(ref, q):
        c = [ref[(4 * q + i) * mixed : (4 * q + i + 1) * mixed, :] for i in range(4)]
        r1, r2, r3 = pltpu.roll(c[1], 96, 1), pltpu.roll(c[2], 64, 1), pltpu.roll(c[3], 32, 1)
        return jnp.where(lane < 96, c[0], r1), jnp.where(lane < 64, r1, r2), jnp.where(lane < 32, r2, r3)

    big = 384

    def along_z(i, _):
        at = pl.ds(pl.multiple_of(i * big, big), big)
        vh, vl = split(jnp.concatenate([real[at, :], imag[at, :]], axis=1))
        kinetic[at, :] = right_table(vh, vl, w2)
        return 0

    lax.fori_loop(0, rows // big, along_z, 0)

    def back(i, sums):
        at = pl.ds(pl.multiple_of(i * size, size), size)
        o = o_ref[at, :]
        shift = field_ref[4, at, :] - energy
        out = []
        for p in range(trials):
            source = (alpha[p] - field_ref[p, at, :]) * o
            image = kinetic[at, p * 128 : p * 128 + 128] + shift * source
            residual = source - step[p] * image
            there = pl.ds(p, size, stride=trials)
            mixed_s[there, :] = step[p] * source
            mixed_r[there, :] = residual
            out.append(sums[p] + fold(residual * residual))
        for flat, ref in ((flat_s, mixed_s), (flat_r, mixed_r)):
            for q in range(size // 48):
                for n, tile in enumerate(tiles(ref, q)):
                    flat[i, :, :, 384 * q + 128 * n : 384 * q + 128 * n + 128] = tile.reshape(planes, trials, 128)
        cells = pl.ds(pl.multiple_of(i * 3072, 3072), 3072)
        begin(flat_s.at[i], response_ref.at[:, :, cells], out_sems.at[0, i])
        begin(flat_r.at[i], residual_ref.at[:, :, cells], out_sems.at[1, i])
        return tuple(out)

    sums = tuple(jnp.zeros((8, 128), f32) for _ in range(trials))
    for n in range(3):
        for copy in copies[n]:
            copy.wait()
        sums = lax.fori_loop(n * (third // size), (n + 1) * (third // size), back, sums)
    norm_ref[...] = tile_of((8, 128), [(0, p, total(s)) for p, s in enumerate(sums)])
    for i in range(rows // size):
        cells = pl.ds(i * 3072, 3072)
        pltpu.make_async_copy(flat_s.at[i], response_ref.at[:, :, cells], out_sems.at[0, i]).wait()
        pltpu.make_async_copy(flat_r.at[i], residual_ref.at[:, :, cells], out_sems.at[1, i]).wait()


def direction_kernel(step_ref, n0, n1, response_ref, residual_ref, direction_ref, first, second, result, sems, out_sems):
    parts = 6
    width = points * points // parts
    loads = []
    for i in range(parts):
        cells = pl.ds(i * width, width)
        loads.append((begin(response_ref.at[:, :, cells], first.at[i], sems.at[0, i]),
                      begin(residual_ref.at[:, :, cells], second.at[i], sems.at[1, i])))
    new = n0[0:1, :] + n1[0:1, :]
    ratio = [new[:, p : p + 1] / step_ref[0:1, 4 + p : 5 + p] / step_ref[0:1, 8 + p : 9 + p] for p in range(trials)]
    r = row_of((trials, 128))
    ratios = jnp.zeros((trials, 128), f32)
    for p in range(trials):
        ratios = jnp.where(r == p, ratio[p], ratios)
    ratios = ratios[:, 0:1][None]
    stores = []
    for i in range(parts):
        for copy in loads[i]:
            copy.wait()
        result[i, :, :, :] = second[i] + ratios * first[i]
        stores.append(begin(result.at[i], direction_ref.at[:, :, pl.ds(i * width, width)], out_sems.at[i]))
    for copy in stores:
        copy.wait()


def density_kernel(packed_far, band_ref, density_ref, packed_ref, bands_in, sems):
    arrival = begin(band_ref, bands_in, sems.at[0])
    kept = begin(packed_far, packed_ref, sems.at[1])
    kept.wait()
    blocks = [packed_ref[q * 36 : q * 36 + 36, :] for q in range(3)]
    fields = [tighten(field) for field in (*blocks, unpack_last(*blocks))]
    sums = [jnp.zeros((27, 128), f32) for _ in range(trials)]
    arrival.wait()
    for v in range(bands):
        square = bands_in[v, 0:27, :]
        square = square * square
        for p in range(trials):
            alpha, step = bands_in[v, 28:29, p : p + 1], bands_in[v, 28:29, 8 + p : 9 + p]
            sums[p] = sums[p] + (step * (alpha - fields[p])) * square
    lane = lane_of((planes, 128))
    for p in range(trials):
        loose = loosen(sums[p]) * (4.0 / bands)
        c = [loose[12 * i : 12 * i + 12] for i in range(3)]
        r1, r2 = pltpu.roll(c[1], 96, 1), pltpu.roll(c[2], 64, 1)
        density_ref[:, p, 0:128] = jnp.where(lane < 96, c[0], r1)
        density_ref[:, p, 128:256] = jnp.where(lane < 64, r1, r2)
        density_ref[:, p, 256:288] = r2[:, 0:32]


vmem = pl.BlockSpec(memory_space=pltpu.VMEM)
smem = pl.BlockSpec(memory_space=pltpu.SMEM)
hbm = pl.BlockSpec(memory_space=pl.ANY)
far = pl.BlockSpec(memory_space=pltpu.HBM)


BIG = 56000000
SOME = 54500000


def shape(*dims, dtype=f32):
    return jax.ShapeDtypeStruct(dims, dtype)


def call(kernel, ins, outs, scratch=(), name=None, room=4 * 2**20, places=None, aliases=None, flops=10**6):
    return pl.pallas_call(
        kernel, out_shape=outs, in_specs=ins,
        out_specs=places if places is not None else jax.tree.map(lambda _: vmem, outs),
        scratch_shapes=scratch, compiler_params=pltpu.CompilerParams(vmem_limit_bytes=room), name=name, input_output_aliases=aliases or {},
        cost_estimate=pl.CostEstimate(flops=flops, bytes_accessed=10**6, transcendentals=0),
    )


def pack(trial, local):
    return call(
        pack_kernel, [far] * 2, shape(144, 128),
        [buffer(planes, trials, 288), buffer(planes, 288), pltpu.SemaphoreType.DMA((2,))], name="pack", room=66000000,
    )(jnp.transpose(trial, (1, 0, 2)), local)


def orbital_rows(orbitals, packed):
    return call(
        orbital_kernel, [vmem, vmem],
        (shape(rows, 128), shape(bands, 32, 128), shape(144, 128)),
        [buffer(rows, 128), buffer(bands, 32, 128), pltpu.SemaphoreType.DMA((3,))],
        name="orbital_rows", places=(far, far, far), room=BIG,
    )(orbitals, packed)


def buffer(*dims, dtype=f32):
    return pltpu.VMEM(dims, dtype)


def forward(pieces, o, tables):
    return call(
        forward_kernel, [hbm] * 8 + [far] * 3,
        (shape(5, rows, 128), shape(rows, 128), shape(8, 128)),
        [buffer(rows, 128), buffer(5, rows, 128), buffer(bands, 144, 128), buffer(2, 640, 256, dtype=bf16), buffer(2, 96, 192, dtype=bf16), buffer(rows, 128),
         buffer(rows, 640, dtype=bf16), buffer(rows, 640, dtype=bf16), buffer(rows, 128), buffer(rows, 128),
         pltpu.SemaphoreType.DMA((11,))],
        name="forward", room=SOME, places=(far, far, vmem),
    )(*pieces, o, tables["w1"], tables["g1"])


def local_sums(energies, fields, o, stat, tables, base):
    size, count = 192, rows // 192
    tile = pl.BlockSpec((8, 128), lambda i: (0, 0))
    kinds = [tables[name] for name in ("g2", "g3", "g4", "w2")]
    return pl.pallas_call(
        local_kernel, grid=(count,),
        in_specs=[smem, pl.BlockSpec((5, size, 128), lambda i: (0, i, 0)), pl.BlockSpec((size, 128), lambda i: (i, 0)),
                  tile] + [far] * 5,
        out_specs=(tile, *[vmem] * 5),
        out_shape=(shape(8, 128), *[shape(*t.shape, dtype=bf16) for t in kinds], shape(bands, 8, 128)),
        scratch_shapes=[buffer(9, 8, 128), pltpu.SemaphoreType.DMA((5,))],
        compiler_params=pltpu.CompilerParams(vmem_limit_bytes=BIG), name="local_sums",
        cost_estimate=pl.CostEstimate(flops=10**7, bytes_accessed=10**7, transcendentals=0),
    )(energies, fields, o, stat, *kinds, base)


def waves(arrived, stat, sums, g2, g3):
    return call(
        wave_kernel, [vmem] * 5, (shape(groups * returned, 128), shape(8, 128)), name="waves", room=8 * 2**20,
    )(arrived, stat, sums, g2, g3)


def steps(arrived, scal, tail, base):
    return call(
        step_kernel, [vmem] * 3 + [far], (shape(8, 128), shape(bands, 32, 128)),
        [buffer(bands, 8, 128), pltpu.SemaphoreType.DMA((1,))],
        name="steps", places=(vmem, far), aliases={3: 1},
    )(arrived, scal, tail, base)


def image(energies, arrived, step, fields, o, g4, w2):
    cells = shape(planes, trials, points * points)
    return call(
        image_kernel, [smem, vmem, vmem, far, far, vmem, vmem], (cells, cells, shape(8, 128)),
        [buffer(5, rows, 128), buffer(rows, 128), buffer(rows, 128), buffer(rows, 128), buffer(rows, 512),
         buffer(1536, 128), buffer(1536, 128),
         buffer(3, planes, trials, 3072), buffer(3, planes, trials, 3072),
         pltpu.SemaphoreType.DMA((6,)), pltpu.SemaphoreType.DMA((2, 6))],
        name="image", room=BIG, places=(far, far, vmem), flops=2 * 10**10,
    )(energies, arrived, step, fields, o, g4, w2)


def direct(step, norms, response, residual):
    part = buffer(6, planes, trials, points * points // 6)
    return call(
        direction_kernel, [vmem] * 3 + [far] * 2, shape(planes, trials, points * points),
        [part, part, part, pltpu.SemaphoreType.DMA((2, 6)), pltpu.SemaphoreType.DMA((6,))],
        name="direction", room=BIG, places=far, flops=10**7,
    )(step, *norms, response, residual)


def density_of(packed, band):
    return call(
        density_kernel, [far, hbm], shape(planes, trials, 288),
        [buffer(144, 128), buffer(bands, 32, 128), pltpu.SemaphoreType.DMA((2,))], name="density",
    )(packed, band)


def outward(value):
    return jnp.transpose(value, (1, 0, 2))


def swapped(value, axis, size, mask):
    return lax.ppermute(value, axis, [(s, s ^ mask) for s in range(size)])


def crossed(value, even, odd):
    return lax.ppermute(value, "band", [(s, s ^ (odd if s & 1 else even)) for s in range(bands)])


first_masks = ((8, 8), (16, 2), (24, 10))
second_masks = ((2, 24), (4, 6), (6, 30))


def gather_first(packed):
    value = packed[None]
    return jnp.concatenate([value] + [crossed(value, *masks) for masks in first_masks], axis=0)


def gather_second(quad):
    quads = [quad] + [crossed(quad, *masks) for masks in second_masks]
    return quads + [swapped(q, "band", bands, 1) for q in quads]


def on_device(orbitals, energies, local_pot, trial_pot):
    tables = {name: jnp.asarray(table) for name, table in build_tables().items()}
    packed = pack(trial_pot, local_pot)
    quad = gather_first(packed)
    o_far, base, packed_far = orbital_rows(orbitals, packed)
    quad, o_far = lax.optimization_barrier((quad, o_far))
    pieces = gather_second(quad)
    fields, sent, stat = forward(pieces, o_far, tables)
    arrived = lax.all_to_all(sent.reshape(groups, chunk, 128), "grid", 0, 0, tiled=True).reshape(rows, 128)
    sums, g2, g3, g4, w2, tail = local_sums(energies, fields, o_far, stat, tables, base)
    back, scal = waves(arrived, stat, sums, g2, g3)
    back = lax.all_to_all(back.reshape(groups, returned, 128), "grid", 0, 0, tiled=True).reshape(groups * returned, 128)
    step, payload = steps(back, scal, tail, base)
    band = lax.all_to_all(payload, "band", 0, 0, tiled=True)
    response, residual, norm = image(energies, back, step, fields, o_far, g4, w2)
    norm = norm + swapped(norm, "grid", groups, 2) + swapped(norm, "grid", groups, 4) + swapped(norm, "grid", groups, 6)
    norms = [norm, swapped(norm, "grid", groups, 1)]
    direction = direct(step, norms, response, residual)
    density = density_of(packed_far, band)
    return outward(response)[None], outward(residual)[None], outward(direction)[None], outward(density)


def solution(mesh):
    return jax.shard_map(
        on_device,
        mesh=mesh,
        in_specs=(P("band", "grid", None), P("band"), P("grid", "band"), P(None, "grid", "band")),
        out_specs=(
            P("band", None, "grid", None),
            P("band", None, "grid", None),
            P("band", None, "grid", None),
            P(None, "grid", "band"),
        ),
        check_vma=False,
    )
```

```python
import math

import jax
import jax.numpy as jnp
import ml_dtypes
import numpy as np
from jax import lax
from jax.experimental import pallas as pl
from jax.experimental.pallas import tpu as pltpu
from jax.sharding import PartitionSpec as P

points = 96
planes = 12
trials = 4
bands = 32
half = 24
groups = 8
rows = points * planes
chunk = rows // groups
returned = 112
spacing = 0.49
prefactor = 0.5 * (2.0 * math.pi / (points * spacing)) ** 2
f32 = jnp.float32
bf16 = jnp.bfloat16


def split_np(table):
    table = np.asarray(table, np.float32)
    high = table.astype(ml_dtypes.bfloat16)
    low = (table - high.astype(np.float32)).astype(ml_dtypes.bfloat16)
    return np.stack([high, low])


def angle(a, b):
    return (np.outer(a, b) % points) * (2.0 * np.pi / points)


def build_tables():
    grid = np.arange(points)
    signed = np.arange(2 * half) - half
    kz = np.arange(half)
    w1 = np.zeros((5 * 128, 256))
    az = angle(grid, kz)
    for p in range(5):
        w1[p * 128 : p * 128 + points, p * half : (p + 1) * half] = np.cos(az)
        w1[p * 128 : p * 128 + points, 128 + p * half : 128 + (p + 1) * half] = -np.sin(az)
    order = np.zeros(points, np.int64)
    part = np.zeros(points, np.int64)
    for jj in range(6):
        for c in range(2):
            for g in range(groups):
                order[(2 * jj + c) * 8 + g] = signed[6 * g + jj]
                part[(2 * jj + c) * 8 + g] = c
    ay = angle(order, grid)
    real = part[:, None] == 0
    g1 = np.concatenate(
        [np.where(real, np.cos(ay), -np.sin(ay)), np.where(real, np.sin(ay), np.cos(ay))], 1
    )
    g4 = np.concatenate(
        [np.where(real, np.cos(ay), -np.sin(ay)), np.where(real, np.sin(ay), np.cos(ay))], 1
    ).T
    ax = angle(signed, grid)
    cx, sx = np.cos(ax), np.sin(ax)
    g2 = np.block([[cx, sx], [-sx, cx]])
    g3 = np.block([[cx.T, -sx.T], [sx.T, cx.T]])
    w2 = np.zeros((256, 4 * 128))
    for p in range(4):
        w2[p * half : (p + 1) * half, p * 128 : p * 128 + points] = np.cos(az).T
        w2[128 + p * half : 128 + (p + 1) * half, p * 128 : p * 128 + points] = -np.sin(az).T
    return {"w1": split_np(w1), "g1": split_np(g1), "g2": split_np(g2), "g3": split_np(g3),
            "g4": split_np(g4), "w2": split_np(w2)}


def dot(a, b):
    return lax.dot_general(a, b, (((1,), (0,)), ((), ())), preferred_element_type=f32)


def split(value):
    high = value.astype(bf16)
    return high, (value - high.astype(f32)).astype(bf16)


def left_table(table, value):
    count = table.shape[1]
    vh, vl = split(value)
    both = dot(jnp.concatenate([table[0], table[1]], axis=0), vh)
    return both[:count] + both[count:] + dot(table[0], vl)


def right_table(vh, vl, table):
    count = vh.shape[0]
    both = dot(jnp.concatenate([vh, vl], axis=0), table[0])
    return both[:count] + both[count:] + dot(vh, table[1])


def begin(source, target, sem):
    copy = pltpu.make_async_copy(source, target, sem)
    copy.start()
    return copy


def lane_of(shape):
    return lax.broadcasted_iota(jnp.int32, shape, 1)


def row_of(shape):
    return lax.broadcasted_iota(jnp.int32, shape, 0)


def total(value):
    return jnp.sum(jnp.sum(value, axis=0, keepdims=True), axis=1, keepdims=True)


def fold(value):
    return jnp.sum(value.reshape(value.shape[0] // 8, 8, 128), axis=0)


def tile_of(shape, entries):
    row, lane = row_of(shape), lane_of(shape)
    out = jnp.zeros(shape, f32)
    for r, l, value in entries:
        out = jnp.where((row == r) & (lane == l), value, out)
    return out


def spread(t0, t1, t2):
    lane = lane_of(t0.shape)
    c1 = pltpu.roll(jnp.where(lane >= 96, t0, t1), 32, 1)
    c2 = pltpu.roll(jnp.where(lane >= 64, t1, t2), 64, 1)
    return t0, c1, c2


def pack_kernel(trial_far, local_far, out_ref, trial_ref, local_ref, sems):
    for copy in [begin(trial_far, trial_ref, sems.at[0]), begin(local_far, local_ref, sems.at[1])]:
        copy.wait()
    lane = lane_of((planes, 128))
    fill = jnp.zeros((planes, 96), f32)

    def pieces(ref, *at):
        t2 = jnp.concatenate([ref[(slice(None), *at, slice(256, 288))], fill], axis=1)
        return spread(ref[(slice(None), *at, slice(0, 128))], ref[(slice(None), *at, slice(128, 256))], t2)

    last = pieces(trial_ref, 3)
    for q in range(3):
        mine = pieces(trial_ref, q)
        for i in range(3):
            tail = pltpu.roll(last[i], 96 - 32 * q, 1)
            out_ref[q * 36 + i * 12 : q * 36 + i * 12 + 12, :] = jnp.where(lane < 96, mine[i], tail)
    mine = pieces(local_ref)
    for i in range(3):
        out_ref[108 + i * 12 : 120 + i * 12, :] = jnp.where(lane < 96, mine[i], 0.0)


def unpack_last(b0, b1, b2):
    lane = lane_of(b0.shape)
    r0, r1, r2 = pltpu.roll(b0, 32, 1), pltpu.roll(b1, 64, 1), pltpu.roll(b2, 96, 1)
    return jnp.where(lane < 32, r0, jnp.where(lane < 64, r1, r2))


def tighten(value):
    lane, tail = lane_of((9, 128)), value[27:36]
    return jnp.concatenate(
        [jnp.where(lane < 96, value[9 * t : 9 * t + 9], pltpu.roll(tail, 96 - 32 * t, 1)) for t in range(3)], axis=0
    )


def loosen(value):
    lane = lane_of((9, 128))
    r0, r1, r2 = (pltpu.roll(value[9 * t : 9 * t + 9], 32 + 32 * t, 1) for t in range(3))
    return jnp.concatenate([value, jnp.where(lane < 32, r0, jnp.where(lane < 64, r1, r2))], axis=0)


def orbital_kernel(o_ref, packed_ref, far_out, base_out, packed_out, out_ref, base_ref, sems):
    kept = begin(packed_ref, packed_out, sems.at[0])
    lane = lane_of((planes, 128))
    for q in range(points // 4):
        t = [o_ref[0, :, 384 * q + 128 * i : 384 * q + 128 * i + 128] for i in range(3)]
        c = [*spread(*t), pltpu.roll(t[2], 96, 1)]
        for i in range(4):
            at = (4 * q + i) * planes
            out_ref[at : at + planes, :] = jnp.where(lane < 96, c[i], 0.0)
    for u in range(bands):
        mine = out_ref[u * 36 : u * 36 + 36, :]
        base_ref[u, 0:27, :] = tighten(mine)
        base_ref[u, 27:32, :] = jnp.zeros((5, 128), f32)
    copies = [begin(out_ref, far_out, sems.at[2]), begin(base_ref, base_out, sems.at[1]), kept]
    for copy in copies:
        copy.wait()


def forward_kernel(p0, p1, p2, p3, p4, p5, p6, p7, o_far, w1_ref, g1_ref,
                   field_out, result_ref, stat_ref,
                   o_ref, field_ref, t_ref, w1, g1, out_ref, high, low, real, imag, sems):
    me = lax.axis_index("band")
    arrivals = [
        begin(piece, t_ref.at[pl.ds(4 * n, 4)], sems.at[n]) for n, piece in enumerate((p0, p1, p2, p3, p4, p5, p6, p7))
    ]
    arrivals.append(begin(o_far, o_ref, sems.at[10]))
    tables = [begin(w1_ref, w1, sems.at[8]), begin(g1_ref, g1, sems.at[9])]
    for copy in arrivals:
        copy.wait()
    norm = jnp.zeros((36, 128), f32)
    corr = [jnp.zeros((36, 128), f32) for _ in range(trials)]
    for u in range(bands):
        d = u ^ me
        z, y = d >> 3, (d >> 1) & 3
        if u & 1:
            z, y = (z >> 1) | ((y >> 1) << 1), ((z ^ (z >> 1)) & 1) | (((y ^ (y >> 1)) & 1) << 1)
            along, across = z, y
        else:
            along, across = y, z
        slot = ((d & 1) << 4) | (along << 2) | across
        blocks = [t_ref[slot, q * 36 : q * 36 + 36, :] for q in range(4)]
        fields = [*blocks[:3], unpack_last(*blocks[:3]), blocks[3]]
        here = slice(u * 36, u * 36 + 36)
        for p in range(5):
            field_ref[p, here, :] = fields[p]
        o = o_ref[here, :]
        square = o * o
        norm = norm + square
        for p in range(trials):
            corr[p] = corr[p] + fields[p] * square
    kept = begin(field_ref, field_out, sems.at[1])
    norm = total(norm)
    mean = [total(c) / norm for c in corr]

    size = 96

    def weigh(i, sums):
        at = pl.ds(pl.multiple_of(i * size, size), size)
        o = o_ref[at, :]
        out = []
        for p in range(trials):
            w = (field_ref[p, at, :] - mean[p]) * o
            high[at, p * 128 : p * 128 + 128], low[at, p * 128 : p * 128 + 128] = split(w)
            out.append(sums[p] + fold(w * w))
        high[at, 512:640], low[at, 512:640] = split(o)
        return tuple(out)

    second = lax.fori_loop(0, rows // size, weigh, tuple(jnp.zeros((8, 128), f32) for _ in range(trials)))
    second = [total(s) for s in second]
    stat_ref[...] = tile_of((8, 128), [(0, 0, norm)] + [(0, 1 + p, mean[p]) for p in range(trials)])

    for copy in tables:
        copy.wait()
    big = 576

    def along_z(i, _):
        at = pl.ds(pl.multiple_of(i * big, big), big)
        a = right_table(high[at, :], low[at, :], w1)
        real[at, :] = a[:, :128]
        imag[at, :] = a[:, 128:]
        return 0

    lax.fori_loop(0, rows // big, along_z, 0)

    row, lane = row_of((points, 128)), lane_of((points, 128))
    ride = jnp.where((row < 8) & (lane == 120), norm, 0.0)
    for p in range(trials):
        ride = jnp.where((row < 8) & (lane == 121 + p), mean[p], ride)
        ride = jnp.where((row >= 8) & (row < 16) & (lane == 120 + p), second[p], ride)
    for x in range(0, planes, 2):
        parts = [
            jnp.concatenate([ref[pl.ds(x + i, points, stride=planes), :] for i in range(2)], axis=1)
            for ref in (real, imag)
        ]
        y = left_table(g1, jnp.concatenate(parts, axis=0))
        for i in range(2):
            mine = y[:, i * 128 : i * 128 + 128] + ride
            for r in range(12):
                out_ref[pl.ds((x + i) * 12 + r, groups, stride=chunk), :] = mine[8 * r : 8 * r + 8]
    begin(out_ref, result_ref, sems.at[0]).wait()
    kept.wait()


def local_kernel(energy_ref, field_ref, o_ref, stat_ref, g2_ref, g3_ref, g4_ref, w2_ref, base_ref,
                 out_ref, g2, g3, g4, w2, tail_ref, sums, sems):
    step = pl.program_id(0)
    pairs = ((g2_ref, g2), (g3_ref, g3), (g4_ref, g4), (w2_ref, w2), (base_ref.at[:, pl.ds(24, 8), :], tail_ref))

    @pl.when(step == 0)
    def _():
        sums[...] = jnp.zeros(sums.shape, f32)
        for n, (source, target) in enumerate(pairs):
            pltpu.make_async_copy(source, target, sems.at[n]).start()

    o = o_ref[...]
    shift = (field_ref[4] - energy_ref[0]) * o
    sums[0] += fold(shift * o)
    for p in range(trials):
        off = field_ref[p] - stat_ref[0:1, 1 + p : 2 + p]
        both = shift * off
        sums[1 + p] += fold(both * o)
        sums[5 + p] += fold(both * (off * o))

    @pl.when(step == pl.num_programs(0) - 1)
    def _():
        out_ref[...] = tile_of((8, 128), [(0, n, total(sums[n])) for n in range(9)])
        for n, (source, target) in enumerate(pairs):
            pltpu.make_async_copy(source, target, sems.at[n]).wait()


def wave_kernel(in_ref, stat_ref, sums_ref, g2, g3, out_ref, scal_ref):
    owner = lax.axis_index("grid")
    s0 = in_ref[pl.ds(0, points, stride=planes), :]
    s1 = in_ref[pl.ds(1, points, stride=planes), :]
    weight = s0[:, 120:121]
    whole = jnp.sum(weight, axis=0, keepdims=True)
    lane = lane_of((points, 128))
    coef = jnp.zeros((points, 128), f32)
    alpha, start = [], []
    for p in range(trials):
        mean = s0[:, 121 + p : 122 + p]
        a = jnp.sum(weight * mean, axis=0, keepdims=True) / whole
        off = a - mean
        spread_sum = jnp.sum(s1[:, 120 + p : 121 + p] + weight * off * off, axis=0, keepdims=True)
        alpha.append(a)
        start.append(spread_sum / planes)
        coef = jnp.where((lane >= p * half) & (lane < (p + 1) * half), off, coef)

    def source_of(r):
        d = in_ref[pl.ds(r, points, stride=planes), :]
        o = jnp.where((lane >= 96) & (lane < 120), d, 0.0)
        o = pltpu.roll(o, 32, 1)
        o = o + pltpu.roll(o, 24, 1)
        o = o + pltpu.roll(o, 48, 1)
        return jnp.where(lane < 96, coef * o - d, 0.0)

    wide = (2 * half, 128)
    m = row_of(wide) - half
    k = lane_of(wide)
    k = k - jnp.where(k >= 72, 72, jnp.where(k >= 48, 48, jnp.where(k >= 24, 24, 0)))
    doubled = jnp.where(k == 0, 1.0, 2.0) * (prefactor / float(points**3))
    energy = jnp.zeros((1, 128), f32)
    own = [jnp.where(lane_of((1, 128)) == 0, 0.0, 0.0)]
    tails, directs = [], []
    for pair in (2, 1, 0):
        parts = [
            jnp.concatenate([source_of(2 * (2 * pair + i) + c) for i in range(2)], axis=1)
            for c in range(2)
        ]
        u = left_table(g2, jnp.concatenate(parts, axis=0))
        weights = []
        for i in range(2):
            j = owner * 6 + (2 * pair + i) - half
            square = m * m + k * k + j * j
            weights.append(jnp.where(square < half * half, doubled * square.astype(f32), 0.0))
        w = jnp.concatenate(weights, axis=1)
        t = u * jnp.concatenate([w, w], axis=0)
        product = jnp.sum(u * t, axis=0, keepdims=True)
        energy = energy + product[:, :128] + product[:, 128:]
        e = left_table(g3, t)
        for i in range(2):
            for c in range(2):
                r = 2 * (2 * pair + i) + c
                value = e[c * points : (c + 1) * points, i * 128 : i * 128 + 128]
                if r >= 9:
                    tails.append((r - 9, value))
                else:
                    directs.append((r, value))
        if pair == 2:
            tails = [value for _, value in sorted(tails, key=lambda entry: entry[0])]
        for r, value in directs:
            spare = pltpu.roll(tails[r // 3], 96 - 32 * (r % 3), 1)
            value = jnp.where(lane < 96, value, spare)
            for g in range(groups):
                out_ref[pl.ds(g * returned + r, planes, stride=9), :] = value[planes * g : planes * g + planes]
        directs = []
    l1 = lane_of((1, 128))
    ride = jnp.zeros((1, 128), f32)
    entries = []
    for p in range(trials):
        kinetic = jnp.sum(jnp.where((l1 >= p * half) & (l1 < (p + 1) * half), energy, 0.0), axis=1, keepdims=True)
        off = alpha[p] - stat_ref[0:1, 1 + p : 2 + p]
        at_p = sums_ref[0:1, 5 + p : 6 + p] - 2.0 * off * sums_ref[0:1, 1 + p : 2 + p] + off * off * sums_ref[0:1, 0:1]
        ride = jnp.where(l1 == 96 + p, kinetic + at_p, ride)
        entries += [(0, p, alpha[p]), (0, 4 + p, start[p])]
    scal_ref[...] = tile_of((8, 128), entries)
    for g in range(groups):
        out_ref[g * returned + 108 : g * returned + 112, :] = jnp.broadcast_to(ride, (4, 128))


def step_kernel(in_ref, scal_ref, tail_ref, base_ref, step_ref, out_ref, tail, sems):
    shares = jnp.sum(in_ref[pl.ds(108, groups, stride=returned), :], axis=0, keepdims=True)
    lane = lane_of((1, 128))
    start = jnp.where((lane >= 4) & (lane < 8), scal_ref[0:1, :], 0.0)
    curvature = pltpu.roll(jnp.where((lane >= 96) & (lane < 100), shares, 0.0), 36, 1)
    step = start / jnp.where((lane >= 4) & (lane < 8), curvature, 1.0)
    row = jnp.where(lane < 8, scal_ref[0:1, :], 0.0) + pltpu.roll(step, 4, 1)
    step_ref[...] = jnp.broadcast_to(row, (8, 128))
    last = jnp.where(row_of((8, 128)) == 4, row, 0.0)
    for v in range(bands):
        tail[v, :, :] = tail_ref[v, :, :] + last
    begin(tail, out_ref.at[:, pl.ds(24, 8), :], sems.at[0]).wait()


def image_kernel(energy_ref, in_ref, step_ref, field_far, o_far, g4, w2,
                 response_ref, residual_ref, norm_ref,
                 field_ref, o_ref, real, imag, kinetic, mixed_s, mixed_r, flat_s, flat_r, sems, out_sems):
    energy = energy_ref[0]
    third = rows // 3
    copies = []
    for n in range(3):
        at = pl.ds(n * third, third)
        copies.append((begin(field_far.at[:, at, :], field_ref.at[:, at, :], sems.at[n]),
                       begin(o_far.at[at], o_ref.at[at], sems.at[3 + n])))
    alpha = [step_ref[0:1, p : p + 1] for p in range(trials)]
    step = [step_ref[0:1, 8 + p : 9 + p] for p in range(trials)]
    narrow = lane_of((groups, 128))

    def waves_of(x):
        r = [in_ref[pl.ds(x * 9 + n, groups, stride=returned), :] for n in range(9)]
        for n in range(3):
            r0, r1, r2 = (pltpu.roll(r[3 * n + t], 32 + 32 * t, 1) for t in range(3))
            r.append(jnp.where(narrow < 32, r0, jnp.where(narrow < 64, r1, r2)))
        return jnp.concatenate(r, axis=0)

    for x in range(0, planes, 2):
        b = jnp.concatenate([waves_of(x), waves_of(x + 1)], axis=1)
        v = left_table(g4, b)
        for i in range(2):
            real[pl.ds(x + i, points, stride=planes), :] = v[:points, i * 128 : i * 128 + 128]
            imag[pl.ds(x + i, points, stride=planes), :] = v[points:, i * 128 : i * 128 + 128]
    size = 384
    mixed = planes * trials
    lane = lane_of((mixed, 128))

    def tiles(ref, q):
        c = [ref[(4 * q + i) * mixed : (4 * q + i + 1) * mixed, :] for i in range(4)]
        r1, r2, r3 = pltpu.roll(c[1], 96, 1), pltpu.roll(c[2], 64, 1), pltpu.roll(c[3], 32, 1)
        return jnp.where(lane < 96, c[0], r1), jnp.where(lane < 64, r1, r2), jnp.where(lane < 32, r2, r3)

    big = 384

    def along_z(i, _):
        at = pl.ds(pl.multiple_of(i * big, big), big)
        vh, vl = split(jnp.concatenate([real[at, :], imag[at, :]], axis=1))
        kinetic[at, :] = right_table(vh, vl, w2)
        return 0

    lax.fori_loop(0, rows // big, along_z, 0)

    def back(i, sums):
        at = pl.ds(pl.multiple_of(i * size, size), size)
        o = o_ref[at, :]
        shift = field_ref[4, at, :] - energy
        out = []
        for p in range(trials):
            source = (alpha[p] - field_ref[p, at, :]) * o
            image = kinetic[at, p * 128 : p * 128 + 128] + shift * source
            residual = source - step[p] * image
            there = pl.ds(p, size, stride=trials)
            mixed_s[there, :] = step[p] * source
            mixed_r[there, :] = residual
            out.append(sums[p] + fold(residual * residual))
        for flat, ref in ((flat_s, mixed_s), (flat_r, mixed_r)):
            for q in range(size // 48):
                for n, tile in enumerate(tiles(ref, q)):
                    flat[i, :, :, 384 * q + 128 * n : 384 * q + 128 * n + 128] = tile.reshape(planes, trials, 128)
        cells = pl.ds(pl.multiple_of(i * 3072, 3072), 3072)
        begin(flat_s.at[i], response_ref.at[:, :, cells], out_sems.at[0, i])
        begin(flat_r.at[i], residual_ref.at[:, :, cells], out_sems.at[1, i])
        return tuple(out)

    sums = tuple(jnp.zeros((8, 128), f32) for _ in range(trials))
    for n in range(3):
        for copy in copies[n]:
            copy.wait()
        sums = lax.fori_loop(n * (third // size), (n + 1) * (third // size), back, sums)
    norm_ref[...] = tile_of((8, 128), [(0, p, total(s)) for p, s in enumerate(sums)])
    for i in range(rows // size):
        cells = pl.ds(i * 3072, 3072)
        pltpu.make_async_copy(flat_s.at[i], response_ref.at[:, :, cells], out_sems.at[0, i]).wait()
        pltpu.make_async_copy(flat_r.at[i], residual_ref.at[:, :, cells], out_sems.at[1, i]).wait()


def direction_kernel(step_ref, n0, n1, response_ref, residual_ref, direction_ref, first, second, result, sems, out_sems):
    parts = 3
    width = points * points // parts
    loads = []
    for i in range(parts):
        cells = pl.ds(i * width, width)
        loads.append((begin(response_ref.at[:, :, cells], first.at[i], sems.at[0, i]),
                      begin(residual_ref.at[:, :, cells], second.at[i], sems.at[1, i])))
    new = n0[0:1, :] + n1[0:1, :]
    ratio = [new[:, p : p + 1] / step_ref[0:1, 4 + p : 5 + p] / step_ref[0:1, 8 + p : 9 + p] for p in range(trials)]
    r = row_of((trials, 128))
    ratios = jnp.zeros((trials, 128), f32)
    for p in range(trials):
        ratios = jnp.where(r == p, ratio[p], ratios)
    ratios = ratios[:, 0:1][None]
    stores = []
    for i in range(parts):
        for copy in loads[i]:
            copy.wait()
        result[i, :, :, :] = second[i] + ratios * first[i]
        stores.append(begin(result.at[i], direction_ref.at[:, :, pl.ds(i * width, width)], out_sems.at[i]))
    for copy in stores:
        copy.wait()


def density_kernel(packed_far, band_ref, density_ref, packed_ref, bands_in, sems):
    arrival = begin(band_ref, bands_in, sems.at[0])
    kept = begin(packed_far, packed_ref, sems.at[1])
    kept.wait()
    blocks = [packed_ref[q * 36 : q * 36 + 36, :] for q in range(3)]
    fields = [tighten(field) for field in (*blocks, unpack_last(*blocks))]
    sums = [jnp.zeros((27, 128), f32) for _ in range(trials)]
    arrival.wait()
    for v in range(bands):
        square = bands_in[v, 0:27, :]
        square = square * square
        for p in range(trials):
            alpha, step = bands_in[v, 28:29, p : p + 1], bands_in[v, 28:29, 8 + p : 9 + p]
            sums[p] = sums[p] + (step * (alpha - fields[p])) * square
    lane = lane_of((planes, 128))
    for p in range(trials):
        loose = loosen(sums[p]) * (4.0 / bands)
        c = [loose[12 * i : 12 * i + 12] for i in range(3)]
        r1, r2 = pltpu.roll(c[1], 96, 1), pltpu.roll(c[2], 64, 1)
        density_ref[:, p, 0:128] = jnp.where(lane < 96, c[0], r1)
        density_ref[:, p, 128:256] = jnp.where(lane < 64, r1, r2)
        density_ref[:, p, 256:288] = r2[:, 0:32]


vmem = pl.BlockSpec(memory_space=pltpu.VMEM)
smem = pl.BlockSpec(memory_space=pltpu.SMEM)
hbm = pl.BlockSpec(memory_space=pl.ANY)
far = pl.BlockSpec(memory_space=pltpu.HBM)


BIG = 56000000
SOME = 54500000


def shape(*dims, dtype=f32):
    return jax.ShapeDtypeStruct(dims, dtype)


def call(kernel, ins, outs, scratch=(), name=None, room=4 * 2**20, places=None, aliases=None, flops=10**6):
    return pl.pallas_call(
        kernel, out_shape=outs, in_specs=ins,
        out_specs=places if places is not None else jax.tree.map(lambda _: vmem, outs),
        scratch_shapes=scratch, compiler_params=pltpu.CompilerParams(vmem_limit_bytes=room), name=name, input_output_aliases=aliases or {},
        cost_estimate=pl.CostEstimate(flops=flops, bytes_accessed=10**6, transcendentals=0),
    )


def pack(trial, local):
    return call(
        pack_kernel, [far] * 2, shape(144, 128),
        [buffer(planes, trials, 288), buffer(planes, 288), pltpu.SemaphoreType.DMA((2,))], name="pack", room=66000000,
    )(jnp.transpose(trial, (1, 0, 2)), local)


def orbital_rows(orbitals, packed):
    return call(
        orbital_kernel, [vmem, vmem],
        (shape(rows, 128), shape(bands, 32, 128), shape(144, 128)),
        [buffer(rows, 128), buffer(bands, 32, 128), pltpu.SemaphoreType.DMA((3,))],
        name="orbital_rows", places=(far, far, far), room=BIG,
    )(orbitals, packed)


def buffer(*dims, dtype=f32):
    return pltpu.VMEM(dims, dtype)


def forward(pieces, o, tables):
    return call(
        forward_kernel, [hbm] * 8 + [far] * 3,
        (shape(5, rows, 128), shape(rows, 128), shape(8, 128)),
        [buffer(rows, 128), buffer(5, rows, 128), buffer(bands, 144, 128), buffer(2, 640, 256, dtype=bf16), buffer(2, 96, 192, dtype=bf16), buffer(rows, 128),
         buffer(rows, 640, dtype=bf16), buffer(rows, 640, dtype=bf16), buffer(rows, 128), buffer(rows, 128),
         pltpu.SemaphoreType.DMA((11,))],
        name="forward", room=SOME, places=(far, far, vmem),
    )(*pieces, o, tables["w1"], tables["g1"])


def local_sums(energies, fields, o, stat, tables, base):
    size, count = 384, rows // 384
    tile = pl.BlockSpec((8, 128), lambda i: (0, 0))
    kinds = [tables[name] for name in ("g2", "g3", "g4", "w2")]
    return pl.pallas_call(
        local_kernel, grid=(count,),
        in_specs=[smem, pl.BlockSpec((5, size, 128), lambda i: (0, i, 0)), pl.BlockSpec((size, 128), lambda i: (i, 0)),
                  tile] + [far] * 5,
        out_specs=(tile, *[vmem] * 5),
        out_shape=(shape(8, 128), *[shape(*t.shape, dtype=bf16) for t in kinds], shape(bands, 8, 128)),
        scratch_shapes=[buffer(9, 8, 128), pltpu.SemaphoreType.DMA((5,))],
        compiler_params=pltpu.CompilerParams(vmem_limit_bytes=BIG), name="local_sums",
        cost_estimate=pl.CostEstimate(flops=10**7, bytes_accessed=10**7, transcendentals=0),
    )(energies, fields, o, stat, *kinds, base)


def waves(arrived, stat, sums, g2, g3):
    return call(
        wave_kernel, [vmem] * 5, (shape(groups * returned, 128), shape(8, 128)), name="waves", room=8 * 2**20,
    )(arrived, stat, sums, g2, g3)


def steps(arrived, scal, tail, base):
    return call(
        step_kernel, [vmem] * 3 + [far], (shape(8, 128), shape(bands, 32, 128)),
        [buffer(bands, 8, 128), pltpu.SemaphoreType.DMA((1,))],
        name="steps", places=(vmem, far), aliases={3: 1},
    )(arrived, scal, tail, base)


def image(energies, arrived, step, fields, o, g4, w2):
    cells = shape(planes, trials, points * points)
    return call(
        image_kernel, [smem, vmem, vmem, far, far, vmem, vmem], (cells, cells, shape(8, 128)),
        [buffer(5, rows, 128), buffer(rows, 128), buffer(rows, 128), buffer(rows, 128), buffer(rows, 512),
         buffer(1536, 128), buffer(1536, 128),
         buffer(3, planes, trials, 3072), buffer(3, planes, trials, 3072),
         pltpu.SemaphoreType.DMA((6,)), pltpu.SemaphoreType.DMA((2, 6))],
        name="image", room=BIG, places=(far, far, vmem), flops=2 * 10**10,
    )(energies, arrived, step, fields, o, g4, w2)


def direct(step, norms, response, residual):
    part = buffer(3, planes, trials, points * points // 3)
    return call(
        direction_kernel, [vmem] * 3 + [far] * 2, shape(planes, trials, points * points),
        [part, part, part, pltpu.SemaphoreType.DMA((2, 6)), pltpu.SemaphoreType.DMA((6,))],
        name="direction", room=BIG, places=far, flops=10**7,
    )(step, *norms, response, residual)


def density_of(packed, band):
    return call(
        density_kernel, [far, hbm], shape(planes, trials, 288),
        [buffer(144, 128), buffer(bands, 32, 128), pltpu.SemaphoreType.DMA((2,))], name="density",
    )(packed, band)


def outward(value):
    return jnp.transpose(value, (1, 0, 2))


def swapped(value, axis, size, mask):
    return lax.ppermute(value, axis, [(s, s ^ mask) for s in range(size)])


def crossed(value, even, odd):
    return lax.ppermute(value, "band", [(s, s ^ (odd if s & 1 else even)) for s in range(bands)])


first_masks = ((8, 8), (16, 2), (24, 10))
second_masks = ((2, 24), (4, 6), (6, 30))


def gather_first(packed):
    value = packed[None]
    return jnp.concatenate([value] + [crossed(value, *masks) for masks in first_masks], axis=0)


def gather_second(quad):
    quads = [quad] + [crossed(quad, *masks) for masks in second_masks]
    return quads + [swapped(q, "band", bands, 1) for q in quads]


def on_device(orbitals, energies, local_pot, trial_pot):
    tables = {name: jnp.asarray(table) for name, table in build_tables().items()}
    packed = pack(trial_pot, local_pot)
    quad = gather_first(packed)
    o_far, base, packed_far = orbital_rows(orbitals, packed)
    quad, o_far = lax.optimization_barrier((quad, o_far))
    pieces = gather_second(quad)
    fields, sent, stat = forward(pieces, o_far, tables)
    arrived = lax.all_to_all(sent.reshape(groups, chunk, 128), "grid", 0, 0, tiled=True).reshape(rows, 128)
    sums, g2, g3, g4, w2, tail = local_sums(energies, fields, o_far, stat, tables, base)
    back, scal = waves(arrived, stat, sums, g2, g3)
    back = lax.all_to_all(back.reshape(groups, returned, 128), "grid", 0, 0, tiled=True).reshape(groups * returned, 128)
    step, payload = steps(back, scal, tail, base)
    band = lax.all_to_all(payload, "band", 0, 0, tiled=True)
    response, residual, norm = image(energies, back, step, fields, o_far, g4, w2)
    norm = norm + swapped(norm, "grid", groups, 2) + swapped(norm, "grid", groups, 4) + swapped(norm, "grid", groups, 6)
    norms = [norm, swapped(norm, "grid", groups, 1)]
    direction = direct(step, norms, response, residual)
    density = density_of(packed_far, band)
    return outward(response)[None], outward(residual)[None], outward(direction)[None], outward(density)


def solution(mesh):
    return jax.shard_map(
        on_device,
        mesh=mesh,
        in_specs=(P("band", "grid", None), P("band"), P("grid", "band"), P(None, "grid", "band")),
        out_specs=(
            P("band", None, "grid", None),
            P("band", None, "grid", None),
            P("band", None, "grid", None),
            P(None, "grid", "band"),
        ),
        check_vma=False,
    )
```
